32 devices in a mesh: blk: 16 (over z, y, core), head: 2 (over x).
Axes of the slice: x: 2, y: 2, z: 4, core: 2. Of those that a mesh axis runs over, the one named last changes fastest.
Arguments:
- queries: bfloat16 [16384, 2048], P(('blk', 'head')), may hold values from -20 to 20
- keys: bfloat16 [16384, 1024], P(('blk', 'head')), may hold values from -20 to 20
- values: bfloat16 [16384, 1024], P(('blk', 'head')), may hold values from -6 to 6
- outputs: bfloat16 [16384, 2048], P(('blk', 'head')), may hold values from -6 to 6
- out_grads: bfloat16 [16384, 2048], P(('blk', 'head')), may hold values from -6 to 6
- segment_ids: int32 [16384], replicated, may hold values from 0 to 63, never falling along the last dimension, each value on 1 to 512 neighbouring positions
- block_order: int32 [32], replicated, may hold values from 0 to 31, as said below
Outputs:
- query_grads: bfloat16 [16384, 2048], P(('blk', 'head'))
- key_grads: bfloat16 [16384, 1024], P(('blk', 'head'))
- value_grads: bfloat16 [16384, 1024], P(('blk', 'head'))
The draws below stay inside these ranges and needn't reach their ends.
Inputs may be any that keep to these rules, and one draw needn't show every extreme that they name: `segment_ids`: never falling along the sequence; each document has 1 to 512 tokens, one exactly 512. `block_order`: slots 2 i and 2 i + 1 hold the half-blocks i and 31 - i, in either order.
All inputs are finite; a program needn't handle non-finite values.
Results may differ from the reference program's by a relative error of at most 0.008.
Values may be sent and summed in bfloat16 or wider, within the bound.
No kernel may reach another device: no remote copies, remote signals or barrier semaphores. Data moves between devices by JAX's collectives and lax.ppermute only.
A program may use at most 128 MiB of HBM per device.

```python
import math
import jax
import jax.numpy as jnp
import numpy as np
from jax import lax

QUERY_HEADS = 16
KEY_VALUE_HEADS = 8
HEAD_SIZE = 128
PACKED_TOKENS = 16384
HALF = 512
HALVES = 32
DOCS = 64
DOC_MOST = 512


def key_base(key):
    return jnp.clip(jax.random.normal(key, (PACKED_TOKENS, KEY_VALUE_HEADS * HEAD_SIZE), jnp.float32), -6.0, 6.0)


def draw_keys(key, part):
    base = key_base(key)
    result = base
    return result.astype(jnp.bfloat16)


def draw_queries(key, part):
    key = jax.random.fold_in(key, 12)
    own = jnp.clip(jax.random.normal(key, (PACKED_TOKENS, QUERY_HEADS * HEAD_SIZE), jnp.float32), -6.0, 6.0)
    result = own
    return result.astype(jnp.bfloat16)


def draw_block_order(key, part):
    key = jax.random.fold_in(key, 13)
    pair_count = HALVES // 2
    early_half = jnp.arange(pair_count, dtype=jnp.int32)
    late_half = (HALVES - 1 - early_half).astype(jnp.int32)
    flipped = jax.random.randint(key, (pair_count,), 0, 2, dtype=jnp.int32)
    slot_low = jnp.where(flipped == 1, late_half, early_half)
    slot_high = jnp.where(flipped == 1, early_half, late_half)
    return jnp.stack([slot_low, slot_high], axis=1).reshape(HALVES).astype(jnp.int32)


def shard_levels(key, dims, pieces, smallest, high):
    loudness = 1.0
    for position, blocks in pieces:
        draws = jax.random.uniform(jax.random.fold_in(jax.random.fold_in(key, 6), position), (blocks,), jnp.float32, smallest / len(pieces), high / len(pieces))
        loudness = loudness * jnp.repeat(jnp.exp(draws), dims[position] // blocks).reshape((-1,) + (1,) * (len(dims) - 1 - position))
    return loudness


def length_profile(number_of, total, reach, slope):
    loads = [(1 << 20) // math.isqrt(grade ** slope) + 1 for grade in range(2, number_of + 1)]
    surplus, given = total - reach - (number_of - 1), [1] * (number_of - 1)
    while surplus > 0:
        movable = [i for i in range(number_of - 1) if given[i] < reach]
        mass, remaining = sum([loads[i] for i in movable]), surplus
        for i in movable:
            more = min(reach - given[i], max(1, remaining * loads[i] // mass), surplus)
            given[i] = given[i] + more
            surplus = surplus - more
    return np.array([reach] + given)


def ragged_sizes(own_key, count, total, bound, lean):
    if count == 2:
        one = jax.random.randint(own_key, (), max(1, total - bound), min(bound, total - 1) + 1)
        return jnp.stack([one, total - one])
    tallies = jnp.asarray(length_profile(count, total, bound, lean), jnp.int32)
    twos = (count - 1) // 2
    source_of, receiver = tallies[1:1 + 2 * twos:2], tallies[2:2 + 2 * twos:2]
    slack = jnp.minimum(source_of - 1, bound - receiver)
    shifted = jax.random.randint(jax.random.fold_in(own_key, 1), (twos,), 0, 1 << 20) % (slack + 1)
    tallies = tallies.at[1:1 + 2 * twos:2].set(source_of - shifted).at[2:2 + 2 * twos:2].set(receiver + shifted)
    return tallies[jax.random.permutation(jax.random.fold_in(own_key, 2), count)]


def scatter_about(key, dims, width, most, pieces=(), held_as=jnp.bfloat16):
    level = shard_levels(key, dims, pieces, -0.22, 0.18) if pieces else 1.0
    entries = jax.random.normal(key, dims, jnp.float32) * width * level
    return jnp.minimum(jnp.maximum(entries, -most), most).astype(held_as)


def setup_inputs(seed: int = 0) -> dict:
    key_of = jax.random.split(jax.random.key(seed), 8)
    return {
        "queries": draw_queries(jax.random.fold_in(key_of[7], 71), 0),
        "keys": draw_keys(jax.random.fold_in(key_of[7], 71), 0),
        "values": scatter_about(key_of[2], (PACKED_TOKENS, KEY_VALUE_HEADS * HEAD_SIZE), 1.0, 6.0, ((0, 32),)),
        "outputs": scatter_about(key_of[3], (PACKED_TOKENS, QUERY_HEADS * HEAD_SIZE), 1.0, 6.0, ((0, 32),)),
        "out_grads": scatter_about(key_of[4], (PACKED_TOKENS, QUERY_HEADS * HEAD_SIZE), 1.0, 6.0, ((0, 32),)),
        "segment_ids": jnp.searchsorted(jnp.cumsum(ragged_sizes(key_of[5], DOCS, PACKED_TOKENS, DOC_MOST, 2)), jnp.arange(PACKED_TOKENS), side="right").astype(jnp.int32),
        "block_order": draw_block_order(jax.random.fold_in(key_of[7], 71), 0),
    }


NEGATIVE = -1e30


def reference(queries, keys, values, outputs, out_grads, segment_ids, block_order):
    softmax_scale = HEAD_SIZE ** -0.5
    query_group_size = QUERY_HEADS // KEY_VALUE_HEADS
    stored = jnp.arange(PACKED_TOKENS, dtype=jnp.int32)
    positions = (block_order[stored // HALF] * HALF + stored % HALF).astype(jnp.int32)
    order = jnp.zeros((PACKED_TOKENS,), jnp.int32).at[positions].set(stored)
    seq_queries = queries[order]
    seq_keys = keys[order]
    seq_values = values[order]
    seq_outputs = outputs[order]
    seq_grads = out_grads[order]
    documents = segment_ids
    block = math.gcd(PACKED_TOKENS, 512)
    count = PACKED_TOKENS // block
    window = min(PACKED_TOKENS, DOC_MOST + block)
    query_parts = []
    key_parts = []
    value_parts = []
    for key_value_head in range(KEY_VALUE_HEADS):
        key_head = seq_keys[:, key_value_head * HEAD_SIZE:(key_value_head + 1) * HEAD_SIZE]
        value_head = seq_values[:, key_value_head * HEAD_SIZE:(key_value_head + 1) * HEAD_SIZE]
        key_acc = jnp.zeros((PACKED_TOKENS, HEAD_SIZE), jnp.float32)
        value_acc = jnp.zeros((PACKED_TOKENS, HEAD_SIZE), jnp.float32)
        for member in range(query_group_size):
            head = key_value_head * query_group_size + member
            query_head = seq_queries[:, head * HEAD_SIZE:(head + 1) * HEAD_SIZE]
            grad_head = seq_grads[:, head * HEAD_SIZE:(head + 1) * HEAD_SIZE]
            output_head = seq_outputs[:, head * HEAD_SIZE:(head + 1) * HEAD_SIZE]

            def one_block(carry, index):
                key_sum, value_sum = carry
                start = (index * block).astype(jnp.int32)
                win_start = jnp.clip(start - DOC_MOST, 0, PACKED_TOKENS - window).astype(jnp.int32)
                query_block = lax.dynamic_slice_in_dim(query_head, start, block, 0)
                grad_block = lax.dynamic_slice_in_dim(grad_head, start, block, 0)
                output_block = lax.dynamic_slice_in_dim(output_head, start, block, 0)
                key_win = lax.dynamic_slice_in_dim(key_head, win_start, window, 0)
                value_win = lax.dynamic_slice_in_dim(value_head, win_start, window, 0)
                pos_block = (start + jnp.arange(block, dtype=jnp.int32)).astype(jnp.int32)
                pos_win = (win_start + jnp.arange(window, dtype=jnp.int32)).astype(jnp.int32)
                doc_block = lax.dynamic_slice_in_dim(documents, start, block, 0)
                doc_win = lax.dynamic_slice_in_dim(documents, win_start, window, 0)
                visible = (doc_block[:, None] == doc_win[None, :]) & (pos_win[None, :] <= pos_block[:, None])
                raw = jnp.dot(query_block, key_win.T, preferred_element_type=jnp.float32) * softmax_scale
                scores = jnp.where(visible, raw, NEGATIVE)
                maxima = jnp.max(scores, axis=1)
                totals = jnp.sum(jnp.where(visible, jnp.exp(scores - maxima[:, None]), 0.0), axis=1)
                log_sums = maxima + jnp.log(totals)
                weights = jnp.where(visible, jnp.exp(scores - log_sums[:, None]), 0.0)
                weights_b = weights.astype(jnp.bfloat16)
                delta = jnp.sum(grad_block.astype(jnp.float32) * output_block.astype(jnp.float32), axis=1)
                weight_grads = jnp.dot(grad_block, value_win.T, preferred_element_type=jnp.float32)
                score_grads = weights * (weight_grads - delta[:, None])
                score_grads_b = score_grads.astype(jnp.bfloat16)
                query_block_grad = (jnp.dot(score_grads_b, key_win, preferred_element_type=jnp.float32) * softmax_scale).astype(jnp.bfloat16)
                key_term = jnp.dot(score_grads_b.T, query_block, preferred_element_type=jnp.float32)
                value_term = jnp.dot(weights_b.T, grad_block, preferred_element_type=jnp.float32)
                key_now = lax.dynamic_slice_in_dim(key_sum, win_start, window, 0)
                value_now = lax.dynamic_slice_in_dim(value_sum, win_start, window, 0)
                key_sum = lax.dynamic_update_slice_in_dim(key_sum, key_now + key_term, win_start, 0)
                value_sum = lax.dynamic_update_slice_in_dim(value_sum, value_now + value_term, win_start, 0)
                return (key_sum, value_sum), query_block_grad

            (key_acc, value_acc), query_blocks = lax.scan(one_block, (key_acc, value_acc), jnp.arange(count, dtype=jnp.int32))
            query_parts.append(query_blocks.reshape(PACKED_TOKENS, HEAD_SIZE))
        key_parts.append((key_acc * softmax_scale).astype(jnp.bfloat16))
        value_parts.append(value_acc.astype(jnp.bfloat16))
    query_seq = jnp.concatenate(query_parts, axis=1)
    key_seq = jnp.concatenate(key_parts, axis=1)
    value_seq = jnp.concatenate(value_parts, axis=1)
    return (query_seq[positions], key_seq[positions], value_seq[positions])
```

```python
import functools

import jax
import jax.numpy as jnp
from jax import lax
from jax.experimental import pallas as pl
from jax.experimental.pallas import tpu as pltpu
from jax.sharding import PartitionSpec as P

HEAD_SIZE = 128
NEGATIVE = -1e30
LOG2_E = 1.4426950408889634
CHUNKS = 2
TILE = 128
VMEM_BYTES = 40 * 1024 * 1024


def dot(left, right, left_dim, right_dim):
    return lax.dot_general(
        left, right, (((left_dim,), (right_dim,)), ((), ())), preferred_element_type=jnp.float32
    )


def attention_body(carried, group_ref, low_ref, q_ref, k_ref, v_ref, o_ref, do_ref, past_ref, *refs):
    dq_ref, dk_ref, dv_ref, back_ref, k_all, v_all, k_turned, dk_sum, dv_sum = refs[carried:]
    rows, head = k_ref.shape
    window = past_ref.shape[1]
    members = q_ref.shape[1] // head
    span = window + TILE
    scale = head**-0.5
    k_all[:window] = past_ref[0]
    k_all[window:] = k_ref[...]
    v_all[:window] = past_ref[1]
    v_all[window:] = v_ref[...]
    k_turned[...] = k_all[...].T
    dk_sum[...] = jnp.zeros_like(dk_sum)
    dv_sum[...] = jnp.zeros_like(dv_sum)

    def stacked(ref, start):
        return jnp.concatenate(
            [ref[start : start + TILE, m * head : (m + 1) * head] for m in range(members)], axis=0
        )

    for start in range(0, rows, TILE):
        queries = stacked(q_ref, start)
        grads = stacked(do_ref, start)
        product = grads.astype(jnp.float32) * stacked(o_ref, start).astype(jnp.float32)
        delta = jnp.sum(product.T, axis=0, keepdims=True)
        low = jnp.concatenate([low_ref[:, start : start + TILE]] * members, axis=1)
        keys = k_all[start : start + span]
        scores = dot(keys, queries, 1, 1)
        key_index = lax.broadcasted_iota(jnp.int32, scores.shape, 0)
        lane = lax.broadcasted_iota(jnp.int32, (1, members * TILE), 1)
        visible = (key_index >= low - start) & (key_index <= window + lane % TILE)
        scores = jnp.where(visible, scores, NEGATIVE)
        top = jnp.max(scores, axis=0, keepdims=True)
        terms = jnp.exp2((scores - top) * (scale * LOG2_E))
        weights = terms * (1.0 / jnp.sum(terms, axis=0, keepdims=True))
        weight_grads = dot(v_all[start : start + span], grads, 1, 1)
        score_grads = (weights * (weight_grads - delta)).astype(jnp.bfloat16)
        dv_sum[start : start + span] += dot(weights.astype(jnp.bfloat16), grads, 1, 0)
        dk_sum[start : start + span] += dot(score_grads, queries, 1, 0)
        dq = (dot(k_turned[:, start : start + span], score_grads, 1, 0) * scale).T
        for m in range(members):
            dq_ref[start : start + TILE, m * head : (m + 1) * head] = dq[
                m * TILE : (m + 1) * TILE
            ].astype(dq_ref.dtype)
    back_ref[0] = dk_sum[:window].astype(back_ref.dtype)
    back_ref[1] = dv_sum[:window].astype(back_ref.dtype)
    dk_ref[...] = dk_sum[window:]
    dv_ref[...] = dv_sum[window:]


def attention(group, low, row_arrays, past, first_head, heads_per_group, carried):
    queries, keys, values, outputs, grads = row_arrays
    rows, window, count = keys.shape[0], past.shape[1], past.shape[2] // HEAD_SIZE
    wide = queries.shape[1] // keys.shape[1] * HEAD_SIZE

    def column(step, group_ref):
        return (0, group_ref[0] * heads_per_group + first_head + step)

    query_spec = pl.BlockSpec((rows, wide), column)
    key_spec = pl.BlockSpec((rows, HEAD_SIZE), column)
    past_spec = pl.BlockSpec((2, window, HEAD_SIZE), lambda step, group_ref: (0, 0, step))
    low_spec = pl.BlockSpec((1, rows), lambda step, group_ref: (0, 0))
    tiles = count * queries.shape[1] // keys.shape[1] * rows * (window + TILE)
    return pl.pallas_call(
        functools.partial(attention_body, len(carried)),
        grid_spec=pltpu.PrefetchScalarGridSpec(
            num_scalar_prefetch=1,
            grid=(count,),
            in_specs=[low_spec, query_spec, key_spec, key_spec, query_spec, query_spec, past_spec]
            + [pl.BlockSpec(memory_space=pl.ANY)] * len(carried),
            out_specs=[query_spec, key_spec, key_spec, past_spec],
            scratch_shapes=[
                pltpu.VMEM((window + rows, HEAD_SIZE), jnp.bfloat16),
                pltpu.VMEM((window + rows, HEAD_SIZE), jnp.bfloat16),
                pltpu.VMEM((HEAD_SIZE, window + rows), jnp.bfloat16),
                pltpu.VMEM((window + rows, HEAD_SIZE), jnp.float32),
                pltpu.VMEM((window + rows, HEAD_SIZE), jnp.float32),
            ],
        ),
        out_shape=[
            jax.ShapeDtypeStruct(queries.shape, jnp.bfloat16),
            jax.ShapeDtypeStruct(keys.shape, jnp.float32),
            jax.ShapeDtypeStruct(keys.shape, jnp.float32),
            jax.ShapeDtypeStruct(past.shape, jnp.bfloat16),
        ],
        input_output_aliases={8 + i: i for i in range(len(carried))},
        compiler_params=pltpu.CompilerParams(vmem_limit_bytes=VMEM_BYTES),
        cost_estimate=pl.CostEstimate(
            flops=10 * tiles * HEAD_SIZE, bytes_accessed=count * rows * 2400, transcendentals=tiles
        ),
        name="attention",
    )(group, low, *row_arrays, past, *carried)


def finish_body(carried, group_ref, dk_ref, dv_ref, back_ref, *refs):
    key_out, value_out = refs[carried:]
    scale = HEAD_SIZE**-0.5
    key_out[...] = ((dk_ref[...] + back_ref[0].astype(jnp.float32)) * scale).astype(key_out.dtype)
    value_out[...] = (dv_ref[...] + back_ref[1].astype(jnp.float32)).astype(value_out.dtype)


def finish(group, own, back, first_head, heads_per_group, carried):
    rows, count = back.shape[1], back.shape[2] // HEAD_SIZE

    def column(step, group_ref):
        return (0, group_ref[0] * heads_per_group + first_head + step)

    key_spec = pl.BlockSpec((rows, HEAD_SIZE), column)
    back_spec = pl.BlockSpec((2, rows, HEAD_SIZE), lambda step, group_ref: (0, 0, step))
    return pl.pallas_call(
        functools.partial(finish_body, len(carried)),
        grid_spec=pltpu.PrefetchScalarGridSpec(
            num_scalar_prefetch=1,
            grid=(count,),
            in_specs=[key_spec, key_spec, back_spec]
            + [pl.BlockSpec(memory_space=pl.ANY)] * len(carried),
            out_specs=[key_spec, key_spec],
        ),
        out_shape=[jax.ShapeDtypeStruct(own[0].shape, jnp.bfloat16)] * 2,
        input_output_aliases={4 + i: i for i in range(len(carried))},
        cost_estimate=pl.CostEstimate(
            flops=count * rows * 512, bytes_accessed=count * rows * 2048, transcendentals=0
        ),
        name="finish",
    )(group, *own, back, *carried)


def pick(items, index):
    result = items[-1]
    for place in range(len(items) - 2, -1, -1):
        result = jnp.where(index == place, items[place], result)
    return result


def local(queries, keys, values, outputs, out_grads, segment_ids, block_order):
    blocks, sharers = lax.axis_size("blk"), lax.axis_size("head")
    block, place = lax.axis_index("blk"), lax.axis_index("head")
    rows = keys.shape[0]
    window = rows * sharers // 2
    parts = sharers // 2
    key_heads = keys.shape[1] // HEAD_SIZE
    heads_per_group = key_heads // sharers
    chunks = min(CHUNKS, heads_per_group)
    per_piece = heads_per_group // chunks
    slots = lax.dynamic_slice_in_dim(block_order, 2 * block, 2)
    early_slot = (slots[0] > slots[1]).astype(jnp.int32)
    last_block = block == blocks - 1

    def other(turn):
        return lax.rem(place + turn + sharers, sharers)

    def turned(value, turn):
        pairs = [(source, (source + turn) % sharers) for source in range(sharers)]
        return lax.ppermute(value, "head", pairs)

    def shifted(value, step):
        first, end = max(0, -step), min(blocks, blocks - step)
        return lax.ppermute(value, "blk", [(source, source + step) for source in range(first, end)])

    def columns(array, group, chunk):
        pieces = []
        for g in range(sharers):
            start = (g * heads_per_group + chunk * per_piece) * HEAD_SIZE
            pieces.append(array[:, start : start + per_piece * HEAD_SIZE])
        return pick(pieces, group)

    def piece_of(group, chunk):
        return jnp.stack([columns(keys, group, chunk), columns(values, group, chunk)])

    def is_early(device):
        return device // parts == early_slot

    def part_rows(array, device, count):
        if parts == 1:
            return array[:, :count]
        return lax.dynamic_slice_in_dim(array, device % parts * rows, count, 1)

    my_half = pick([slots[0], slots[1]], place // parts)
    start = my_half * window + place % parts * rows
    padded = jnp.concatenate([jnp.full((window,), -1, jnp.int32), segment_ids])
    near = lax.dynamic_slice_in_dim(padded, start, window + rows)
    low = jnp.sum((near[None, :] < near[window:, None]).astype(jnp.int32), axis=1)[None, :]

    row_arrays = (queries, keys, values, outputs, out_grads)
    groups = [other(-turn) for turn in range(sharers)]

    def halves_of(pieces):
        return [
            jnp.concatenate(
                [
                    pick(pieces, lax.rem(place - (slot * parts + p) + sharers, sharers))
                    for p in range(parts)
                ],
                axis=1,
            )
            for slot in (early_slot, 1 - early_slot)
        ]

    pasts = []
    for chunk in range(chunks):
        pieces = [piece_of(place, chunk)]
        for turn in range(1, sharers):
            pieces.append(turned(piece_of(other(turn), chunk), turn))
        early, late = halves_of(pieces)
        before_early, before_late = shifted(early, 1), shifted(late, -1)
        before_late = jnp.where(last_block, early, before_late)

        def past_of(device):
            before = jnp.where(is_early(device), before_early, before_late)
            if parts == 1:
                return before
            own = jnp.where(is_early(device), early, late)
            return part_rows(jnp.concatenate([before, own], axis=1), device, window)

        pasts.append(
            [past_of(place)]
            + [turned(past_of(other(turn)), turn) for turn in range(1, sharers)]
        )

    carried = ()
    backs = []
    for chunk in range(chunks):
        backs.append([])
        for turn in range(sharers):
            *carried, back = attention(
                groups[turn].reshape(1),
                low,
                row_arrays,
                pasts[chunk][turn],
                chunk * per_piece,
                heads_per_group,
                tuple(carried),
            )
            backs[chunk].append(back)

    query_grads, *own = carried
    results = ()
    for chunk in range(chunks):
        terms = [backs[chunk][0]]
        for turn in range(1, sharers):
            terms.append(turned(backs[chunk][turn], -turn))
        to_before, to_own = [], []
        for slot in (early_slot, 1 - early_slot):
            if parts == 1:
                to_before.append(pick(terms, lax.rem(slot - place + sharers, sharers)))
                to_own.append(None)
            else:
                total = jnp.zeros((2, 2 * window, terms[0].shape[2]), jnp.float32)
                for turn in range(sharers):
                    device = other(turn)
                    mine = jnp.where(device // parts == slot, terms[turn].astype(jnp.float32), 0.0)
                    wide = jnp.pad(mine, ((0, 0), (window, window), (0, 0)))
                    total += lax.dynamic_slice_in_dim(
                        wide, window - device % parts * rows, 2 * window, 1
                    )
                to_before.append(total[:, :window].astype(jnp.bfloat16))
                to_own.append(total[:, window:])
        for_early, for_late = shifted(to_before[0], -1), shifted(to_before[1], 1)
        for_early = jnp.where(last_block, to_before[1], for_early)
        sums = [
            came if more is None else (came.astype(jnp.float32) + more).astype(jnp.bfloat16)
            for came, more in zip((for_early, for_late), to_own)
        ]

        def rows_of(device):
            return part_rows(jnp.where(is_early(device), sums[0], sums[1]), device, rows)

        for turn in range(sharers):
            back = rows_of(other(turn))
            if turn:
                back = turned(back, turn)
            results = finish(
                groups[turn].reshape(1),
                own,
                back,
                chunk * per_piece,
                heads_per_group,
                tuple(results),
            )
    return (query_grads, *results)


def solution(mesh):
    spread = P(("blk", "head"), None)
    return jax.shard_map(
        local,
        mesh=mesh,
        in_specs=(spread,) * 5 + (P(), P()),
        out_specs=(spread,) * 3,
        check_vma=False,
    )
```

```python
import functools

import jax
import jax.numpy as jnp
from jax import lax
from jax.experimental import pallas as pl
from jax.experimental.pallas import tpu as pltpu
from jax.sharding import PartitionSpec as P

HEAD_SIZE = 128
NEGATIVE = -1e30
LOG2_E = 1.4426950408889634
CHUNKS = 2
TILE = 128
VMEM_BYTES = 60 * 1024 * 1024


def dot(left, right, left_dim, right_dim):
    return lax.dot_general(
        left, right, (((left_dim,), (right_dim,)), ((), ())), preferred_element_type=jnp.float32
    )


def attention_body(carried, group_ref, low_ref, q_ref, k_ref, v_ref, o_ref, do_ref, past_ref, *refs):
    dq_ref, dk_ref, dv_ref, back_ref, k_all, v_all, k_turned, dk_sum, dv_sum = refs[carried:]
    rows, head = k_ref.shape
    window = past_ref.shape[1]
    members = q_ref.shape[1] // head
    span = window + TILE
    scale = head**-0.5
    k_all[:window] = past_ref[0]
    k_all[window:] = k_ref[...]
    v_all[:window] = past_ref[1]
    v_all[window:] = v_ref[...]
    k_turned[...] = k_all[...].T
    dk_sum[...] = jnp.zeros_like(dk_sum)
    dv_sum[...] = jnp.zeros_like(dv_sum)

    def stacked(ref, start):
        return jnp.concatenate(
            [ref[start : start + TILE, m * head : (m + 1) * head] for m in range(members)], axis=0
        )

    for start in range(0, rows, TILE):
        queries = stacked(q_ref, start)
        grads = stacked(do_ref, start)
        product = grads.astype(jnp.float32) * stacked(o_ref, start).astype(jnp.float32)
        delta = jnp.sum(product.T, axis=0, keepdims=True)
        low = jnp.concatenate([low_ref[:, start : start + TILE]] * members, axis=1)
        keys = k_all[start : start + span]
        scores = dot(keys, queries, 1, 1)
        key_index = lax.broadcasted_iota(jnp.int32, scores.shape, 0)
        lane = lax.broadcasted_iota(jnp.int32, (1, members * TILE), 1)
        visible = (key_index >= low - start) & (key_index <= window + lane % TILE)
        scores = jnp.where(visible, scores, NEGATIVE)
        top = jnp.max(scores, axis=0, keepdims=True)
        terms = jnp.exp2((scores - top) * (scale * LOG2_E))
        weights = terms * (1.0 / jnp.sum(terms, axis=0, keepdims=True))
        weight_grads = dot(v_all[start : start + span], grads, 1, 1)
        score_grads = (weights * (weight_grads - delta)).astype(jnp.bfloat16)
        dv_sum[start : start + span] += dot(weights.astype(jnp.bfloat16), grads, 1, 0)
        dk_sum[start : start + span] += dot(score_grads, queries, 1, 0)
        dq = (dot(k_turned[:, start : start + span], score_grads, 1, 0) * scale).T
        for m in range(members):
            dq_ref[start : start + TILE, m * head : (m + 1) * head] = dq[
                m * TILE : (m + 1) * TILE
            ].astype(dq_ref.dtype)
    back_ref[0] = dk_sum[:window].astype(back_ref.dtype)
    back_ref[1] = dv_sum[:window].astype(back_ref.dtype)
    dk_ref[...] = dk_sum[window:]
    dv_ref[...] = dv_sum[window:]


def attention(group, low, row_arrays, past, first_head, heads_per_group, carried):
    queries, keys, values, outputs, grads = row_arrays
    rows, window, count = keys.shape[0], past.shape[1], past.shape[2] // HEAD_SIZE
    wide = queries.shape[1] // keys.shape[1] * HEAD_SIZE

    def column(step, group_ref):
        return (0, group_ref[0] * heads_per_group + first_head + step)

    query_spec = pl.BlockSpec((rows, wide), column)
    key_spec = pl.BlockSpec((rows, HEAD_SIZE), column)
    past_spec = pl.BlockSpec((2, window, HEAD_SIZE), lambda step, group_ref: (0, 0, step))
    low_spec = pl.BlockSpec((1, rows), lambda step, group_ref: (0, 0))
    tiles = count * queries.shape[1] // keys.shape[1] * rows * (window + TILE)
    return pl.pallas_call(
        functools.partial(attention_body, len(carried)),
        grid_spec=pltpu.PrefetchScalarGridSpec(
            num_scalar_prefetch=1,
            grid=(count,),
            in_specs=[low_spec, query_spec, key_spec, key_spec, query_spec, query_spec, past_spec]
            + [pl.BlockSpec(memory_space=pl.ANY)] * len(carried),
            out_specs=[query_spec, key_spec, key_spec, past_spec],
            scratch_shapes=[
                pltpu.VMEM((window + rows, HEAD_SIZE), jnp.bfloat16),
                pltpu.VMEM((window + rows, HEAD_SIZE), jnp.bfloat16),
                pltpu.VMEM((HEAD_SIZE, window + rows), jnp.bfloat16),
                pltpu.VMEM((window + rows, HEAD_SIZE), jnp.float32),
                pltpu.VMEM((window + rows, HEAD_SIZE), jnp.float32),
            ],
        ),
        out_shape=[
            jax.ShapeDtypeStruct(queries.shape, jnp.bfloat16),
            jax.ShapeDtypeStruct(keys.shape, jnp.float32),
            jax.ShapeDtypeStruct(keys.shape, jnp.float32),
            jax.ShapeDtypeStruct(past.shape, jnp.bfloat16),
        ],
        input_output_aliases={8 + i: i for i in range(len(carried))},
        compiler_params=pltpu.CompilerParams(vmem_limit_bytes=VMEM_BYTES),
        cost_estimate=pl.CostEstimate(
            flops=10 * tiles * HEAD_SIZE, bytes_accessed=count * rows * 2400, transcendentals=tiles
        ),
        name="attention",
    )(group, low, *row_arrays, past, *carried)


def finish_body(carried, group_ref, dk_ref, dv_ref, back_ref, *refs):
    key_out, value_out = refs[carried:]
    scale = HEAD_SIZE**-0.5
    key_out[...] = ((dk_ref[...] + back_ref[0].astype(jnp.float32)) * scale).astype(key_out.dtype)
    value_out[...] = (dv_ref[...] + back_ref[1].astype(jnp.float32)).astype(value_out.dtype)


def finish(group, own, back, first_head, heads_per_group, carried):
    rows, count = back.shape[1], back.shape[2] // HEAD_SIZE

    def column(step, group_ref):
        return (0, group_ref[0] * heads_per_group + first_head + step)

    key_spec = pl.BlockSpec((rows, HEAD_SIZE), column)
    back_spec = pl.BlockSpec((2, rows, HEAD_SIZE), lambda step, group_ref: (0, 0, step))
    return pl.pallas_call(
        functools.partial(finish_body, len(carried)),
        grid_spec=pltpu.PrefetchScalarGridSpec(
            num_scalar_prefetch=1,
            grid=(count,),
            in_specs=[key_spec, key_spec, back_spec]
            + [pl.BlockSpec(memory_space=pl.ANY)] * len(carried),
            out_specs=[key_spec, key_spec],
        ),
        out_shape=[jax.ShapeDtypeStruct(own[0].shape, jnp.bfloat16)] * 2,
        input_output_aliases={4 + i: i for i in range(len(carried))},
        compiler_params=pltpu.CompilerParams(vmem_limit_bytes=VMEM_BYTES),
        cost_estimate=pl.CostEstimate(
            flops=count * rows * 512, bytes_accessed=count * rows * 2048, transcendentals=0
        ),
        name="finish",
    )(group, *own, back, *carried)


def pick(items, index):
    result = items[-1]
    for place in range(len(items) - 2, -1, -1):
        result = jnp.where(index == place, items[place], result)
    return result


def local(queries, keys, values, outputs, out_grads, segment_ids, block_order):
    blocks, sharers = lax.axis_size("blk"), lax.axis_size("head")
    block, place = lax.axis_index("blk"), lax.axis_index("head")
    rows = keys.shape[0]
    window = rows * sharers // 2
    parts = sharers // 2
    key_heads = keys.shape[1] // HEAD_SIZE
    heads_per_group = key_heads // sharers
    chunks = min(CHUNKS, heads_per_group)
    per_piece = heads_per_group // chunks
    slots = lax.dynamic_slice_in_dim(block_order, 2 * block, 2)
    early_slot = (slots[0] > slots[1]).astype(jnp.int32)
    last_block = block == blocks - 1

    def other(turn):
        return lax.rem(place + turn + sharers, sharers)

    def turned(value, turn):
        pairs = [(source, (source + turn) % sharers) for source in range(sharers)]
        return lax.ppermute(value, "head", pairs)

    def shifted(value, step):
        first, end = max(0, -step), min(blocks, blocks - step)
        return lax.ppermute(value, "blk", [(source, source + step) for source in range(first, end)])

    def columns(array, group, chunk):
        pieces = []
        for g in range(sharers):
            start = (g * heads_per_group + chunk * per_piece) * HEAD_SIZE
            pieces.append(array[:, start : start + per_piece * HEAD_SIZE])
        return pick(pieces, group)

    def piece_of(group, chunk):
        return jnp.stack([columns(keys, group, chunk), columns(values, group, chunk)])

    def is_early(device):
        return device // parts == early_slot

    def part_rows(array, device, count):
        if parts == 1:
            return array[:, :count]
        return lax.dynamic_slice_in_dim(array, device % parts * rows, count, 1)

    my_half = pick([slots[0], slots[1]], place // parts)
    start = my_half * window + place % parts * rows
    padded = jnp.concatenate([jnp.full((window,), -1, jnp.int32), segment_ids])
    near = lax.dynamic_slice_in_dim(padded, start, window + rows)
    low = jnp.sum((near[None, :] < near[window:, None]).astype(jnp.int32), axis=1)[None, :]

    row_arrays = (queries, keys, values, outputs, out_grads)
    groups = [other(-turn) for turn in range(sharers)]

    def halves_of(pieces):
        return [
            jnp.concatenate(
                [
                    pick(pieces, lax.rem(place - (slot * parts + p) + sharers, sharers))
                    for p in range(parts)
                ],
                axis=1,
            )
            for slot in (early_slot, 1 - early_slot)
        ]

    pasts = []
    for chunk in range(chunks):
        pieces = [piece_of(place, chunk)]
        for turn in range(1, sharers):
            pieces.append(turned(piece_of(other(turn), chunk), turn))
        early, late = halves_of(pieces)
        before_early, before_late = shifted(early, 1), shifted(late, -1)
        before_late = jnp.where(last_block, early, before_late)

        def past_of(device):
            before = jnp.where(is_early(device), before_early, before_late)
            if parts == 1:
                return before
            own = jnp.where(is_early(device), early, late)
            return part_rows(jnp.concatenate([before, own], axis=1), device, window)

        pasts.append(
            [past_of(place)]
            + [turned(past_of(other(turn)), turn) for turn in range(1, sharers)]
        )

    carried = ()
    backs = [[] for chunk in range(chunks)]
    for turn in range(sharers):
        for chunk in range(chunks):
            *carried, back = attention(
                groups[turn].reshape(1),
                low,
                row_arrays,
                pasts[chunk][turn],
                chunk * per_piece,
                heads_per_group,
                tuple(carried),
            )
            backs[chunk].append(back)

    query_grads, *own = carried
    results = ()
    for chunk in range(chunks):
        terms = [backs[chunk][0]]
        for turn in range(1, sharers):
            terms.append(turned(backs[chunk][turn], -turn))
        to_before, to_own = [], []
        for slot in (early_slot, 1 - early_slot):
            if parts == 1:
                to_before.append(pick(terms, lax.rem(slot - place + sharers, sharers)))
                to_own.append(None)
            else:
                total = jnp.zeros((2, 2 * window, terms[0].shape[2]), jnp.float32)
                for turn in range(sharers):
                    device = other(turn)
                    mine = jnp.where(device // parts == slot, terms[turn].astype(jnp.float32), 0.0)
                    wide = jnp.pad(mine, ((0, 0), (window, window), (0, 0)))
                    total += lax.dynamic_slice_in_dim(
                        wide, window - device % parts * rows, 2 * window, 1
                    )
                to_before.append(total[:, :window].astype(jnp.bfloat16))
                to_own.append(total[:, window:])
        for_early, for_late = shifted(to_before[0], -1), shifted(to_before[1], 1)
        for_early = jnp.where(last_block, to_before[1], for_early)
        sums = [
            came if more is None else (came.astype(jnp.float32) + more).astype(jnp.bfloat16)
            for came, more in zip((for_early, for_late), to_own)
        ]

        def rows_of(device):
            return part_rows(jnp.where(is_early(device), sums[0], sums[1]), device, rows)

        for turn in range(sharers):
            back = rows_of(other(turn))
            if turn:
                back = turned(back, turn)
            results = finish(
                groups[turn].reshape(1),
                own,
                back,
                chunk * per_piece,
                heads_per_group,
                tuple(results),
            )
    return (query_grads, *results)


def solution(mesh):
    spread = P(("blk", "head"), None)
    return jax.shard_map(
        local,
        mesh=mesh,
        in_specs=(spread,) * 5 + (P(), P()),
        out_specs=(spread,) * 3,
        check_vma=False,
    )
```

```python
import functools

import jax
import jax.numpy as jnp
from jax import lax
from jax.experimental import pallas as pl
from jax.experimental.pallas import tpu as pltpu
from jax.sharding import PartitionSpec as P

HEAD_SIZE = 128
NEGATIVE = -1e30
LOG2_E = 1.4426950408889634
CHUNKS = 2
TILE = 128
OWN_STEP = 2
VMEM_BYTES = 60 * 1024 * 1024


def dot(left, right, left_dim, right_dim):
    return lax.dot_general(
        left, right, (((left_dim,), (right_dim,)), ((), ())), preferred_element_type=jnp.float32
    )


def stacked(ref, start, head):
    return jnp.concatenate(
        [
            ref[start : start + TILE, column : column + head]
            for column in range(0, ref.shape[1], head)
        ],
        axis=0,
    )


def seen_scores(keys, queries, low, first, causal):
    scores = dot(keys, queries, 1, 1)
    key_index = lax.broadcasted_iota(jnp.int32, scores.shape, 0)
    visible = key_index >= low - first
    if causal:
        lane = lax.broadcasted_iota(jnp.int32, (1, scores.shape[1]), 1)
        visible &= key_index <= keys.shape[0] - TILE + lane % TILE
    return jnp.where(visible, scores, NEGATIVE)


def low_of(low_ref, start, members):
    return jnp.concatenate([low_ref[:, start : start + TILE]] * members, axis=1)


def for_each_tile(first_ref, rows, blocks_of, body):
    for tile in range(rows // TILE):
        for block in blocks_of(tile):
            pl.when(first_ref[tile] == block)(functools.partial(body, tile, block))


def own_stats_body(first_ref, low_ref, q_ref, k_ref, o_ref, do_ref, stats_ref):
    rows, head = k_ref.shape
    members = q_ref.shape[1] // head

    def body(tile, block):
        start, begin = tile * TILE, block * TILE
        queries, grads = stacked(q_ref, start, head), stacked(do_ref, start, head)
        product = grads.astype(jnp.float32) * stacked(o_ref, start, head).astype(jnp.float32)
        scores = seen_scores(
            k_ref[begin : start + TILE], queries, low_of(low_ref, start, members), begin, True
        )
        top = jnp.max(scores, axis=0, keepdims=True)
        total = jnp.sum(jnp.exp2((scores - top) * (head**-0.5 * LOG2_E)), axis=0, keepdims=True)
        lanes = pl.ds(tile * members * TILE, members * TILE)
        stats_ref[0, 0:1, lanes] = top
        stats_ref[0, 1:2, lanes] = total
        stats_ref[0, 2:3, lanes] = jnp.sum(product.T, axis=0, keepdims=True)

    for_each_tile(first_ref, rows, lambda tile: range(tile + 1), body)


def window_body(
    carried, group_ref, first_ref, low_ref, q_ref, do_ref, past_ref, stats_ref, *refs
):
    merged_ref, turned_ref, back_ref, k_turned, dk_sum, dv_sum = refs[carried:]
    window, head = past_ref.shape[1:]
    rows = q_ref.shape[0]
    members = q_ref.shape[1] // head
    factor = head**-0.5 * LOG2_E
    dk_sum[...] = jnp.zeros_like(dk_sum)
    dv_sum[...] = jnp.zeros_like(dv_sum)
    turned_ref[...] = jnp.zeros_like(turned_ref)
    merged_ref[0, 0:1] = stats_ref[0, 0:1]
    merged_ref[0, 1:2] = 1.0 / stats_ref[0, 1:2]
    merged_ref[0, 2:3] = stats_ref[0, 2:3]
    k_turned[...] = past_ref[0].T

    def body(tile, block):
        start, begin = tile * TILE, block * TILE
        lanes = pl.ds(tile * members * TILE, members * TILE)
        queries, grads = stacked(q_ref, start, head), stacked(do_ref, start, head)
        scores = seen_scores(
            past_ref[0, begin:], queries, low_of(low_ref, start, members), begin, False
        )
        own_top, own_total = stats_ref[0, 0:1, lanes], stats_ref[0, 1:2, lanes]
        top = jnp.maximum(own_top, jnp.max(scores, axis=0, keepdims=True))
        terms = jnp.exp2((scores - top) * factor)
        total = own_total * jnp.exp2((own_top - top) * factor)
        inverse = 1.0 / (total + jnp.sum(terms, axis=0, keepdims=True))
        merged_ref[0, 0:1, lanes] = top
        merged_ref[0, 1:2, lanes] = inverse
        weights = terms * inverse
        weight_grads = dot(past_ref[1, begin:], grads, 1, 1)
        score_grads = weights * (weight_grads - stats_ref[0, 2:3, lanes])
        score_grads = score_grads.astype(jnp.bfloat16)
        dv_sum[begin:] += dot(weights.astype(jnp.bfloat16), grads, 1, 0)
        dk_sum[begin:] += dot(score_grads, queries, 1, 0)
        turned_ref[0, :, lanes] = dot(k_turned[:, begin:], score_grads, 1, 0)

    for_each_tile(first_ref, rows, lambda tile: range(tile, window // TILE), body)
    back_ref[0] = dk_sum[...].astype(back_ref.dtype)
    back_ref[1] = dv_sum[...].astype(back_ref.dtype)


def own_body(
    carried, first_ref, low_ref, q_ref, k_ref, v_ref, do_ref, merged_ref, turned_ref, *refs
):
    dq_ref, dk_ref, dv_ref, k_turned = refs[carried:]
    rows, head = k_ref.shape
    members = q_ref.shape[1] // head
    scale = head**-0.5
    dk_ref[...] = jnp.zeros_like(dk_ref)
    dv_ref[...] = jnp.zeros_like(dv_ref)
    k_turned[...] = k_ref[...].T

    def body(tile, block):
        start, begin = tile * TILE, block * TILE
        end = start + TILE
        lanes = pl.ds(tile * members * TILE, members * TILE)
        queries, grads = stacked(q_ref, start, head), stacked(do_ref, start, head)
        scores = seen_scores(
            k_ref[begin:end], queries, low_of(low_ref, start, members), begin, True
        )
        terms = jnp.exp2((scores - merged_ref[0, 0:1, lanes]) * (scale * LOG2_E))
        weights = terms * merged_ref[0, 1:2, lanes]
        weight_grads = dot(v_ref[begin:end], grads, 1, 1)
        score_grads = weights * (weight_grads - merged_ref[0, 2:3, lanes])
        score_grads = score_grads.astype(jnp.bfloat16)
        dv_ref[begin:end] += dot(weights.astype(jnp.bfloat16), grads, 1, 0)
        dk_ref[begin:end] += dot(score_grads, queries, 1, 0)
        turned = turned_ref[0, :, lanes] + dot(k_turned[:, begin:end], score_grads, 1, 0)
        dq = (turned * scale).T
        for m in range(members):
            dq_ref[start:end, m * head : (m + 1) * head] = dq[
                m * TILE : (m + 1) * TILE
            ].astype(dq_ref.dtype)

    for_each_tile(first_ref, rows, lambda tile: range(tile + 1), body)


def cost(count, rows, keys, members, products):
    tiles = count * members * rows * keys
    return pl.CostEstimate(
        flops=2 * products * tiles * HEAD_SIZE,
        bytes_accessed=count * rows * members * HEAD_SIZE * 16,
        transcendentals=tiles,
    )


def specs_of(row_arrays, head_index):
    queries, keys = row_arrays[:2]
    rows, members = keys.shape[0], queries.shape[1] // keys.shape[1]

    def column(*at):
        return (0, head_index(*at))

    def leading(*at):
        return (head_index(*at), 0, 0)

    return (
        pl.BlockSpec((rows, members * HEAD_SIZE), column),
        pl.BlockSpec((rows, HEAD_SIZE), column),
        pl.BlockSpec((1, 3, members * rows), leading),
        pl.BlockSpec((1, HEAD_SIZE, members * rows), leading),
    )


def whole_spec(array):
    return pl.BlockSpec(array.shape, lambda *at: (0,) * array.ndim)


def own_stats(first, low, row_arrays):
    queries, keys, values, outputs, grads = row_arrays
    rows, heads = keys.shape[0], keys.shape[1] // HEAD_SIZE
    members = queries.shape[1] // keys.shape[1]
    query_spec, key_spec, stats_spec, _ = specs_of(row_arrays, lambda step, first_ref: step)
    return pl.pallas_call(
        own_stats_body,
        grid_spec=pltpu.PrefetchScalarGridSpec(
            num_scalar_prefetch=1,
            grid=(heads,),
            in_specs=[whole_spec(low), query_spec, key_spec, query_spec, query_spec],
            out_specs=stats_spec,
        ),
        out_shape=jax.ShapeDtypeStruct((heads, 3, members * rows), jnp.float32),
        compiler_params=pltpu.CompilerParams(vmem_limit_bytes=VMEM_BYTES),
        cost_estimate=cost(heads, rows, rows // 2, members, 1),
        name="own_stats",
    )(first, low, queries, keys, outputs, grads)


def window_terms(group, first, low, row_arrays, past, stats, first_head, heads_per_group, carried):
    queries, keys, values, outputs, grads = row_arrays
    rows, heads = keys.shape[0], keys.shape[1] // HEAD_SIZE
    window, count = past.shape[1], past.shape[2] // HEAD_SIZE
    members = queries.shape[1] // keys.shape[1]
    query_spec, _, stats_spec, turned_spec = specs_of(
        row_arrays,
        lambda step, group_ref, first_ref: group_ref[0] * heads_per_group + first_head + step,
    )
    past_spec = pl.BlockSpec((2, window, HEAD_SIZE), lambda step, *refs: (0, 0, step))
    return pl.pallas_call(
        functools.partial(window_body, len(carried)),
        grid_spec=pltpu.PrefetchScalarGridSpec(
            num_scalar_prefetch=2,
            grid=(count,),
            in_specs=[whole_spec(low), query_spec, query_spec, past_spec, stats_spec]
            + [pl.BlockSpec(memory_space=pl.ANY)] * len(carried),
            out_specs=[stats_spec, turned_spec, past_spec],
            scratch_shapes=[
                pltpu.VMEM((HEAD_SIZE, window), jnp.bfloat16),
                pltpu.VMEM((window, HEAD_SIZE), jnp.float32),
                pltpu.VMEM((window, HEAD_SIZE), jnp.float32),
            ],
        ),
        out_shape=[
            jax.ShapeDtypeStruct(stats.shape, jnp.float32),
            jax.ShapeDtypeStruct((heads, HEAD_SIZE, members * rows), jnp.float32),
            jax.ShapeDtypeStruct(past.shape, jnp.bfloat16),
        ],
        input_output_aliases={7 + i: i for i in range(len(carried))},
        compiler_params=pltpu.CompilerParams(vmem_limit_bytes=VMEM_BYTES),
        cost_estimate=cost(count, rows, window // 4, members, 5),
        name="window_terms",
    )(group, first, low, queries, grads, past, stats, *carried)


def own_terms(first, low, row_arrays, merged, turned, first_head, count, carried):
    queries, keys, values, outputs, grads = row_arrays
    rows, members = keys.shape[0], queries.shape[1] // keys.shape[1]
    query_spec, key_spec, stats_spec, turned_spec = specs_of(
        row_arrays, lambda step, first_ref: first_head + step
    )
    return pl.pallas_call(
        functools.partial(own_body, len(carried)),
        grid_spec=pltpu.PrefetchScalarGridSpec(
            num_scalar_prefetch=1,
            grid=(count,),
            in_specs=[
                whole_spec(low), query_spec, key_spec, key_spec, query_spec, stats_spec, turned_spec
            ]
            + [pl.BlockSpec(memory_space=pl.ANY)] * len(carried),
            out_specs=[query_spec, key_spec, key_spec],
            scratch_shapes=[pltpu.VMEM((HEAD_SIZE, rows), jnp.bfloat16)],
        ),
        out_shape=[
            jax.ShapeDtypeStruct(queries.shape, jnp.bfloat16),
            jax.ShapeDtypeStruct(keys.shape, jnp.float32),
            jax.ShapeDtypeStruct(keys.shape, jnp.float32),
        ],
        input_output_aliases={8 + i: i for i in range(len(carried))},
        compiler_params=pltpu.CompilerParams(vmem_limit_bytes=VMEM_BYTES),
        cost_estimate=cost(count, rows, rows // 2, members, 5),
        name="own_terms",
    )(first, low, queries, keys, values, grads, merged, turned, *carried)


def finish_body(carried, group_ref, dk_ref, dv_ref, back_ref, *refs):
    key_out, value_out = refs[carried:]
    scale = HEAD_SIZE**-0.5
    key_out[...] = ((dk_ref[...] + back_ref[0].astype(jnp.float32)) * scale).astype(key_out.dtype)
    value_out[...] = (dv_ref[...] + back_ref[1].astype(jnp.float32)).astype(value_out.dtype)


def finish(group, own, back, first_head, heads_per_group, carried):
    rows, count = back.shape[1], back.shape[2] // HEAD_SIZE

    def column(step, group_ref):
        return (0, group_ref[0] * heads_per_group + first_head + step)

    key_spec = pl.BlockSpec((rows, HEAD_SIZE), column)
    back_spec = pl.BlockSpec((2, rows, HEAD_SIZE), lambda step, group_ref: (0, 0, step))
    return pl.pallas_call(
        functools.partial(finish_body, len(carried)),
        grid_spec=pltpu.PrefetchScalarGridSpec(
            num_scalar_prefetch=1,
            grid=(count,),
            in_specs=[key_spec, key_spec, back_spec]
            + [pl.BlockSpec(memory_space=pl.ANY)] * len(carried),
            out_specs=[key_spec, key_spec],
        ),
        out_shape=[jax.ShapeDtypeStruct(own[0].shape, jnp.bfloat16)] * 2,
        input_output_aliases={4 + i: i for i in range(len(carried))},
        compiler_params=pltpu.CompilerParams(vmem_limit_bytes=VMEM_BYTES),
        cost_estimate=pl.CostEstimate(
            flops=count * rows * 512, bytes_accessed=count * rows * 2048, transcendentals=0
        ),
        name="finish",
    )(group, *own, back, *carried)


def together(*values):
    return lax.optimization_barrier(values)


def pick(items, index):
    result = items[-1]
    for place in range(len(items) - 2, -1, -1):
        result = jnp.where(index == place, items[place], result)
    return result


def local(queries, keys, values, outputs, out_grads, segment_ids, block_order):
    blocks, sharers = lax.axis_size("blk"), lax.axis_size("head")
    block, place = lax.axis_index("blk"), lax.axis_index("head")
    rows = keys.shape[0]
    window = rows * sharers // 2
    parts = sharers // 2
    key_heads = keys.shape[1] // HEAD_SIZE
    heads_per_group = key_heads // sharers
    chunks = min(CHUNKS, heads_per_group)
    per_piece = heads_per_group // chunks
    slots = lax.dynamic_slice_in_dim(block_order, 2 * block, 2)
    early_slot = (slots[0] > slots[1]).astype(jnp.int32)
    last_block = block == blocks - 1

    def other(turn):
        return lax.rem(place + turn + sharers, sharers)

    def turned(value, turn):
        pairs = [(source, (source + turn) % sharers) for source in range(sharers)]
        return lax.ppermute(value, "head", pairs)

    def shifted(value, step):
        first, end = max(0, -step), min(blocks, blocks - step)
        return lax.ppermute(value, "blk", [(source, source + step) for source in range(first, end)])

    def columns(array, group, chunk):
        pieces = []
        for g in range(sharers):
            start = (g * heads_per_group + chunk * per_piece) * HEAD_SIZE
            pieces.append(array[:, start : start + per_piece * HEAD_SIZE])
        return pick(pieces, group)

    def piece_of(group, chunk):
        return jnp.stack([columns(keys, group, chunk), columns(values, group, chunk)])

    def is_early(device):
        return device // parts == early_slot

    def part_rows(array, device, count):
        if parts == 1:
            return array[:, :count]
        return lax.dynamic_slice_in_dim(array, device % parts * rows, count, 1)

    my_half = pick([slots[0], slots[1]], place // parts)
    start = my_half * window + place % parts * rows
    padded = jnp.concatenate([jnp.full((window,), -1, jnp.int32), segment_ids])
    near = lax.dynamic_slice_in_dim(padded, start, window + rows)
    low = jnp.sum((near[None, :] < near[window:, None]).astype(jnp.int32), axis=1)[None, :]

    tile_low = low[0, ::TILE]
    first_past = tile_low // TILE
    first_own = jnp.maximum(tile_low - window, 0) // TILE

    row_arrays = (queries, keys, values, outputs, out_grads)
    groups = [other(-turn) for turn in range(sharers)]

    def halves_of(pieces):
        return [
            jnp.concatenate(
                [
                    pick(pieces, lax.rem(place - (slot * parts + p) + sharers, sharers))
                    for p in range(parts)
                ],
                axis=1,
            )
            for slot in (early_slot, 1 - early_slot)
        ]

    pieces = [
        [piece_of(place, chunk)]
        + [turned(piece_of(other(turn), chunk), turn) for turn in range(1, sharers)]
        for chunk in range(chunks)
    ]
    stats = own_stats(first_own, low - window, row_arrays)
    stats, pieces[0][-1] = together(stats, pieces[0][-1])
    halves = [halves_of(pieces[chunk]) for chunk in range(chunks)]
    before = [(shifted(early, 1), shifted(late, -1)) for early, late in halves]

    merged, own_backs, pasts = (), [], []
    for chunk in range(chunks):
        (early, late), (before_early, before_late) = halves[chunk], before[chunk]
        if chunk:
            *merged, before_early, before_late = together(*merged, before_early, before_late)
        before_late = jnp.where(last_block, early, before_late)

        def past_of(device):
            before = jnp.where(is_early(device), before_early, before_late)
            if parts == 1:
                return before
            own = jnp.where(is_early(device), early, late)
            return part_rows(jnp.concatenate([before, own], axis=1), device, window)

        pasts.append([turned(past_of(other(turn)), turn) for turn in range(1, sharers)])
        *merged, back = window_terms(
            groups[0].reshape(1), first_past, low, row_arrays, past_of(place), stats,
            chunk * per_piece, heads_per_group, tuple(merged),
        )
        own_backs.append(back)

    terms = [[back] for back in own_backs]
    for chunk in range(chunks):
        for turn in range(1, sharers):
            *merged, back = window_terms(
                groups[turn].reshape(1), first_past, low, row_arrays, pasts[chunk][turn - 1], stats,
                chunk * per_piece, heads_per_group, tuple(merged),
            )
            terms[chunk].append(turned(back, -turn))

    carried = ()
    for head in range(0, key_heads, OWN_STEP):
        carried = own_terms(
            first_own, low - window, row_arrays, *merged, head, OWN_STEP, tuple(carried)
        )
        step = head // OWN_STEP
        if step % 2 and step // 2 < chunks:
            chunk = step // 2
            *carried, terms[chunk][-1] = together(*carried, terms[chunk][-1])
    query_grads, *own = carried
    results = ()
    for chunk in range(chunks):
        to_before, to_own = [], []
        for slot in (early_slot, 1 - early_slot):
            if parts == 1:
                to_before.append(pick(terms[chunk], lax.rem(slot - place + sharers, sharers)))
                to_own.append(None)
            else:
                total = jnp.zeros((2, 2 * window, terms[chunk][0].shape[2]), jnp.float32)
                for turn in range(sharers):
                    device = other(turn)
                    mine = jnp.where(device // parts == slot, terms[chunk][turn].astype(jnp.float32), 0.0)
                    wide = jnp.pad(mine, ((0, 0), (window, window), (0, 0)))
                    total += lax.dynamic_slice_in_dim(
                        wide, window - device % parts * rows, 2 * window, 1
                    )
                to_before.append(total[:, :window].astype(jnp.bfloat16))
                to_own.append(total[:, window:])
        for_early, for_late = shifted(to_before[0], -1), shifted(to_before[1], 1)
        for_early = jnp.where(last_block, to_before[1], for_early)
        sums = [
            came if more is None else (came.astype(jnp.float32) + more).astype(jnp.bfloat16)
            for came, more in zip((for_early, for_late), to_own)
        ]

        def rows_of(device):
            return part_rows(jnp.where(is_early(device), sums[0], sums[1]), device, rows)

        for turn in range(sharers):
            back = rows_of(other(turn))
            if turn:
                back = turned(back, turn)
            results = finish(
                groups[turn].reshape(1),
                own,
                back,
                chunk * per_piece,
                heads_per_group,
                tuple(results),
            )
    return (query_grads, *results)


def solution(mesh):
    spread = P(("blk", "head"), None)
    return jax.shard_map(
        local,
        mesh=mesh,
        in_specs=(spread,) * 5 + (P(), P()),
        out_specs=(spread,) * 3,
        check_vma=False,
    )
```

```python
import functools

import jax
import jax.numpy as jnp
from jax import lax
from jax.experimental import pallas as pl
from jax.experimental.pallas import tpu as pltpu
from jax.sharding import PartitionSpec as P

HEAD_SIZE = 128
NEGATIVE = -1e30
LOG2_E = 1.4426950408889634
CHUNKS = 2
TILE = 128
STRIP = 64
VMEM_BYTES = 60 * 1024 * 1024


def dot(left, right, left_dim, right_dim):
    return lax.dot_general(
        left, right, (((left_dim,), (right_dim,)), ((), ())), preferred_element_type=jnp.float32
    )


def strips(count):
    return [slice(start, start + STRIP) for start in range(0, count, STRIP)]


def folded(strip, reduce):
    return reduce(strip.reshape(strip.shape[0] // 8, 8, strip.shape[1]), axis=0)


def attention_body(carried, group_ref, low_ref, q_ref, k_ref, v_ref, o_ref, do_ref, past_ref, *refs):
    dq_ref, dk_ref, dv_ref, back_ref = refs[carried : carried + 4]
    k_all, v_all, k_turned, dk_sum, dv_sum, scores, slopes, weights_b, slopes_b = refs[carried + 4 :]
    rows, head = k_ref.shape
    window = past_ref.shape[1]
    members = q_ref.shape[1] // head
    span, lanes = window + TILE, members * TILE
    scale = head**-0.5
    k_all[:window] = past_ref[0]
    k_all[window:] = k_ref[...]
    v_all[:window] = past_ref[1]
    v_all[window:] = v_ref[...]
    k_turned[...] = k_all[...].T
    dk_sum[...] = jnp.zeros_like(dk_sum)
    dv_sum[...] = jnp.zeros_like(dv_sum)
    lane = lax.broadcasted_iota(jnp.int32, (1, lanes), 1) % TILE
    tiles = range(rows // TILE)

    def stacked(ref, start):
        return jnp.concatenate(
            [ref[start : start + TILE, m * head : (m + 1) * head] for m in range(members)], axis=0
        )

    def enter(tile):
        keys = pl.ds(tile * TILE, span)
        queries, grads = stacked(q_ref, tile * TILE), stacked(do_ref, tile * TILE)
        scores[tile] = dot(k_all[keys], queries, 1, 1)
        slopes[tile] = dot(v_all[keys], grads, 1, 1)
        return queries, grads

    def weigh(tile, grads):
        start = tile * TILE
        product = grads.astype(jnp.float32) * stacked(o_ref, start).astype(jnp.float32)
        delta = jnp.sum(product.T, axis=0, keepdims=True)
        low = jnp.concatenate([low_ref[:, start : start + TILE]] * members, axis=1) - start

        def visible(strip):
            index = strip.start + lax.broadcasted_iota(jnp.int32, (STRIP, lanes), 0)
            seen = index >= low
            return seen & (index <= window + lane) if strip.stop > window else seen

        top = jnp.full((8, lanes), NEGATIVE, jnp.float32)
        for strip in strips(span):
            masked = jnp.where(visible(strip), scores[tile, strip], NEGATIVE)
            top = jnp.maximum(top, folded(masked, jnp.max))
        top = jnp.max(top, axis=0, keepdims=True)
        total = jnp.zeros((8, lanes), jnp.float32)
        for strip in strips(span):
            terms = jnp.exp2((scores[tile, strip] - top) * (scale * LOG2_E))
            terms = jnp.where(visible(strip), terms, 0.0)
            total = total + folded(terms, jnp.sum)
            scores[tile, strip] = terms
        inverse = 1.0 / jnp.sum(total, axis=0, keepdims=True)
        for strip in strips(span):
            weights = scores[tile, strip] * inverse
            weights_b[tile, strip] = weights.astype(jnp.bfloat16)
            slopes_b[tile, strip] = (weights * (slopes[tile, strip] - delta)).astype(jnp.bfloat16)

    def leave(tile, queries, grads):
        start = tile * TILE
        keys = pl.ds(start, span)
        dv_sum[keys] += dot(weights_b[tile], grads, 1, 0)
        dk_sum[keys] += dot(slopes_b[tile], queries, 1, 0)
        dq = (dot(k_turned[:, keys], slopes_b[tile], 1, 0) * scale).T
        for m in range(members):
            dq_ref[start : start + TILE, m * head : (m + 1) * head] = dq[
                m * TILE : (m + 1) * TILE
            ].astype(dq_ref.dtype)

    entered = {0: enter(0)}
    for tile in tiles:
        if tile + 1 in tiles:
            entered[tile + 1] = enter(tile + 1)
        weigh(tile, entered[tile][1])
        leave(tile, *entered[tile])
    back_ref[0] = dk_sum[:window].astype(back_ref.dtype)
    back_ref[1] = dv_sum[:window].astype(back_ref.dtype)
    dk_ref[...] = dk_sum[window:]
    dv_ref[...] = dv_sum[window:]


def attention(group, low, row_arrays, past, first_head, heads_per_group, carried):
    queries, keys, values, outputs, grads = row_arrays
    rows, window, count = keys.shape[0], past.shape[1], past.shape[2] // HEAD_SIZE
    wide = queries.shape[1] // keys.shape[1] * HEAD_SIZE

    def column(step, group_ref):
        return (0, group_ref[0] * heads_per_group + first_head + step)

    query_spec = pl.BlockSpec((rows, wide), column)
    key_spec = pl.BlockSpec((rows, HEAD_SIZE), column)
    past_spec = pl.BlockSpec((2, window, HEAD_SIZE), lambda step, group_ref: (0, 0, step))
    low_spec = pl.BlockSpec((1, rows), lambda step, group_ref: (0, 0))
    square = (rows // TILE, window + TILE, wide // HEAD_SIZE * TILE)
    tiles = count * queries.shape[1] // keys.shape[1] * rows * (window + TILE)
    return pl.pallas_call(
        functools.partial(attention_body, len(carried)),
        grid_spec=pltpu.PrefetchScalarGridSpec(
            num_scalar_prefetch=1,
            grid=(count,),
            in_specs=[low_spec, query_spec, key_spec, key_spec, query_spec, query_spec, past_spec]
            + [pl.BlockSpec(memory_space=pl.ANY)] * len(carried),
            out_specs=[query_spec, key_spec, key_spec, past_spec],
            scratch_shapes=[
                pltpu.VMEM((window + rows, HEAD_SIZE), jnp.bfloat16),
                pltpu.VMEM((window + rows, HEAD_SIZE), jnp.bfloat16),
                pltpu.VMEM((HEAD_SIZE, window + rows), jnp.bfloat16),
                pltpu.VMEM((window + rows, HEAD_SIZE), jnp.float32),
                pltpu.VMEM((window + rows, HEAD_SIZE), jnp.float32),
                pltpu.VMEM(square, jnp.float32),
                pltpu.VMEM(square, jnp.float32),
                pltpu.VMEM(square, jnp.bfloat16),
                pltpu.VMEM(square, jnp.bfloat16),
            ],
        ),
        out_shape=[
            jax.ShapeDtypeStruct(queries.shape, jnp.bfloat16),
            jax.ShapeDtypeStruct(keys.shape, jnp.float32),
            jax.ShapeDtypeStruct(keys.shape, jnp.float32),
            jax.ShapeDtypeStruct(past.shape, jnp.bfloat16),
        ],
        input_output_aliases={8 + i: i for i in range(len(carried))},
        compiler_params=pltpu.CompilerParams(vmem_limit_bytes=VMEM_BYTES),
        cost_estimate=pl.CostEstimate(
            flops=10 * tiles * HEAD_SIZE, bytes_accessed=count * rows * 2400, transcendentals=tiles
        ),
        name="attention",
    )(group, low, *row_arrays, past, *carried)


def finish_body(carried, group_ref, dk_ref, dv_ref, back_ref, *refs):
    key_out, value_out = refs[carried:]
    scale = HEAD_SIZE**-0.5
    key_out[...] = ((dk_ref[...] + back_ref[0].astype(jnp.float32)) * scale).astype(key_out.dtype)
    value_out[...] = (dv_ref[...] + back_ref[1].astype(jnp.float32)).astype(value_out.dtype)


def finish(group, own, back, first_head, heads_per_group, carried):
    rows, count = back.shape[1], back.shape[2] // HEAD_SIZE

    def column(step, group_ref):
        return (0, group_ref[0] * heads_per_group + first_head + step)

    key_spec = pl.BlockSpec((rows, HEAD_SIZE), column)
    back_spec = pl.BlockSpec((2, rows, HEAD_SIZE), lambda step, group_ref: (0, 0, step))
    return pl.pallas_call(
        functools.partial(finish_body, len(carried)),
        grid_spec=pltpu.PrefetchScalarGridSpec(
            num_scalar_prefetch=1,
            grid=(count,),
            in_specs=[key_spec, key_spec, back_spec]
            + [pl.BlockSpec(memory_space=pl.ANY)] * len(carried),
            out_specs=[key_spec, key_spec],
        ),
        out_shape=[jax.ShapeDtypeStruct(own[0].shape, jnp.bfloat16)] * 2,
        input_output_aliases={4 + i: i for i in range(len(carried))},
        compiler_params=pltpu.CompilerParams(vmem_limit_bytes=VMEM_BYTES),
        cost_estimate=pl.CostEstimate(
            flops=count * rows * 512, bytes_accessed=count * rows * 2048, transcendentals=0
        ),
        name="finish",
    )(group, *own, back, *carried)


def together(*values):
    return lax.optimization_barrier(values)


def pick(items, index):
    result = items[-1]
    for place in range(len(items) - 2, -1, -1):
        result = jnp.where(index == place, items[place], result)
    return result


def local(queries, keys, values, outputs, out_grads, segment_ids, block_order):
    blocks, sharers = lax.axis_size("blk"), lax.axis_size("head")
    block, place = lax.axis_index("blk"), lax.axis_index("head")
    rows = keys.shape[0]
    window = rows * sharers // 2
    parts = sharers // 2
    key_heads = keys.shape[1] // HEAD_SIZE
    heads_per_group = key_heads // sharers
    chunks = min(CHUNKS, heads_per_group)
    per_piece = heads_per_group // chunks
    slots = lax.dynamic_slice_in_dim(block_order, 2 * block, 2)
    early_slot = (slots[0] > slots[1]).astype(jnp.int32)
    last_block = block == blocks - 1

    def other(turn):
        return lax.rem(place + turn + sharers, sharers)

    def turned(value, turn):
        pairs = [(source, (source + turn) % sharers) for source in range(sharers)]
        return lax.ppermute(value, "head", pairs)

    def shifted(value, step):
        first, end = max(0, -step), min(blocks, blocks - step)
        return lax.ppermute(value, "blk", [(source, source + step) for source in range(first, end)])

    def columns(array, group, chunk):
        pieces = []
        for g in range(sharers):
            start = (g * heads_per_group + chunk * per_piece) * HEAD_SIZE
            pieces.append(array[:, start : start + per_piece * HEAD_SIZE])
        return pick(pieces, group)

    def piece_of(group, chunk):
        return jnp.stack([columns(keys, group, chunk), columns(values, group, chunk)])

    def is_early(device):
        return device // parts == early_slot

    def part_rows(array, device, count):
        if parts == 1:
            return array[:, :count]
        return lax.dynamic_slice_in_dim(array, device % parts * rows, count, 1)

    my_half = pick([slots[0], slots[1]], place // parts)
    start = my_half * window + place % parts * rows
    padded = jnp.concatenate([jnp.full((window,), -1, jnp.int32), segment_ids])
    near = lax.dynamic_slice_in_dim(padded, start, window + rows)
    low = jnp.sum((near[None, :] < near[window:, None]).astype(jnp.int32), axis=1)[None, :]

    row_arrays = (queries, keys, values, outputs, out_grads)
    groups = [other(-turn) for turn in range(sharers)]

    def halves_of(pieces):
        return [
            jnp.concatenate(
                [
                    pick(pieces, lax.rem(place - (slot * parts + p) + sharers, sharers))
                    for p in range(parts)
                ],
                axis=1,
            )
            for slot in (early_slot, 1 - early_slot)
        ]

    halves = []
    for chunk in range(chunks):
        pieces = [piece_of(place, chunk)]
        pieces += [turned(piece_of(other(turn), chunk), turn) for turn in range(1, sharers)]
        halves.append(halves_of(pieces))
    before = [(shifted(early, 1), shifted(late, -1)) for early, late in halves]

    def run(turn, chunk, past, carried):
        *carried, back = attention(
            groups[turn].reshape(1), low, row_arrays, past,
            chunk * per_piece, heads_per_group, tuple(carried),
        )
        return carried, back

    carried, terms, pasts = (), [], []
    for chunk in range(chunks):
        (early, late), (before_early, before_late) = halves[chunk], before[chunk]
        if chunk:
            *carried, before_early, before_late = together(*carried, before_early, before_late)
        before_late = jnp.where(last_block, early, before_late)

        def past_of(device):
            before = jnp.where(is_early(device), before_early, before_late)
            if parts == 1:
                return before
            own = jnp.where(is_early(device), early, late)
            return part_rows(jnp.concatenate([before, own], axis=1), device, window)

        pasts.append([turned(past_of(other(turn)), turn) for turn in range(1, sharers)])
        carried, back = run(0, chunk, past_of(place), carried)
        terms.append([back])

    for chunk in range(chunks):
        for turn in range(1, sharers):
            carried, back = run(turn, chunk, pasts[chunk][turn - 1], carried)
            terms[chunk].append(turned(back, -turn))

    query_grads, *own = carried
    results = ()
    for chunk in range(chunks):
        to_before, to_own = [], []
        for slot in (early_slot, 1 - early_slot):
            if parts == 1:
                to_before.append(pick(terms[chunk], lax.rem(slot - place + sharers, sharers)))
                to_own.append(None)
            else:
                total = jnp.zeros((2, 2 * window, terms[chunk][0].shape[2]), jnp.float32)
                for turn in range(sharers):
                    device = other(turn)
                    mine = jnp.where(device // parts == slot, terms[chunk][turn].astype(jnp.float32), 0.0)
                    wide = jnp.pad(mine, ((0, 0), (window, window), (0, 0)))
                    total += lax.dynamic_slice_in_dim(
                        wide, window - device % parts * rows, 2 * window, 1
                    )
                to_before.append(total[:, :window].astype(jnp.bfloat16))
                to_own.append(total[:, window:])
        for_early, for_late = shifted(to_before[0], -1), shifted(to_before[1], 1)
        for_early = jnp.where(last_block, to_before[1], for_early)
        sums = [
            came if more is None else (came.astype(jnp.float32) + more).astype(jnp.bfloat16)
            for came, more in zip((for_early, for_late), to_own)
        ]

        def rows_of(device):
            return part_rows(jnp.where(is_early(device), sums[0], sums[1]), device, rows)

        for turn in range(sharers):
            back = rows_of(other(turn))
            if turn:
                back = turned(back, turn)
            results = finish(
                groups[turn].reshape(1),
                own,
                back,
                chunk * per_piece,
                heads_per_group,
                tuple(results),
            )
    return (query_grads, *results)


def solution(mesh):
    spread = P(("blk", "head"), None)
    return jax.shard_map(
        local,
        mesh=mesh,
        in_specs=(spread,) * 5 + (P(), P()),
        out_specs=(spread,) * 3,
        check_vma=False,
    )
```

```python
import functools

import jax
import jax.numpy as jnp
from jax import lax
from jax.experimental import pallas as pl
from jax.experimental.pallas import tpu as pltpu
from jax.sharding import PartitionSpec as P

HEAD_SIZE = 128
NEGATIVE = -1e30
LOG2_E = 1.4426950408889634
CHUNKS = 2
TILE = 128
STRIP = 64
TOGETHER = 2
VMEM_BYTES = 60 * 1024 * 1024


def dot(left, right, left_dim, right_dim):
    return lax.dot_general(
        left, right, (((left_dim,), (right_dim,)), ((), ())), preferred_element_type=jnp.float32
    )


def strips(count):
    return [slice(start, start + STRIP) for start in range(0, count, STRIP)]


def folded(strip, reduce):
    return reduce(strip.reshape(strip.shape[0] // 8, 8, strip.shape[1]), axis=0)


def attention_body(carried, group_ref, low_ref, q_ref, k_ref, v_ref, o_ref, do_ref, past_ref, *refs):
    dq_ref, dk_ref, dv_ref, back_ref = refs[carried : carried + 4]
    k_all, v_all, k_turned, dk_sum, dv_sum, scores, slopes, weights_b, slopes_b = refs[carried + 4 :]
    rows, head = k_ref.shape
    window = past_ref.shape[1]
    members = q_ref.shape[1] // head
    span, lanes = window + TILE, members * TILE
    scale = head**-0.5
    k_all[:window] = past_ref[0]
    k_all[window:] = k_ref[...]
    v_all[:window] = past_ref[1]
    v_all[window:] = v_ref[...]
    k_turned[...] = k_all[...].T
    dk_sum[...] = jnp.zeros_like(dk_sum)
    dv_sum[...] = jnp.zeros_like(dv_sum)
    lane = lax.broadcasted_iota(jnp.int32, (1, lanes), 1) % TILE
    together = scores.shape[0]

    def stacked(ref, start):
        return jnp.concatenate(
            [ref[pl.ds(start, TILE), m * head : (m + 1) * head] for m in range(members)], axis=0
        )

    def enter(start, tile):
        keys = pl.ds(start, span)
        queries, grads = stacked(q_ref, start), stacked(do_ref, start)
        scores[tile] = dot(k_all[keys], queries, 1, 1)
        slopes[tile] = dot(v_all[keys], grads, 1, 1)
        return queries, grads

    def weigh(start, tile, grads):
        product = grads.astype(jnp.float32) * stacked(o_ref, start).astype(jnp.float32)
        delta = jnp.sum(product.T, axis=0, keepdims=True)
        low = jnp.concatenate([low_ref[:, pl.ds(start, TILE)]] * members, axis=1) - start

        def visible(strip):
            index = strip.start + lax.broadcasted_iota(jnp.int32, (STRIP, lanes), 0)
            seen = index >= low
            return seen & (index <= window + lane) if strip.stop > window else seen

        top = jnp.full((8, lanes), NEGATIVE, jnp.float32)
        for strip in strips(span):
            masked = jnp.where(visible(strip), scores[tile, strip], NEGATIVE)
            top = jnp.maximum(top, folded(masked, jnp.max))
        top = jnp.max(top, axis=0, keepdims=True)
        total = jnp.zeros((8, lanes), jnp.float32)
        for strip in strips(span):
            terms = jnp.exp2((scores[tile, strip] - top) * (scale * LOG2_E))
            terms = jnp.where(visible(strip), terms, 0.0)
            total = total + folded(terms, jnp.sum)
            scores[tile, strip] = terms
        inverse = 1.0 / jnp.sum(total, axis=0, keepdims=True)
        for strip in strips(span):
            weights = scores[tile, strip] * inverse
            weights_b[tile, strip] = weights.astype(jnp.bfloat16)
            slopes_b[tile, strip] = (weights * (slopes[tile, strip] - delta)).astype(jnp.bfloat16)

    def leave(start, tile, queries, grads):
        keys = pl.ds(start, span)
        dv_sum[keys] += dot(weights_b[tile], grads, 1, 0)
        dk_sum[keys] += dot(slopes_b[tile], queries, 1, 0)
        dq = (dot(k_turned[:, keys], slopes_b[tile], 1, 0) * scale).T
        for m in range(members):
            dq_ref[pl.ds(start, TILE), m * head : (m + 1) * head] = dq[
                m * TILE : (m + 1) * TILE
            ].astype(dq_ref.dtype)

    @pl.loop(0, rows // TILE, step=together)
    def _(first):
        starts = [pl.multiple_of((first + tile) * TILE, TILE) for tile in range(together)]
        entered = [enter(start, tile) for tile, start in enumerate(starts)]
        for tile, start in enumerate(starts):
            weigh(start, tile, entered[tile][1])
        for tile, start in enumerate(starts):
            leave(start, tile, *entered[tile])

    back_ref[0] = dk_sum[:window].astype(back_ref.dtype)
    back_ref[1] = dv_sum[:window].astype(back_ref.dtype)
    dk_ref[...] = dk_sum[window:]
    dv_ref[...] = dv_sum[window:]


def attention(group, low, row_arrays, past, first_head, heads_per_group, carried):
    queries, keys, values, outputs, grads = row_arrays
    rows, window, count = keys.shape[0], past.shape[1], past.shape[2] // HEAD_SIZE
    wide = queries.shape[1] // keys.shape[1] * HEAD_SIZE

    def column(step, group_ref):
        return (0, group_ref[0] * heads_per_group + first_head + step)

    query_spec = pl.BlockSpec((rows, wide), column)
    key_spec = pl.BlockSpec((rows, HEAD_SIZE), column)
    past_spec = pl.BlockSpec((2, window, HEAD_SIZE), lambda step, group_ref: (0, 0, step))
    low_spec = pl.BlockSpec((1, rows), lambda step, group_ref: (0, 0))
    square = (min(TOGETHER, rows // TILE), window + TILE, wide // HEAD_SIZE * TILE)
    tiles = count * queries.shape[1] // keys.shape[1] * rows * (window + TILE)
    return pl.pallas_call(
        functools.partial(attention_body, len(carried)),
        grid_spec=pltpu.PrefetchScalarGridSpec(
            num_scalar_prefetch=1,
            grid=(count,),
            in_specs=[low_spec, query_spec, key_spec, key_spec, query_spec, query_spec, past_spec]
            + [pl.BlockSpec(memory_space=pl.ANY)] * len(carried),
            out_specs=[query_spec, key_spec, key_spec, past_spec],
            scratch_shapes=[
                pltpu.VMEM((window + rows, HEAD_SIZE), jnp.bfloat16),
                pltpu.VMEM((window + rows, HEAD_SIZE), jnp.bfloat16),
                pltpu.VMEM((HEAD_SIZE, window + rows), jnp.bfloat16),
                pltpu.VMEM((window + rows, HEAD_SIZE), jnp.float32),
                pltpu.VMEM((window + rows, HEAD_SIZE), jnp.float32),
                pltpu.VMEM(square, jnp.float32),
                pltpu.VMEM(square, jnp.float32),
                pltpu.VMEM(square, jnp.bfloat16),
                pltpu.VMEM(square, jnp.bfloat16),
            ],
        ),
        out_shape=[
            jax.ShapeDtypeStruct(queries.shape, jnp.bfloat16),
            jax.ShapeDtypeStruct(keys.shape, jnp.float32),
            jax.ShapeDtypeStruct(keys.shape, jnp.float32),
            jax.ShapeDtypeStruct(past.shape, jnp.bfloat16),
        ],
        input_output_aliases={8 + i: i for i in range(len(carried))},
        compiler_params=pltpu.CompilerParams(vmem_limit_bytes=VMEM_BYTES),
        cost_estimate=pl.CostEstimate(
            flops=10 * tiles * HEAD_SIZE, bytes_accessed=count * rows * 2400, transcendentals=tiles
        ),
        name="attention",
    )(group, low, *row_arrays, past, *carried)


def finish_body(carried, group_ref, dk_ref, dv_ref, back_ref, *refs):
    key_out, value_out = refs[carried:]
    scale = HEAD_SIZE**-0.5
    key_out[...] = ((dk_ref[...] + back_ref[0].astype(jnp.float32)) * scale).astype(key_out.dtype)
    value_out[...] = (dv_ref[...] + back_ref[1].astype(jnp.float32)).astype(value_out.dtype)


def finish(group, own, back, first_head, heads_per_group, carried):
    rows, count = back.shape[1], back.shape[2] // HEAD_SIZE

    def column(step, group_ref):
        return (0, group_ref[0] * heads_per_group + first_head + step)

    key_spec = pl.BlockSpec((rows, HEAD_SIZE), column)
    back_spec = pl.BlockSpec((2, rows, HEAD_SIZE), lambda step, group_ref: (0, 0, step))
    return pl.pallas_call(
        functools.partial(finish_body, len(carried)),
        grid_spec=pltpu.PrefetchScalarGridSpec(
            num_scalar_prefetch=1,
            grid=(count,),
            in_specs=[key_spec, key_spec, back_spec]
            + [pl.BlockSpec(memory_space=pl.ANY)] * len(carried),
            out_specs=[key_spec, key_spec],
        ),
        out_shape=[jax.ShapeDtypeStruct(own[0].shape, jnp.bfloat16)] * 2,
        input_output_aliases={4 + i: i for i in range(len(carried))},
        compiler_params=pltpu.CompilerParams(vmem_limit_bytes=VMEM_BYTES),
        cost_estimate=pl.CostEstimate(
            flops=count * rows * 512, bytes_accessed=count * rows * 2048, transcendentals=0
        ),
        name="finish",
    )(group, *own, back, *carried)


def together(*values):
    return lax.optimization_barrier(values)


def pick(items, index):
    result = items[-1]
    for place in range(len(items) - 2, -1, -1):
        result = jnp.where(index == place, items[place], result)
    return result


def local(queries, keys, values, outputs, out_grads, segment_ids, block_order):
    blocks, sharers = lax.axis_size("blk"), lax.axis_size("head")
    block, place = lax.axis_index("blk"), lax.axis_index("head")
    rows = keys.shape[0]
    window = rows * sharers // 2
    parts = sharers // 2
    key_heads = keys.shape[1] // HEAD_SIZE
    heads_per_group = key_heads // sharers
    chunks = min(CHUNKS, heads_per_group)
    per_piece = heads_per_group // chunks
    slots = lax.dynamic_slice_in_dim(block_order, 2 * block, 2)
    early_slot = (slots[0] > slots[1]).astype(jnp.int32)
    last_block = block == blocks - 1

    def other(turn):
        return lax.rem(place + turn + sharers, sharers)

    def turned(value, turn):
        pairs = [(source, (source + turn) % sharers) for source in range(sharers)]
        return lax.ppermute(value, "head", pairs)

    def shifted(value, step):
        first, end = max(0, -step), min(blocks, blocks - step)
        return lax.ppermute(value, "blk", [(source, source + step) for source in range(first, end)])

    def columns(array, group, chunk):
        pieces = []
        for g in range(sharers):
            start = (g * heads_per_group + chunk * per_piece) * HEAD_SIZE
            pieces.append(array[:, start : start + per_piece * HEAD_SIZE])
        return pick(pieces, group)

    def piece_of(group, chunk):
        return jnp.stack([columns(keys, group, chunk), columns(values, group, chunk)])

    def is_early(device):
        return device // parts == early_slot

    def part_rows(array, device, count):
        if parts == 1:
            return array[:, :count]
        return lax.dynamic_slice_in_dim(array, device % parts * rows, count, 1)

    my_half = pick([slots[0], slots[1]], place // parts)
    start = my_half * window + place % parts * rows
    padded = jnp.concatenate([jnp.full((window,), -1, jnp.int32), segment_ids])
    near = lax.dynamic_slice_in_dim(padded, start, window + rows)
    low = jnp.sum((near[None, :] < near[window:, None]).astype(jnp.int32), axis=1)[None, :]

    row_arrays = (queries, keys, values, outputs, out_grads)
    groups = [other(-turn) for turn in range(sharers)]

    def halves_of(pieces):
        return [
            jnp.concatenate(
                [
                    pick(pieces, lax.rem(place - (slot * parts + p) + sharers, sharers))
                    for p in range(parts)
                ],
                axis=1,
            )
            for slot in (early_slot, 1 - early_slot)
        ]

    halves = []
    for chunk in range(chunks):
        pieces = [piece_of(place, chunk)]
        pieces += [turned(piece_of(other(turn), chunk), turn) for turn in range(1, sharers)]
        halves.append(halves_of(pieces))
    before = [(shifted(early, 1), shifted(late, -1)) for early, late in halves]

    def run(turn, chunk, past, carried):
        *carried, back = attention(
            groups[turn].reshape(1), low, row_arrays, past,
            chunk * per_piece, heads_per_group, tuple(carried),
        )
        return carried, back

    carried, terms, pasts = (), [], []
    for chunk in range(chunks):
        (early, late), (before_early, before_late) = halves[chunk], before[chunk]
        if chunk:
            *carried, before_early, before_late = together(*carried, before_early, before_late)
        before_late = jnp.where(last_block, early, before_late)

        def past_of(device):
            before = jnp.where(is_early(device), before_early, before_late)
            if parts == 1:
                return before
            own = jnp.where(is_early(device), early, late)
            return part_rows(jnp.concatenate([before, own], axis=1), device, window)

        pasts.append([turned(past_of(other(turn)), turn) for turn in range(1, sharers)])
        carried, back = run(0, chunk, past_of(place), carried)
        terms.append([back])

    for chunk in range(chunks):
        for turn in range(1, sharers):
            carried, back = run(turn, chunk, pasts[chunk][turn - 1], carried)
            terms[chunk].append(turned(back, -turn))

    query_grads, *own = carried
    results = ()
    for chunk in range(chunks):
        to_before, to_own = [], []
        for slot in (early_slot, 1 - early_slot):
            if parts == 1:
                to_before.append(pick(terms[chunk], lax.rem(slot - place + sharers, sharers)))
                to_own.append(None)
            else:
                total = jnp.zeros((2, 2 * window, terms[chunk][0].shape[2]), jnp.float32)
                for turn in range(sharers):
                    device = other(turn)
                    mine = jnp.where(device // parts == slot, terms[chunk][turn].astype(jnp.float32), 0.0)
                    wide = jnp.pad(mine, ((0, 0), (window, window), (0, 0)))
                    total += lax.dynamic_slice_in_dim(
                        wide, window - device % parts * rows, 2 * window, 1
                    )
                to_before.append(total[:, :window].astype(jnp.bfloat16))
                to_own.append(total[:, window:])
        for_early, for_late = shifted(to_before[0], -1), shifted(to_before[1], 1)
        for_early = jnp.where(last_block, to_before[1], for_early)
        sums = [
            came if more is None else (came.astype(jnp.float32) + more).astype(jnp.bfloat16)
            for came, more in zip((for_early, for_late), to_own)
        ]

        def rows_of(device):
            return part_rows(jnp.where(is_early(device), sums[0], sums[1]), device, rows)

        for turn in range(sharers):
            back = rows_of(other(turn))
            if turn:
                back = turned(back, turn)
            results = finish(
                groups[turn].reshape(1),
                own,
                back,
                chunk * per_piece,
                heads_per_group,
                tuple(results),
            )
    return (query_grads, *results)


def solution(mesh):
    spread = P(("blk", "head"), None)
    return jax.shard_map(
        local,
        mesh=mesh,
        in_specs=(spread,) * 5 + (P(), P()),
        out_specs=(spread,) * 3,
        check_vma=False,
    )
```

```python
import functools

import jax
import jax.numpy as jnp
from jax import lax
from jax.experimental import pallas as pl
from jax.experimental.pallas import tpu as pltpu
from jax.sharding import PartitionSpec as P

HEAD_SIZE = 128
NEGATIVE = -1e30
LOG2_E = 1.4426950408889634
CHUNKS = 2
TILE = 128
STRIP = 64
VMEM_BYTES = 60 * 1024 * 1024


def dot(left, right, left_dim, right_dim):
    return lax.dot_general(
        left, right, (((left_dim,), (right_dim,)), ((), ())), preferred_element_type=jnp.float32
    )


def strips(count):
    return [slice(start, start + STRIP) for start in range(0, count, STRIP)]


def folded(strip, reduce):
    return reduce(strip.reshape(strip.shape[0] // 8, 8, strip.shape[1]), axis=0)


def attention_body(
    carried, group_ref, need_ref, low_ref, q_ref, k_ref, v_ref, o_ref, do_ref, past_ref, *refs
):
    dq_ref, dk_ref, dv_ref, back_ref = refs[carried : carried + 4]
    k_all, v_all, k_turned, dk_sum, dv_sum, scores, slopes, weights_b, slopes_b = refs[carried + 4 :]
    rows, head = k_ref.shape
    window = past_ref.shape[1]
    members = q_ref.shape[1] // head
    lanes = members * TILE
    scale = head**-0.5
    tiles = range(rows // TILE)
    k_all[:window] = past_ref[0]
    k_all[window:] = k_ref[...]
    v_all[:window] = past_ref[1]
    v_all[window:] = v_ref[...]
    k_turned[...] = k_all[...].T
    dk_sum[...] = jnp.zeros_like(dk_sum)
    dv_sum[...] = jnp.zeros_like(dv_sum)

    def stacked(ref, tile):
        rows_of_tile = slice(tile * TILE, (tile + 1) * TILE)
        return jnp.concatenate(
            [ref[rows_of_tile, m * head : (m + 1) * head] for m in range(members)], axis=0
        )

    def enter(tile, keys):
        queries, grads = stacked(q_ref, tile), stacked(do_ref, tile)
        count = keys.stop - keys.start
        scores[tile, :count] = dot(k_all[keys], queries, 1, 1)
        slopes[tile, :count] = dot(v_all[keys], grads, 1, 1)
        return queries, grads

    def weigh(tile, keys, grads):
        count = keys.stop - keys.start
        product = grads.astype(jnp.float32) * stacked(o_ref, tile).astype(jnp.float32)
        delta = jnp.sum(product.T, axis=0, keepdims=True)
        low = jnp.concatenate([low_ref[:, tile * TILE : (tile + 1) * TILE]] * members, axis=1)
        low = low - keys.start
        lane = lax.broadcasted_iota(jnp.int32, (1, lanes), 1) % TILE

        def visible(strip):
            index = strip.start + lax.broadcasted_iota(jnp.int32, (STRIP, lanes), 0)
            seen = index >= low
            return seen & (index <= count - TILE + lane) if strip.stop > count - TILE else seen

        top = jnp.full((8, lanes), NEGATIVE, jnp.float32)
        for strip in strips(count):
            masked = jnp.where(visible(strip), scores[tile, strip], NEGATIVE)
            top = jnp.maximum(top, folded(masked, jnp.max))
        top = jnp.max(top, axis=0, keepdims=True)
        total = jnp.zeros((8, lanes), jnp.float32)
        for strip in strips(count):
            terms = jnp.exp2((scores[tile, strip] - top) * (scale * LOG2_E))
            terms = jnp.where(visible(strip), terms, 0.0)
            total = total + folded(terms, jnp.sum)
            scores[tile, strip] = terms
        inverse = 1.0 / jnp.sum(total, axis=0, keepdims=True)
        for strip in strips(count):
            weights = scores[tile, strip] * inverse
            weights_b[tile, strip] = weights.astype(jnp.bfloat16)
            slopes_b[tile, strip] = (weights * (slopes[tile, strip] - delta)).astype(jnp.bfloat16)

    def leave(tile, keys, queries, grads):
        count = keys.stop - keys.start
        dv_sum[keys] += dot(weights_b[tile, :count], grads, 1, 0)
        dk_sum[keys] += dot(slopes_b[tile, :count], queries, 1, 0)
        dq = (dot(k_turned[:, keys], slopes_b[tile, :count], 1, 0) * scale).T
        for m in range(members):
            dq_ref[tile * TILE : (tile + 1) * TILE, m * head : (m + 1) * head] = dq[
                m * TILE : (m + 1) * TILE
            ].astype(dq_ref.dtype)

    def straight(past_blocks, past_tiles):
        keys = []
        for tile in tiles:
            first = -past_blocks if tile < past_tiles else max(past_tiles - 1, 0)
            keys.append(slice(window + first * TILE, window + (tile + 1) * TILE))
        entered = {0: enter(0, keys[0])}
        for tile in tiles:
            if tile + 1 in tiles:
                entered[tile + 1] = enter(tile + 1, keys[tile + 1])
            if tile:
                leave(tile - 1, keys[tile - 1], *entered[tile - 1])
            weigh(tile, keys[tile], entered[tile][1])
        leave(tiles[-1], keys[-1], *entered[tiles[-1]])

    for past_blocks, past_tiles in needs(rows, window):
        same = (need_ref[0] == past_blocks) & (need_ref[1] == past_tiles)
        pl.when(same)(functools.partial(straight, past_blocks, past_tiles))
    back_ref[0] = dk_sum[:window].astype(back_ref.dtype)
    back_ref[1] = dv_sum[:window].astype(back_ref.dtype)
    dk_ref[...] = dk_sum[window:]
    dv_ref[...] = dv_sum[window:]


def needs(rows, window):
    most = window // TILE
    pairs = [
        (blocks, tiles)
        for tiles in range(1, rows // TILE + 1)
        for blocks in range(1, most + 2 - tiles)
    ]
    return [(0, 0)] + pairs


def attention(group, need, low, row_arrays, past, first_head, heads_per_group, carried):
    queries, keys, values, outputs, grads = row_arrays
    rows, window, count = keys.shape[0], past.shape[1], past.shape[2] // HEAD_SIZE
    wide = queries.shape[1] // keys.shape[1] * HEAD_SIZE

    def column(step, group_ref, need_ref):
        return (0, group_ref[0] * heads_per_group + first_head + step)

    query_spec = pl.BlockSpec((rows, wide), column)
    key_spec = pl.BlockSpec((rows, HEAD_SIZE), column)
    past_spec = pl.BlockSpec((2, window, HEAD_SIZE), lambda step, *refs: (0, 0, step))
    low_spec = pl.BlockSpec((1, rows), lambda step, *refs: (0, 0))
    square = (rows // TILE, window + TILE, wide // HEAD_SIZE * TILE)
    tiles = count * queries.shape[1] // keys.shape[1] * rows * (window + TILE)
    return pl.pallas_call(
        functools.partial(attention_body, len(carried)),
        grid_spec=pltpu.PrefetchScalarGridSpec(
            num_scalar_prefetch=2,
            grid=(count,),
            in_specs=[low_spec, query_spec, key_spec, key_spec, query_spec, query_spec, past_spec]
            + [pl.BlockSpec(memory_space=pl.ANY)] * len(carried),
            out_specs=[query_spec, key_spec, key_spec, past_spec],
            scratch_shapes=[
                pltpu.VMEM((window + rows, HEAD_SIZE), jnp.bfloat16),
                pltpu.VMEM((window + rows, HEAD_SIZE), jnp.bfloat16),
                pltpu.VMEM((HEAD_SIZE, window + rows), jnp.bfloat16),
                pltpu.VMEM((window + rows, HEAD_SIZE), jnp.float32),
                pltpu.VMEM((window + rows, HEAD_SIZE), jnp.float32),
                pltpu.VMEM(square, jnp.float32),
                pltpu.VMEM(square, jnp.float32),
                pltpu.VMEM(square, jnp.bfloat16),
                pltpu.VMEM(square, jnp.bfloat16),
            ],
        ),
        out_shape=[
            jax.ShapeDtypeStruct(queries.shape, jnp.bfloat16),
            jax.ShapeDtypeStruct(keys.shape, jnp.float32),
            jax.ShapeDtypeStruct(keys.shape, jnp.float32),
            jax.ShapeDtypeStruct(past.shape, jnp.bfloat16),
        ],
        input_output_aliases={9 + i: i for i in range(len(carried))},
        compiler_params=pltpu.CompilerParams(vmem_limit_bytes=VMEM_BYTES),
        cost_estimate=pl.CostEstimate(
            flops=10 * tiles * HEAD_SIZE, bytes_accessed=count * rows * 2400, transcendentals=tiles
        ),
        name="attention",
    )(group, need, low, *row_arrays, past, *carried)


def finish_body(carried, group_ref, dk_ref, dv_ref, back_ref, *refs):
    key_out, value_out = refs[carried:]
    scale = HEAD_SIZE**-0.5
    key_out[...] = ((dk_ref[...] + back_ref[0].astype(jnp.float32)) * scale).astype(key_out.dtype)
    value_out[...] = (dv_ref[...] + back_ref[1].astype(jnp.float32)).astype(value_out.dtype)


def finish(group, own, back, first_head, heads_per_group, carried):
    rows, count = back.shape[1], back.shape[2] // HEAD_SIZE

    def column(step, group_ref):
        return (0, group_ref[0] * heads_per_group + first_head + step)

    key_spec = pl.BlockSpec((rows, HEAD_SIZE), column)
    back_spec = pl.BlockSpec((2, rows, HEAD_SIZE), lambda step, group_ref: (0, 0, step))
    return pl.pallas_call(
        functools.partial(finish_body, len(carried)),
        grid_spec=pltpu.PrefetchScalarGridSpec(
            num_scalar_prefetch=1,
            grid=(count,),
            in_specs=[key_spec, key_spec, back_spec]
            + [pl.BlockSpec(memory_space=pl.ANY)] * len(carried),
            out_specs=[key_spec, key_spec],
        ),
        out_shape=[jax.ShapeDtypeStruct(own[0].shape, jnp.bfloat16)] * 2,
        input_output_aliases={4 + i: i for i in range(len(carried))},
        compiler_params=pltpu.CompilerParams(vmem_limit_bytes=VMEM_BYTES),
        cost_estimate=pl.CostEstimate(
            flops=count * rows * 512, bytes_accessed=count * rows * 2048, transcendentals=0
        ),
        name="finish",
    )(group, *own, back, *carried)


def together(*values):
    return lax.optimization_barrier(values)


def pick(items, index):
    result = items[-1]
    for place in range(len(items) - 2, -1, -1):
        result = jnp.where(index == place, items[place], result)
    return result


def local(queries, keys, values, outputs, out_grads, segment_ids, block_order):
    blocks, sharers = lax.axis_size("blk"), lax.axis_size("head")
    block, place = lax.axis_index("blk"), lax.axis_index("head")
    rows = keys.shape[0]
    window = rows * sharers // 2
    parts = sharers // 2
    key_heads = keys.shape[1] // HEAD_SIZE
    heads_per_group = key_heads // sharers
    chunks = min(CHUNKS, heads_per_group)
    per_piece = heads_per_group // chunks
    slots = lax.dynamic_slice_in_dim(block_order, 2 * block, 2)
    early_slot = (slots[0] > slots[1]).astype(jnp.int32)
    last_block = block == blocks - 1

    def other(turn):
        return lax.rem(place + turn + sharers, sharers)

    def turned(value, turn):
        pairs = [(source, (source + turn) % sharers) for source in range(sharers)]
        return lax.ppermute(value, "head", pairs)

    def shifted(value, step):
        first, end = max(0, -step), min(blocks, blocks - step)
        return lax.ppermute(value, "blk", [(source, source + step) for source in range(first, end)])

    def columns(array, group, chunk):
        pieces = []
        for g in range(sharers):
            start = (g * heads_per_group + chunk * per_piece) * HEAD_SIZE
            pieces.append(array[:, start : start + per_piece * HEAD_SIZE])
        return pick(pieces, group)

    def piece_of(group, chunk):
        return jnp.stack([columns(keys, group, chunk), columns(values, group, chunk)])

    def is_early(device):
        return device // parts == early_slot

    def part_rows(array, device, count):
        if parts == 1:
            return array[:, :count]
        return lax.dynamic_slice_in_dim(array, device % parts * rows, count, 1)

    my_half = pick([slots[0], slots[1]], place // parts)
    start = my_half * window + place % parts * rows
    padded = jnp.concatenate([jnp.full((window,), -1, jnp.int32), segment_ids])
    near = lax.dynamic_slice_in_dim(padded, start, window + rows)
    low = jnp.sum((near[None, :] < near[window:, None]).astype(jnp.int32), axis=1)[None, :]

    past_rows = jnp.sum((low < window).astype(jnp.int32))
    past_keys = jnp.where(past_rows > 0, window - low[0, 0], 0)
    need = (jnp.stack([past_keys, past_rows]) + TILE - 1) // TILE

    row_arrays = (queries, keys, values, outputs, out_grads)
    groups = [other(-turn) for turn in range(sharers)]

    def halves_of(pieces):
        return [
            jnp.concatenate(
                [
                    pick(pieces, lax.rem(place - (slot * parts + p) + sharers, sharers))
                    for p in range(parts)
                ],
                axis=1,
            )
            for slot in (early_slot, 1 - early_slot)
        ]

    halves = []
    for chunk in range(chunks):
        pieces = [piece_of(place, chunk)]
        pieces += [turned(piece_of(other(turn), chunk), turn) for turn in range(1, sharers)]
        halves.append(halves_of(pieces))
    before = [(shifted(early, 1), shifted(late, -1)) for early, late in halves]

    def run(turn, chunk, past, carried):
        *carried, back = attention(
            groups[turn].reshape(1), need, low, row_arrays, past,
            chunk * per_piece, heads_per_group, tuple(carried),
        )
        return carried, back

    carried, terms, pasts = (), [], []
    for chunk in range(chunks):
        (early, late), (before_early, before_late) = halves[chunk], before[chunk]
        if chunk:
            *carried, before_early, before_late = together(*carried, before_early, before_late)
        before_late = jnp.where(last_block, early, before_late)

        def past_of(device):
            before = jnp.where(is_early(device), before_early, before_late)
            if parts == 1:
                return before
            own = jnp.where(is_early(device), early, late)
            return part_rows(jnp.concatenate([before, own], axis=1), device, window)

        pasts.append([turned(past_of(other(turn)), turn) for turn in range(1, sharers)])
        carried, back = run(0, chunk, past_of(place), carried)
        terms.append([back])

    for chunk in range(chunks):
        for turn in range(1, sharers):
            carried, back = run(turn, chunk, pasts[chunk][turn - 1], carried)
            terms[chunk].append(turned(back, -turn))

    query_grads, *own = carried
    results = ()
    for chunk in range(chunks):
        to_before, to_own = [], []
        for slot in (early_slot, 1 - early_slot):
            if parts == 1:
                to_before.append(pick(terms[chunk], lax.rem(slot - place + sharers, sharers)))
                to_own.append(None)
            else:
                total = jnp.zeros((2, 2 * window, terms[chunk][0].shape[2]), jnp.float32)
                for turn in range(sharers):
                    device = other(turn)
                    mine = jnp.where(device // parts == slot, terms[chunk][turn].astype(jnp.float32), 0.0)
                    wide = jnp.pad(mine, ((0, 0), (window, window), (0, 0)))
                    total += lax.dynamic_slice_in_dim(
                        wide, window - device % parts * rows, 2 * window, 1
                    )
                to_before.append(total[:, :window].astype(jnp.bfloat16))
                to_own.append(total[:, window:])
        for_early, for_late = shifted(to_before[0], -1), shifted(to_before[1], 1)
        for_early = jnp.where(last_block, to_before[1], for_early)
        sums = [
            came if more is None else (came.astype(jnp.float32) + more).astype(jnp.bfloat16)
            for came, more in zip((for_early, for_late), to_own)
        ]

        def rows_of(device):
            return part_rows(jnp.where(is_early(device), sums[0], sums[1]), device, rows)

        for turn in range(sharers):
            back = rows_of(other(turn))
            if turn:
                back = turned(back, turn)
            results = finish(
                groups[turn].reshape(1),
                own,
                back,
                chunk * per_piece,
                heads_per_group,
                tuple(results),
            )
    return (query_grads, *results)


def solution(mesh):
    spread = P(("blk", "head"), None)
    return jax.shard_map(
        local,
        mesh=mesh,
        in_specs=(spread,) * 5 + (P(), P()),
        out_specs=(spread,) * 3,
        check_vma=False,
    )
```

```python
import functools

import jax
import jax.numpy as jnp
from jax import lax
from jax.experimental import pallas as pl
from jax.experimental.pallas import tpu as pltpu
from jax.sharding import PartitionSpec as P

HEAD_SIZE = 128
NEGATIVE = -1e30
LOG2_E = 1.4426950408889634
CHUNKS = 2
TILE = 128
STRIP = 64
VMEM_BYTES = 60 * 1024 * 1024


def dot(left, right, left_dim, right_dim):
    return lax.dot_general(
        left, right, (((left_dim,), (right_dim,)), ((), ())), preferred_element_type=jnp.float32
    )


def strips(count):
    return [slice(start, start + STRIP) for start in range(0, count, STRIP)]


def folded(strip, reduce):
    return reduce(strip.reshape(strip.shape[0] // 8, 8, strip.shape[1]), axis=0)


def arrange_body(q_ref, k_ref, v_ref, o_ref, do_ref, q_out, do_out, delta_out, k_out, k_turned_out, v_out):
    rows, head = k_ref.shape
    members = q_ref.shape[1] // head
    for tile in range(rows // TILE):
        own = slice(tile * TILE, (tile + 1) * TILE)
        for m in range(members):
            place = slice((tile * members + m) * TILE, (tile * members + m + 1) * TILE)
            columns = slice(m * head, (m + 1) * head)
            q_out[0, place] = q_ref[own, columns]
            do_out[0, place] = do_ref[own, columns]
            product = do_ref[own, columns].astype(jnp.float32) * o_ref[own, columns].astype(jnp.float32)
            delta_out[0, :, place] = jnp.sum(product.T, axis=0, keepdims=True)
    k_out[0] = k_ref[...]
    k_turned_out[0] = k_ref[...].T
    v_out[0] = v_ref[...]


def arrange(row_arrays, first_head, heads_per_group, per_piece):
    queries, keys, values, outputs, grads = row_arrays
    rows, members = keys.shape[0], queries.shape[1] // keys.shape[1]
    groups = keys.shape[1] // HEAD_SIZE // heads_per_group
    count = groups * per_piece

    def column(group, step):
        return (0, group * heads_per_group + first_head + step)

    def leading(group, step):
        return (group * per_piece + step, 0, 0)

    query_spec = pl.BlockSpec((rows, members * HEAD_SIZE), column)
    key_spec = pl.BlockSpec((rows, HEAD_SIZE), column)
    shapes = [
        ((members * rows, HEAD_SIZE), jnp.bfloat16),
        ((members * rows, HEAD_SIZE), jnp.bfloat16),
        ((1, members * rows), jnp.float32),
        ((rows, HEAD_SIZE), jnp.bfloat16),
        ((HEAD_SIZE, rows), jnp.bfloat16),
        ((rows, HEAD_SIZE), jnp.bfloat16),
    ]
    return pl.pallas_call(
        arrange_body,
        grid=(groups, per_piece),
        in_specs=[query_spec, key_spec, key_spec, query_spec, query_spec],
        out_specs=[pl.BlockSpec((1, *shape), leading) for shape, _ in shapes],
        out_shape=[jax.ShapeDtypeStruct((count, *shape), dtype) for shape, dtype in shapes],
        compiler_params=pltpu.CompilerParams(vmem_limit_bytes=VMEM_BYTES),
        cost_estimate=pl.CostEstimate(
            flops=count * rows * 1024, bytes_accessed=count * rows * 4096, transcendentals=0
        ),
        name="arrange",
    )(queries, keys, values, outputs, grads)


def attention_body(
    carried, group_ref, low_ref, q_ref, do_ref, delta_ref, k_ref, k_turned_ref, v_ref, past_ref, *refs
):
    dq_ref, dk_ref, dv_ref, back_ref = refs[carried : carried + 4]
    k_all, v_all, k_turned, dk_sum, dv_sum, scores, slopes, weights_b, slopes_b = refs[carried + 4 :]
    rows, head = k_ref.shape[1:]
    window = past_ref.shape[1]
    members = q_ref.shape[1] // rows
    span, lanes = window + TILE, members * TILE
    scale = head**-0.5
    k_all[:window] = past_ref[0]
    k_all[window:] = k_ref[0]
    v_all[:window] = past_ref[1]
    v_all[window:] = v_ref[0]
    k_turned[:, :window] = past_ref[0].T
    k_turned[:, window:] = k_turned_ref[0]
    dk_sum[...] = jnp.zeros_like(dk_sum)
    dv_sum[...] = jnp.zeros_like(dv_sum)
    lane = lax.broadcasted_iota(jnp.int32, (1, lanes), 1) % TILE
    tiles = range(rows // TILE)

    def enter(tile):
        keys = pl.ds(tile * TILE, span)
        place = pl.ds(tile * lanes, lanes)
        queries, grads = q_ref[0, place], do_ref[0, place]
        scores[tile] = dot(k_all[keys], queries, 1, 1)
        slopes[tile] = dot(v_all[keys], grads, 1, 1)
        return queries, grads

    def weigh(tile):
        start = tile * TILE
        delta = delta_ref[0, :, pl.ds(tile * lanes, lanes)]
        low = jnp.concatenate([low_ref[:, start : start + TILE]] * members, axis=1) - start

        def visible(strip):
            index = strip.start + lax.broadcasted_iota(jnp.int32, (STRIP, lanes), 0)
            seen = index >= low
            return seen & (index <= window + lane) if strip.stop > window else seen

        top = jnp.full((8, lanes), NEGATIVE, jnp.float32)
        for strip in strips(span):
            masked = jnp.where(visible(strip), scores[tile, strip], NEGATIVE)
            top = jnp.maximum(top, folded(masked, jnp.max))
        top = jnp.max(top, axis=0, keepdims=True)
        total = jnp.zeros((8, lanes), jnp.float32)
        for strip in strips(span):
            terms = jnp.exp2((scores[tile, strip] - top) * (scale * LOG2_E))
            terms = jnp.where(visible(strip), terms, 0.0)
            total = total + folded(terms, jnp.sum)
            scores[tile, strip] = terms
        inverse = 1.0 / jnp.sum(total, axis=0, keepdims=True)
        for strip in strips(span):
            weights = scores[tile, strip] * inverse
            weights_b[tile, strip] = weights.astype(jnp.bfloat16)
            slopes_b[tile, strip] = (weights * (slopes[tile, strip] - delta)).astype(jnp.bfloat16)

    def leave(tile, queries, grads):
        start = tile * TILE
        keys = pl.ds(start, span)
        dv_sum[keys] += dot(weights_b[tile], grads, 1, 0)
        dk_sum[keys] += dot(slopes_b[tile], queries, 1, 0)
        dq = (dot(k_turned[:, keys], slopes_b[tile], 1, 0) * scale).T
        for m in range(members):
            dq_ref[start : start + TILE, m * head : (m + 1) * head] = dq[
                m * TILE : (m + 1) * TILE
            ].astype(dq_ref.dtype)

    entered = {0: enter(0)}
    for tile in tiles:
        if tile + 1 in tiles:
            entered[tile + 1] = enter(tile + 1)
        if tile:
            leave(tile - 1, *entered[tile - 1])
        weigh(tile)
    leave(tiles[-1], *entered[tiles[-1]])
    back_ref[0] = dk_sum[:window].astype(back_ref.dtype)
    back_ref[1] = dv_sum[:window].astype(back_ref.dtype)
    dk_ref[0] = dk_sum[window:].astype(dk_ref.dtype)
    dv_ref[0] = dv_sum[window:].astype(dv_ref.dtype)


def attention(group, low, arranged, past, first_head, heads_per_group, heads, carried):
    rows, window, count = arranged[3].shape[1], past.shape[1], past.shape[2] // HEAD_SIZE
    members = arranged[0].shape[1] // rows

    def leading(step, group_ref):
        return (group_ref[0] * count + step, 0, 0)

    def column(step, group_ref):
        return (0, group_ref[0] * heads_per_group + first_head + step)

    past_spec = pl.BlockSpec((2, window, HEAD_SIZE), lambda step, group_ref: (0, 0, step))
    low_spec = pl.BlockSpec((1, rows), lambda step, group_ref: (0, 0))
    own_spec = pl.BlockSpec((1, rows, HEAD_SIZE), lambda step, group_ref: (step, 0, 0))
    own_shape = jax.ShapeDtypeStruct((count, rows, HEAD_SIZE), jnp.bfloat16)
    square = (rows // TILE, window + TILE, members * TILE)
    tiles = count * members * rows * (window + TILE)
    return pl.pallas_call(
        functools.partial(attention_body, len(carried)),
        grid_spec=pltpu.PrefetchScalarGridSpec(
            num_scalar_prefetch=1,
            grid=(count,),
            in_specs=[low_spec]
            + [pl.BlockSpec((1, *array.shape[1:]), leading) for array in arranged]
            + [past_spec]
            + [pl.BlockSpec(memory_space=pl.ANY)] * len(carried),
            out_specs=[pl.BlockSpec((rows, members * HEAD_SIZE), column), own_spec, own_spec, past_spec],
            scratch_shapes=[
                pltpu.VMEM((window + rows, HEAD_SIZE), jnp.bfloat16),
                pltpu.VMEM((window + rows, HEAD_SIZE), jnp.bfloat16),
                pltpu.VMEM((HEAD_SIZE, window + rows), jnp.bfloat16),
                pltpu.VMEM((window + rows, HEAD_SIZE), jnp.float32),
                pltpu.VMEM((window + rows, HEAD_SIZE), jnp.float32),
                pltpu.VMEM(square, jnp.float32),
                pltpu.VMEM(square, jnp.float32),
                pltpu.VMEM(square, jnp.bfloat16),
                pltpu.VMEM(square, jnp.bfloat16),
            ],
        ),
        out_shape=[
            jax.ShapeDtypeStruct((rows, heads * members * HEAD_SIZE), jnp.bfloat16),
            own_shape,
            own_shape,
            jax.ShapeDtypeStruct(past.shape, jnp.bfloat16),
        ],
        input_output_aliases={9 + i: i for i in range(len(carried))},
        compiler_params=pltpu.CompilerParams(vmem_limit_bytes=VMEM_BYTES),
        cost_estimate=pl.CostEstimate(
            flops=10 * tiles * HEAD_SIZE, bytes_accessed=count * rows * 2400, transcendentals=tiles
        ),
        name="attention",
    )(group, low, *arranged, past, *carried)


def finish_body(carried, group_ref, dk_ref, dv_ref, back_ref, *refs):
    key_out, value_out = refs[carried:]
    sums = [
        own[0].astype(jnp.float32) + back_ref[i].astype(jnp.float32)
        for i, own in enumerate((dk_ref, dv_ref))
    ]
    key_out[...] = (sums[0] * HEAD_SIZE**-0.5).astype(key_out.dtype)
    value_out[...] = sums[1].astype(value_out.dtype)


def finish(group, own, back, first_head, heads_per_group, heads, carried):
    rows, count = back.shape[1], back.shape[2] // HEAD_SIZE

    def column(step, group_ref):
        return (0, group_ref[0] * heads_per_group + first_head + step)

    key_spec = pl.BlockSpec((rows, HEAD_SIZE), column)
    own_spec = pl.BlockSpec((1, rows, HEAD_SIZE), lambda step, group_ref: (step, 0, 0))
    back_spec = pl.BlockSpec((2, rows, HEAD_SIZE), lambda step, group_ref: (0, 0, step))
    return pl.pallas_call(
        functools.partial(finish_body, len(carried)),
        grid_spec=pltpu.PrefetchScalarGridSpec(
            num_scalar_prefetch=1,
            grid=(count,),
            in_specs=[own_spec, own_spec, back_spec]
            + [pl.BlockSpec(memory_space=pl.ANY)] * len(carried),
            out_specs=[key_spec, key_spec],
        ),
        out_shape=[jax.ShapeDtypeStruct((rows, heads * HEAD_SIZE), jnp.bfloat16)] * 2,
        input_output_aliases={4 + i: i for i in range(len(carried))},
        compiler_params=pltpu.CompilerParams(vmem_limit_bytes=VMEM_BYTES),
        cost_estimate=pl.CostEstimate(
            flops=count * rows * 512, bytes_accessed=count * rows * 2048, transcendentals=0
        ),
        name="finish",
    )(group, *own, back, *carried)


def together(*values):
    return lax.optimization_barrier(values)


def pick(items, index):
    result = items[-1]
    for place in range(len(items) - 2, -1, -1):
        result = jnp.where(index == place, items[place], result)
    return result


def local(queries, keys, values, outputs, out_grads, segment_ids, block_order):
    blocks, sharers = lax.axis_size("blk"), lax.axis_size("head")
    block, place = lax.axis_index("blk"), lax.axis_index("head")
    rows = keys.shape[0]
    window = rows * sharers // 2
    parts = sharers // 2
    key_heads = keys.shape[1] // HEAD_SIZE
    heads_per_group = key_heads // sharers
    chunks = min(CHUNKS, heads_per_group)
    per_piece = heads_per_group // chunks
    slots = lax.dynamic_slice_in_dim(block_order, 2 * block, 2)
    early_slot = (slots[0] > slots[1]).astype(jnp.int32)
    last_block = block == blocks - 1

    def other(turn):
        return lax.rem(place + turn + sharers, sharers)

    def turned(value, turn):
        pairs = [(source, (source + turn) % sharers) for source in range(sharers)]
        return lax.ppermute(value, "head", pairs)

    def shifted(value, step):
        first, end = max(0, -step), min(blocks, blocks - step)
        return lax.ppermute(value, "blk", [(source, source + step) for source in range(first, end)])

    def columns(array, group, chunk):
        pieces = []
        for g in range(sharers):
            start = (g * heads_per_group + chunk * per_piece) * HEAD_SIZE
            pieces.append(array[:, start : start + per_piece * HEAD_SIZE])
        return pick(pieces, group)

    def piece_of(group, chunk):
        return jnp.stack([columns(keys, group, chunk), columns(values, group, chunk)])

    def is_early(device):
        return device // parts == early_slot

    def part_rows(array, device, count):
        if parts == 1:
            return array[:, :count]
        return lax.dynamic_slice_in_dim(array, device % parts * rows, count, 1)

    my_half = pick([slots[0], slots[1]], place // parts)
    start = my_half * window + place % parts * rows
    padded = jnp.concatenate([jnp.full((window,), -1, jnp.int32), segment_ids])
    near = lax.dynamic_slice_in_dim(padded, start, window + rows)
    low = jnp.sum((near[None, :] < near[window:, None]).astype(jnp.int32), axis=1)[None, :]

    row_arrays = (queries, keys, values, outputs, out_grads)
    groups = [other(-turn) for turn in range(sharers)]

    def halves_of(pieces):
        return [
            jnp.concatenate(
                [
                    pick(pieces, lax.rem(place - (slot * parts + p) + sharers, sharers))
                    for p in range(parts)
                ],
                axis=1,
            )
            for slot in (early_slot, 1 - early_slot)
        ]

    arranged, halves = [], []
    for chunk in range(chunks):
        pieces = [piece_of(place, chunk)]
        pieces += [turned(piece_of(other(turn), chunk), turn) for turn in range(1, sharers)]
        arrays = arrange(row_arrays, chunk * per_piece, heads_per_group, per_piece)
        *arrays, pieces[-1] = together(*arrays, pieces[-1])
        arranged.append(arrays)
        halves.append(halves_of(pieces))
    before = [(shifted(early, 1), shifted(late, -1)) for early, late in halves]

    def run(turn, chunk, past, carried):
        query_grads, *own[chunk, turn], back = attention(
            groups[turn].reshape(1), low, arranged[chunk], past,
            chunk * per_piece, heads_per_group, key_heads, carried,
        )
        return (query_grads,), back

    carried, own, terms, pasts = (), {}, [], []
    for chunk in range(chunks):
        (early, late), (before_early, before_late) = halves[chunk], before[chunk]
        if chunk:
            *carried, before_early, before_late = together(*carried, before_early, before_late)
        before_late = jnp.where(last_block, early, before_late)

        def past_of(device):
            before = jnp.where(is_early(device), before_early, before_late)
            if parts == 1:
                return before
            own = jnp.where(is_early(device), early, late)
            return part_rows(jnp.concatenate([before, own], axis=1), device, window)

        pasts.append([turned(past_of(other(turn)), turn) for turn in range(1, sharers)])
        carried, back = run(0, chunk, past_of(place), carried)
        terms.append([back])

    for chunk in range(chunks):
        for turn in range(1, sharers):
            carried, back = run(turn, chunk, pasts[chunk][turn - 1], carried)
            terms[chunk].append(turned(back, -turn))

    (query_grads,) = carried
    results = ()
    for chunk in range(chunks):
        to_before, to_own = [], []
        for slot in (early_slot, 1 - early_slot):
            if parts == 1:
                to_before.append(pick(terms[chunk], lax.rem(slot - place + sharers, sharers)))
                to_own.append(None)
            else:
                total = jnp.zeros((2, 2 * window, terms[chunk][0].shape[2]), jnp.float32)
                for turn in range(sharers):
                    device = other(turn)
                    mine = jnp.where(device // parts == slot, terms[chunk][turn].astype(jnp.float32), 0.0)
                    wide = jnp.pad(mine, ((0, 0), (window, window), (0, 0)))
                    total += lax.dynamic_slice_in_dim(
                        wide, window - device % parts * rows, 2 * window, 1
                    )
                to_before.append(total[:, :window].astype(jnp.bfloat16))
                to_own.append(total[:, window:])
        for_early, for_late = shifted(to_before[0], -1), shifted(to_before[1], 1)
        for_early = jnp.where(last_block, to_before[1], for_early)
        sums = [
            came if more is None else (came.astype(jnp.float32) + more).astype(jnp.bfloat16)
            for came, more in zip((for_early, for_late), to_own)
        ]

        def rows_of(device):
            return part_rows(jnp.where(is_early(device), sums[0], sums[1]), device, rows)

        for turn in range(sharers):
            back = rows_of(other(turn))
            if turn:
                back = turned(back, turn)
            results = finish(
                groups[turn].reshape(1), own[chunk, turn], back,
                chunk * per_piece, heads_per_group, key_heads, tuple(results),
            )
    return (query_grads, *results)


def solution(mesh):
    spread = P(("blk", "head"), None)
    return jax.shard_map(
        local,
        mesh=mesh,
        in_specs=(spread,) * 5 + (P(), P()),
        out_specs=(spread,) * 3,
        check_vma=False,
    )
```

```python
import functools

import jax
import jax.numpy as jnp
from jax import lax
from jax.experimental import pallas as pl
from jax.experimental.pallas import tpu as pltpu
from jax.sharding import PartitionSpec as P

HEAD_SIZE = 128
NEGATIVE = -1e30
LOG2_E = 1.4426950408889634
TILE = 128
STRIP = 64
VMEM_BYTES = 60 * 1024 * 1024


def dot(left, right, left_dim, right_dim):
    return lax.dot_general(
        left, right, (((left_dim,), (right_dim,)), ((), ())), preferred_element_type=jnp.float32
    )


def strips(count):
    return [slice(start, start + STRIP) for start in range(0, count, STRIP)]


def folded(strip, reduce):
    return reduce(strip.reshape(strip.shape[0] // 8, 8, strip.shape[1]), axis=0)


def arrange_body(q_ref, k_ref, v_ref, o_ref, do_ref, q_out, do_out, delta_out, k_out, k_turned_out, v_out):
    rows, head = k_ref.shape
    members = q_ref.shape[1] // head
    for tile in range(rows // TILE):
        own = slice(tile * TILE, (tile + 1) * TILE)
        for m in range(members):
            place = slice((tile * members + m) * TILE, (tile * members + m + 1) * TILE)
            columns = slice(m * head, (m + 1) * head)
            q_out[0, place] = q_ref[own, columns]
            do_out[0, place] = do_ref[own, columns]
            product = do_ref[own, columns].astype(jnp.float32) * o_ref[own, columns].astype(jnp.float32)
            delta_out[0, :, place] = jnp.sum(product.T, axis=0, keepdims=True)
    k_out[0] = k_ref[...]
    k_turned_out[0] = k_ref[...].T
    v_out[0] = v_ref[...]


def arrange(row_arrays, first_head, heads_per_group, per_piece):
    queries, keys, values, outputs, grads = row_arrays
    rows, members = keys.shape[0], queries.shape[1] // keys.shape[1]
    groups = keys.shape[1] // HEAD_SIZE // heads_per_group
    count = groups * per_piece

    def column(group, step):
        return (0, group * heads_per_group + first_head + step)

    def leading(group, step):
        return (group * per_piece + step, 0, 0)

    query_spec = pl.BlockSpec((rows, members * HEAD_SIZE), column)
    key_spec = pl.BlockSpec((rows, HEAD_SIZE), column)
    shapes = [
        ((members * rows, HEAD_SIZE), jnp.bfloat16),
        ((members * rows, HEAD_SIZE), jnp.bfloat16),
        ((1, members * rows), jnp.float32),
        ((rows, HEAD_SIZE), jnp.bfloat16),
        ((HEAD_SIZE, rows), jnp.bfloat16),
        ((rows, HEAD_SIZE), jnp.bfloat16),
    ]
    return pl.pallas_call(
        arrange_body,
        grid=(groups, per_piece),
        in_specs=[query_spec, key_spec, key_spec, query_spec, query_spec],
        out_specs=[pl.BlockSpec((1, *shape), leading) for shape, _ in shapes],
        out_shape=[jax.ShapeDtypeStruct((count, *shape), dtype) for shape, dtype in shapes],
        compiler_params=pltpu.CompilerParams(vmem_limit_bytes=VMEM_BYTES),
        name="arrange",
    )(queries, keys, values, outputs, grads)


def attention_body(
    carried, group_ref, low_ref, q_ref, do_ref, delta_ref, k_ref, k_turned_ref, v_ref, past_ref, *refs
):
    dq_ref, dk_ref, dv_ref, back_ref = refs[carried : carried + 4]
    k_all, v_all, k_turned, dk_sum, dv_sum, scores, slopes, weights_b, slopes_b = refs[carried + 4 :]
    rows, head = k_ref.shape[1:]
    window = past_ref.shape[1]
    members = q_ref.shape[1] // rows
    span, lanes = window + TILE, members * TILE
    scale = head**-0.5
    k_all[:window] = past_ref[0]
    k_all[window:] = k_ref[0]
    v_all[:window] = past_ref[1]
    v_all[window:] = v_ref[0]
    k_turned[:, :window] = past_ref[0].T
    k_turned[:, window:] = k_turned_ref[0]
    dk_sum[...] = jnp.zeros_like(dk_sum)
    dv_sum[...] = jnp.zeros_like(dv_sum)
    lane = lax.broadcasted_iota(jnp.int32, (1, lanes), 1) % TILE
    tiles = range(rows // TILE)

    def enter(tile):
        keys = pl.ds(tile * TILE, span)
        place = pl.ds(tile * lanes, lanes)
        queries, grads = q_ref[0, place], do_ref[0, place]
        scores[tile] = dot(k_all[keys], queries, 1, 1)
        slopes[tile] = dot(v_all[keys], grads, 1, 1)
        return queries, grads

    def weigh(tile):
        start = tile * TILE
        delta = delta_ref[0, :, pl.ds(tile * lanes, lanes)]
        low = jnp.concatenate([low_ref[:, start : start + TILE]] * members, axis=1) - start

        def visible(strip):
            index = strip.start + lax.broadcasted_iota(jnp.int32, (STRIP, lanes), 0)
            seen = index >= low
            return seen & (index <= window + lane) if strip.stop > window else seen

        top = jnp.full((8, lanes), NEGATIVE, jnp.float32)
        for strip in strips(span):
            masked = jnp.where(visible(strip), scores[tile, strip], NEGATIVE)
            top = jnp.maximum(top, folded(masked, jnp.max))
        top = jnp.max(top, axis=0, keepdims=True)
        total = jnp.zeros((8, lanes), jnp.float32)
        for strip in strips(span):
            terms = jnp.exp2((scores[tile, strip] - top) * (scale * LOG2_E))
            terms = jnp.where(visible(strip), terms, 0.0)
            total = total + folded(terms, jnp.sum)
            scores[tile, strip] = terms
        inverse = 1.0 / jnp.sum(total, axis=0, keepdims=True)
        for strip in strips(span):
            weights = scores[tile, strip] * inverse
            weights_b[tile, strip] = weights.astype(jnp.bfloat16)
            slopes_b[tile, strip] = (weights * (slopes[tile, strip] - delta)).astype(jnp.bfloat16)

    def leave(tile, queries, grads):
        start = tile * TILE
        keys = pl.ds(start, span)
        dv_sum[keys] += dot(weights_b[tile], grads, 1, 0)
        dk_sum[keys] += dot(slopes_b[tile], queries, 1, 0)
        dq = (dot(k_turned[:, keys], slopes_b[tile], 1, 0) * scale).T
        for m in range(members):
            dq_ref[start : start + TILE, m * head : (m + 1) * head] = dq[
                m * TILE : (m + 1) * TILE
            ].astype(dq_ref.dtype)

    entered = {0: enter(0)}
    for tile in tiles:
        if tile + 1 in tiles:
            entered[tile + 1] = enter(tile + 1)
        if tile:
            leave(tile - 1, *entered[tile - 1])
        weigh(tile)
    leave(tiles[-1], *entered[tiles[-1]])
    back_ref[0] = dk_sum[:window].astype(back_ref.dtype)
    back_ref[1] = dv_sum[:window].astype(back_ref.dtype)
    dk_ref[0] = dk_sum[window:].astype(dk_ref.dtype)
    dv_ref[0] = dv_sum[window:].astype(dv_ref.dtype)


def attention(group, low, arranged, past, first_head, per_group, heads_per_group, heads, carried):
    rows, window, count = arranged[3].shape[1], past.shape[1], past.shape[2] // HEAD_SIZE
    members = arranged[0].shape[1] // rows

    def leading(step, group_ref):
        return (group_ref[0] * per_group + step, 0, 0)

    def column(step, group_ref):
        group = group_ref[0] + step // per_group
        return (0, group * heads_per_group + first_head + step % per_group)

    past_spec = pl.BlockSpec((2, window, HEAD_SIZE), lambda step, group_ref: (0, 0, step))
    low_spec = pl.BlockSpec((1, rows), lambda step, group_ref: (0, 0))
    own_spec = pl.BlockSpec((1, rows, HEAD_SIZE), lambda step, group_ref: (step, 0, 0))
    own_shape = jax.ShapeDtypeStruct((count, rows, HEAD_SIZE), jnp.bfloat16)
    square = (rows // TILE, window + TILE, members * TILE)
    return pl.pallas_call(
        functools.partial(attention_body, len(carried)),
        grid_spec=pltpu.PrefetchScalarGridSpec(
            num_scalar_prefetch=1,
            grid=(count,),
            in_specs=[low_spec]
            + [pl.BlockSpec((1, *array.shape[1:]), leading) for array in arranged]
            + [past_spec]
            + [pl.BlockSpec(memory_space=pl.ANY)] * len(carried),
            out_specs=[pl.BlockSpec((rows, members * HEAD_SIZE), column), own_spec, own_spec, past_spec],
            scratch_shapes=[
                pltpu.VMEM((window + rows, HEAD_SIZE), jnp.bfloat16),
                pltpu.VMEM((window + rows, HEAD_SIZE), jnp.bfloat16),
                pltpu.VMEM((HEAD_SIZE, window + rows), jnp.bfloat16),
                pltpu.VMEM((window + rows, HEAD_SIZE), jnp.float32),
                pltpu.VMEM((window + rows, HEAD_SIZE), jnp.float32),
                pltpu.VMEM(square, jnp.float32),
                pltpu.VMEM(square, jnp.float32),
                pltpu.VMEM(square, jnp.bfloat16),
                pltpu.VMEM(square, jnp.bfloat16),
            ],
        ),
        out_shape=[
            jax.ShapeDtypeStruct((rows, heads * members * HEAD_SIZE), jnp.bfloat16),
            own_shape,
            own_shape,
            jax.ShapeDtypeStruct(past.shape, jnp.bfloat16),
        ],
        input_output_aliases={9 + i: i for i in range(len(carried))},
        compiler_params=pltpu.CompilerParams(vmem_limit_bytes=VMEM_BYTES),
        name="attention",
    )(group, low, *arranged, past, *carried)


def finish_body(carried, group_ref, dk_ref, dv_ref, back_ref, *refs):
    key_out, value_out = refs[carried:]
    sums = [
        own[0].astype(jnp.float32) + back_ref[i].astype(jnp.float32)
        for i, own in enumerate((dk_ref, dv_ref))
    ]
    key_out[...] = (sums[0] * HEAD_SIZE**-0.5).astype(key_out.dtype)
    value_out[...] = sums[1].astype(value_out.dtype)


def finish(group, own, back, first_head, per_group, heads_per_group, heads, carried):
    rows, count = back.shape[1], back.shape[2] // HEAD_SIZE

    def column(step, group_ref):
        group = group_ref[0] + step // per_group
        return (0, group * heads_per_group + first_head + step % per_group)

    key_spec = pl.BlockSpec((rows, HEAD_SIZE), column)
    own_spec = pl.BlockSpec((1, rows, HEAD_SIZE), lambda step, group_ref: (step, 0, 0))
    back_spec = pl.BlockSpec((2, rows, HEAD_SIZE), lambda step, group_ref: (0, 0, step))
    return pl.pallas_call(
        functools.partial(finish_body, len(carried)),
        grid_spec=pltpu.PrefetchScalarGridSpec(
            num_scalar_prefetch=1,
            grid=(count,),
            in_specs=[own_spec, own_spec, back_spec]
            + [pl.BlockSpec(memory_space=pl.ANY)] * len(carried),
            out_specs=[key_spec, key_spec],
        ),
        out_shape=[jax.ShapeDtypeStruct((rows, heads * HEAD_SIZE), jnp.bfloat16)] * 2,
        input_output_aliases={4 + i: i for i in range(len(carried))},
        compiler_params=pltpu.CompilerParams(vmem_limit_bytes=VMEM_BYTES),
        name="finish",
    )(group, *own, back, *carried)


def together(*values):
    return lax.optimization_barrier(values)


def pick(items, index):
    result = items[-1]
    for place in range(len(items) - 2, -1, -1):
        result = jnp.where(index == place, items[place], result)
    return result


def plan(heads_per_group, sharers):
    direct = heads_per_group // 4 if sharers == 2 else 0
    rest = heads_per_group - direct
    large = (2 * rest + 2) // 3
    chunks = [(direct, large), (direct + large, rest - large)]
    return direct, [chunk for chunk in chunks if chunk[1]]


def local(queries, keys, values, outputs, out_grads, segment_ids, block_order):
    blocks, sharers = lax.axis_size("blk"), lax.axis_size("head")
    block, place = lax.axis_index("blk"), lax.axis_index("head")
    rows = keys.shape[0]
    window = rows * sharers // 2
    parts = sharers // 2
    key_heads = keys.shape[1] // HEAD_SIZE
    heads_per_group = key_heads // sharers
    direct, chunks = plan(heads_per_group, sharers)
    last_block = block == blocks - 1

    def early_slot_of(block):
        slots = lax.dynamic_slice_in_dim(block_order, 2 * jnp.clip(block, 0, blocks - 1), 2)
        return (slots[0] > slots[1]).astype(jnp.int32)

    early_slot = early_slot_of(block)

    def other(turn):
        return lax.rem(place + turn + sharers, sharers)

    def turned(value, turn):
        pairs = [(source, (source + turn) % sharers) for source in range(sharers)]
        return lax.ppermute(value, "head", pairs)

    def shifted(value, step):
        first, end = max(0, -step), min(blocks, blocks - step)
        return lax.ppermute(value, "blk", [(source, source + step) for source in range(first, end)])

    def columns(array, group, first, count):
        start = (group * heads_per_group + first) * HEAD_SIZE
        return array[:, start : start + count * HEAD_SIZE]

    def piece_of(group, first, count):
        return jnp.stack(
            [
                pick([columns(array, g, first, count) for g in range(sharers)], group)
                for array in (keys, values)
            ]
        )

    def is_early(device):
        return device // parts == early_slot

    def part_rows(array, device, count):
        if parts == 1:
            return array[:, :count]
        return lax.dynamic_slice_in_dim(array, device % parts * rows, count, 1)

    my_slots = lax.dynamic_slice_in_dim(block_order, 2 * block, 2)
    my_half = pick([my_slots[0], my_slots[1]], place // parts)
    start = my_half * window + place % parts * rows
    padded = jnp.concatenate([jnp.full((window,), -1, jnp.int32), segment_ids])
    near = lax.dynamic_slice_in_dim(padded, start, window + rows)
    low = jnp.sum((near[None, :] < near[window:, None]).astype(jnp.int32), axis=1)[None, :]

    row_arrays = (queries, keys, values, outputs, out_grads)
    groups = [other(-turn) for turn in range(sharers)]
    early = is_early(place)

    def halves_of(pieces):
        return [
            jnp.concatenate(
                [
                    pick(pieces, lax.rem(place - (slot * parts + p) + sharers, sharers))
                    for p in range(parts)
                ],
                axis=1,
            )
            for slot in (early_slot, 1 - early_slot)
        ]

    pieces = []
    for first, count in chunks:
        sent = [piece_of(other(turn), first, count) for turn in range(1, sharers)]
        if not pieces:
            key_rows, value_rows, _ = together(keys, values, sent[0])
        pieces.append(
            [piece_of(place, first, count)]
            + [turned(piece, turn) for turn, piece in enumerate(sent, 1)]
        )
    arranged = []
    for chunk, (first, count) in enumerate(chunks):
        arrays = arrange(row_arrays, first, heads_per_group, count)
        *arrays, pieces[chunk][-1] = together(*arrays, pieces[chunk][-1])
        arranged.append(arrays)
    if direct:
        straight = jnp.stack(
            [
                jnp.concatenate([columns(array, g, 0, direct) for g in range(sharers)], axis=1)
                for array in (key_rows, value_rows)
            ]
        )
        from_left, from_right = shifted(straight, 1), shifted(straight, -1)
        same_left = early_slot_of(block - 1) == early_slot
        same_right = (early_slot_of(block + 1) == early_slot) & ~last_block
        mine = jnp.where(early, from_left, from_right)
        theirs = jnp.where(early, jnp.where(last_block, straight, from_right), from_left)
        direct_past = jnp.where(jnp.where(early, same_left, same_right), mine, turned(theirs, 1))
        direct_arranged = arrange(row_arrays, 0, heads_per_group, direct)
    halves = [halves_of(chunk_pieces) for chunk_pieces in pieces]
    before = [(shifted(early_half, 1), shifted(late_half, -1)) for early_half, late_half in halves]

    carried, own, terms, pasts = (), {}, {}, []

    def run(key, group, arrays, past, first, per_group, carried):
        query_grads, *own[key], terms[key] = attention(
            group.reshape(1), low, arrays, past, first, per_group, heads_per_group, key_heads, carried
        )
        return (query_grads,)

    for chunk, (first, count) in enumerate(chunks):
        (early_half, late_half), (before_early, before_late) = halves[chunk], before[chunk]
        if chunk:
            *carried, before_early, before_late = together(*carried, before_early, before_late)
            carried = tuple(carried)
        before_late = jnp.where(last_block, early_half, before_late)

        def past_of(device):
            before = jnp.where(is_early(device), before_early, before_late)
            if parts == 1:
                return before
            half = jnp.where(is_early(device), early_half, late_half)
            return part_rows(jnp.concatenate([before, half], axis=1), device, window)

        pasts.append(
            [past_of(place)] + [turned(past_of(other(turn)), turn) for turn in range(1, sharers)]
        )
        if chunk == 0:
            carried = run((0, 0), groups[0], arranged[0], pasts[0][0], first, count, carried)

    if direct:
        carried = run(
            "direct", jnp.zeros((), jnp.int32), direct_arranged, direct_past, 0, direct, carried
        )
    if len(chunks) > 1:
        pasts[0][1], _ = together(pasts[0][1], pasts[1][0])
    for chunk, (first, count) in enumerate(chunks):
        for turn in range(sharers):
            if (chunk, turn) != (0, 0):
                carried = run(
                    (chunk, turn), groups[turn], arranged[chunk], pasts[chunk][turn],
                    first, count, carried,
                )
    (query_grads,) = carried

    results = ()
    if direct:
        term = terms["direct"]
        from_right, from_left = shifted(term, -1), shifted(term, 1)
        mine = jnp.where(early, from_right, from_left)
        theirs = jnp.where(early, from_left, jnp.where(last_block, term, from_right))
        direct_back = jnp.where(jnp.where(early, same_right, same_left), mine, turned(theirs, 1))

    for chunk, (first, count) in enumerate(chunks):
        came = [terms[chunk, 0]]
        came += [turned(terms[chunk, turn], -turn) for turn in range(1, sharers)]
        to_before, to_own = [], []
        for slot in (early_slot, 1 - early_slot):
            if parts == 1:
                to_before.append(pick(came, lax.rem(slot - place + sharers, sharers)))
                to_own.append(None)
            else:
                total = jnp.zeros((2, 2 * window, came[0].shape[2]), jnp.float32)
                for turn in range(sharers):
                    device = other(turn)
                    mine = jnp.where(device // parts == slot, came[turn].astype(jnp.float32), 0.0)
                    wide = jnp.pad(mine, ((0, 0), (window, window), (0, 0)))
                    total += lax.dynamic_slice_in_dim(
                        wide, window - device % parts * rows, 2 * window, 1
                    )
                to_before.append(total[:, :window].astype(jnp.bfloat16))
                to_own.append(total[:, window:])
        for_early, for_late = shifted(to_before[0], -1), shifted(to_before[1], 1)
        for_early = jnp.where(last_block, to_before[1], for_early)
        sums = [
            half if more is None else (half.astype(jnp.float32) + more).astype(jnp.bfloat16)
            for half, more in zip((for_early, for_late), to_own)
        ]

        def rows_of(device):
            return part_rows(jnp.where(is_early(device), sums[0], sums[1]), device, rows)

        for turn in range(sharers):
            back = rows_of(other(turn))
            if turn:
                back = turned(back, turn)
            results = finish(
                groups[turn].reshape(1), own[chunk, turn], back,
                first, count, heads_per_group, key_heads, tuple(results),
            )
        if chunk == 0 and direct:
            results = finish(
                jnp.zeros((1,), jnp.int32), own["direct"], direct_back,
                0, direct, heads_per_group, key_heads, tuple(results),
            )
    return (query_grads, *results)


def solution(mesh):
    spread = P(("blk", "head"), None)
    return jax.shard_map(
        local,
        mesh=mesh,
        in_specs=(spread,) * 5 + (P(), P()),
        out_specs=(spread,) * 3,
        check_vma=False,
    )
```

```python
import functools

import jax
import jax.numpy as jnp
from jax import lax
from jax.experimental import pallas as pl
from jax.experimental.pallas import tpu as pltpu
from jax.sharding import PartitionSpec as P

HEAD_SIZE = 128
NEGATIVE = -1e30
LOG2_E = 1.4426950408889634
CHUNKS = 2
TILE = 128
STRIP = 64
VMEM_BYTES = 60 * 1024 * 1024


def dot(left, right, left_dim, right_dim):
    return lax.dot_general(
        left, right, (((left_dim,), (right_dim,)), ((), ())), preferred_element_type=jnp.float32
    )


def strips(count):
    return [slice(start, start + STRIP) for start in range(0, count, STRIP)]


def folded(strip, reduce):
    return reduce(strip.reshape(strip.shape[0] // 8, 8, strip.shape[1]), axis=0)


def attention_body(carried, group_ref, low_ref, q_ref, k_ref, v_ref, o_ref, do_ref, past_ref, *refs):
    dq_ref, dk_ref, dv_ref, back_ref = refs[carried : carried + 4]
    k_all, v_all, k_turned, dk_sum, dv_sum, scores, slopes, weights_b, slopes_b = refs[carried + 4 :]
    rows, head = k_ref.shape
    window = past_ref.shape[1]
    members = q_ref.shape[1] // head
    span, lanes = window + TILE, members * TILE
    scale = head**-0.5
    k_all[:window] = past_ref[0]
    k_all[window:] = k_ref[...]
    v_all[:window] = past_ref[1]
    v_all[window:] = v_ref[...]
    k_turned[...] = k_all[...].T
    dk_sum[...] = jnp.zeros_like(dk_sum)
    dv_sum[...] = jnp.zeros_like(dv_sum)
    lane = lax.broadcasted_iota(jnp.int32, (1, lanes), 1) % TILE
    tiles = range(rows // TILE)

    def stacked(ref, start):
        return jnp.concatenate(
            [ref[start : start + TILE, m * head : (m + 1) * head] for m in range(members)], axis=0
        )

    def enter(tile):
        keys = pl.ds(tile * TILE, span)
        queries, grads = stacked(q_ref, tile * TILE), stacked(do_ref, tile * TILE)
        scores[tile] = dot(k_all[keys], queries, 1, 1)
        slopes[tile] = dot(v_all[keys], grads, 1, 1)
        return queries, grads

    def bounds(tile, grads):
        start = tile * TILE
        product = grads.astype(jnp.float32) * stacked(o_ref, start).astype(jnp.float32)
        delta = jnp.sum(product.T, axis=0, keepdims=True)
        return delta, jnp.concatenate([low_ref[:, start : start + TILE]] * members, axis=1) - start

    def visible(strip, low):
        index = strip.start + lax.broadcasted_iota(jnp.int32, (STRIP, lanes), 0)
        seen = index >= low
        return seen & (index <= window + lane) if strip.stop > window else seen

    def find_top(tile, low):
        top = jnp.full((8, lanes), NEGATIVE, jnp.float32)
        for strip in strips(span):
            masked = jnp.where(visible(strip, low), scores[tile, strip], NEGATIVE)
            top = jnp.maximum(top, folded(masked, jnp.max))
        return jnp.max(top, axis=0, keepdims=True)

    def find_terms(tile, low, top):
        total = jnp.zeros((8, lanes), jnp.float32)
        for strip in strips(span):
            terms = jnp.exp2((scores[tile, strip] - top) * (scale * LOG2_E))
            terms = jnp.where(visible(strip, low), terms, 0.0)
            total = total + folded(terms, jnp.sum)
            scores[tile, strip] = terms
        return 1.0 / jnp.sum(total, axis=0, keepdims=True)

    def weigh(tile, inverse, delta):
        for strip in strips(span):
            weights = scores[tile, strip] * inverse
            weights_b[tile, strip] = weights.astype(jnp.bfloat16)
            slopes_b[tile, strip] = (weights * (slopes[tile, strip] - delta)).astype(jnp.bfloat16)

    def leave(tile, queries, grads):
        start = tile * TILE
        keys = pl.ds(start, span)
        dv_sum[keys] += dot(weights_b[tile], grads, 1, 0)
        dk_sum[keys] += dot(slopes_b[tile], queries, 1, 0)
        dq = (dot(k_turned[:, keys], slopes_b[tile], 1, 0) * scale).T
        for m in range(members):
            dq_ref[start : start + TILE, m * head : (m + 1) * head] = dq[
                m * TILE : (m + 1) * TILE
            ].astype(dq_ref.dtype)

    entered = [enter(tile) for tile in tiles]
    limits = [bounds(tile, entered[tile][1]) for tile in tiles]
    tops = [find_top(tile, limits[tile][1]) for tile in tiles]
    inverses = [find_terms(tile, limits[tile][1], tops[tile]) for tile in tiles]
    for tile in tiles:
        weigh(tile, inverses[tile], limits[tile][0])
    for tile in tiles:
        leave(tile, *entered[tile])
    back_ref[0] = dk_sum[:window].astype(back_ref.dtype)
    back_ref[1] = dv_sum[:window].astype(back_ref.dtype)
    dk_ref[...] = dk_sum[window:]
    dv_ref[...] = dv_sum[window:]


def attention(group, low, row_arrays, past, first_head, heads_per_group, carried):
    queries, keys, values, outputs, grads = row_arrays
    rows, window, count = keys.shape[0], past.shape[1], past.shape[2] // HEAD_SIZE
    wide = queries.shape[1] // keys.shape[1] * HEAD_SIZE

    def column(step, group_ref):
        return (0, group_ref[0] * heads_per_group + first_head + step)

    query_spec = pl.BlockSpec((rows, wide), column)
    key_spec = pl.BlockSpec((rows, HEAD_SIZE), column)
    past_spec = pl.BlockSpec((2, window, HEAD_SIZE), lambda step, group_ref: (0, 0, step))
    low_spec = pl.BlockSpec((1, rows), lambda step, group_ref: (0, 0))
    square = (rows // TILE, window + TILE, wide // HEAD_SIZE * TILE)
    tiles = count * queries.shape[1] // keys.shape[1] * rows * (window + TILE)
    return pl.pallas_call(
        functools.partial(attention_body, len(carried)),
        grid_spec=pltpu.PrefetchScalarGridSpec(
            num_scalar_prefetch=1,
            grid=(count,),
            in_specs=[low_spec, query_spec, key_spec, key_spec, query_spec, query_spec, past_spec]
            + [pl.BlockSpec(memory_space=pl.ANY)] * len(carried),
            out_specs=[query_spec, key_spec, key_spec, past_spec],
            scratch_shapes=[
                pltpu.VMEM((window + rows, HEAD_SIZE), jnp.bfloat16),
                pltpu.VMEM((window + rows, HEAD_SIZE), jnp.bfloat16),
                pltpu.VMEM((HEAD_SIZE, window + rows), jnp.bfloat16),
                pltpu.VMEM((window + rows, HEAD_SIZE), jnp.float32),
                pltpu.VMEM((window + rows, HEAD_SIZE), jnp.float32),
                pltpu.VMEM(square, jnp.float32),
                pltpu.VMEM(square, jnp.float32),
                pltpu.VMEM(square, jnp.bfloat16),
                pltpu.VMEM(square, jnp.bfloat16),
            ],
        ),
        out_shape=[
            jax.ShapeDtypeStruct(queries.shape, jnp.bfloat16),
            jax.ShapeDtypeStruct(keys.shape, jnp.float32),
            jax.ShapeDtypeStruct(keys.shape, jnp.float32),
            jax.ShapeDtypeStruct(past.shape, jnp.bfloat16),
        ],
        input_output_aliases={8 + i: i for i in range(len(carried))},
        compiler_params=pltpu.CompilerParams(vmem_limit_bytes=VMEM_BYTES),
        cost_estimate=pl.CostEstimate(
            flops=10 * tiles * HEAD_SIZE, bytes_accessed=count * rows * 2400, transcendentals=tiles
        ),
        name="attention",
    )(group, low, *row_arrays, past, *carried)


def finish_body(carried, group_ref, dk_ref, dv_ref, back_ref, *refs):
    key_out, value_out = refs[carried:]
    scale = HEAD_SIZE**-0.5
    key_out[...] = ((dk_ref[...] + back_ref[0].astype(jnp.float32)) * scale).astype(key_out.dtype)
    value_out[...] = (dv_ref[...] + back_ref[1].astype(jnp.float32)).astype(value_out.dtype)


def finish(group, own, back, first_head, heads_per_group, carried):
    rows, count = back.shape[1], back.shape[2] // HEAD_SIZE

    def column(step, group_ref):
        return (0, group_ref[0] * heads_per_group + first_head + step)

    key_spec = pl.BlockSpec((rows, HEAD_SIZE), column)
    back_spec = pl.BlockSpec((2, rows, HEAD_SIZE), lambda step, group_ref: (0, 0, step))
    return pl.pallas_call(
        functools.partial(finish_body, len(carried)),
        grid_spec=pltpu.PrefetchScalarGridSpec(
            num_scalar_prefetch=1,
            grid=(count,),
            in_specs=[key_spec, key_spec, back_spec]
            + [pl.BlockSpec(memory_space=pl.ANY)] * len(carried),
            out_specs=[key_spec, key_spec],
        ),
        out_shape=[jax.ShapeDtypeStruct(own[0].shape, jnp.bfloat16)] * 2,
        input_output_aliases={4 + i: i for i in range(len(carried))},
        compiler_params=pltpu.CompilerParams(vmem_limit_bytes=VMEM_BYTES),
        cost_estimate=pl.CostEstimate(
            flops=count * rows * 512, bytes_accessed=count * rows * 2048, transcendentals=0
        ),
        name="finish",
    )(group, *own, back, *carried)


def together(*values):
    return lax.optimization_barrier(values)


def pick(items, index):
    result = items[-1]
    for place in range(len(items) - 2, -1, -1):
        result = jnp.where(index == place, items[place], result)
    return result


def local(queries, keys, values, outputs, out_grads, segment_ids, block_order):
    blocks, sharers = lax.axis_size("blk"), lax.axis_size("head")
    block, place = lax.axis_index("blk"), lax.axis_index("head")
    rows = keys.shape[0]
    window = rows * sharers // 2
    parts = sharers // 2
    key_heads = keys.shape[1] // HEAD_SIZE
    heads_per_group = key_heads // sharers
    chunks = min(CHUNKS, heads_per_group)
    per_piece = heads_per_group // chunks
    slots = lax.dynamic_slice_in_dim(block_order, 2 * block, 2)
    early_slot = (slots[0] > slots[1]).astype(jnp.int32)
    last_block = block == blocks - 1

    def other(turn):
        return lax.rem(place + turn + sharers, sharers)

    def turned(value, turn):
        pairs = [(source, (source + turn) % sharers) for source in range(sharers)]
        return lax.ppermute(value, "head", pairs)

    def shifted(value, step):
        first, end = max(0, -step), min(blocks, blocks - step)
        return lax.ppermute(value, "blk", [(source, source + step) for source in range(first, end)])

    def columns(array, group, chunk):
        pieces = []
        for g in range(sharers):
            start = (g * heads_per_group + chunk * per_piece) * HEAD_SIZE
            pieces.append(array[:, start : start + per_piece * HEAD_SIZE])
        return pick(pieces, group)

    def piece_of(group, chunk):
        return jnp.stack([columns(keys, group, chunk), columns(values, group, chunk)])

    def is_early(device):
        return device // parts == early_slot

    def part_rows(array, device, count):
        if parts == 1:
            return array[:, :count]
        return lax.dynamic_slice_in_dim(array, device % parts * rows, count, 1)

    my_half = pick([slots[0], slots[1]], place // parts)
    start = my_half * window + place % parts * rows
    padded = jnp.concatenate([jnp.full((window,), -1, jnp.int32), segment_ids])
    near = lax.dynamic_slice_in_dim(padded, start, window + rows)
    low = jnp.sum((near[None, :] < near[window:, None]).astype(jnp.int32), axis=1)[None, :]

    row_arrays = (queries, keys, values, outputs, out_grads)
    groups = [other(-turn) for turn in range(sharers)]

    def halves_of(pieces):
        return [
            jnp.concatenate(
                [
                    pick(pieces, lax.rem(place - (slot * parts + p) + sharers, sharers))
                    for p in range(parts)
                ],
                axis=1,
            )
            for slot in (early_slot, 1 - early_slot)
        ]

    halves = []
    for chunk in range(chunks):
        pieces = [piece_of(place, chunk)]
        pieces += [turned(piece_of(other(turn), chunk), turn) for turn in range(1, sharers)]
        halves.append(halves_of(pieces))
    before = [(shifted(early, 1), shifted(late, -1)) for early, late in halves]

    def run(turn, chunk, past, carried):
        *carried, back = attention(
            groups[turn].reshape(1), low, row_arrays, past,
            chunk * per_piece, heads_per_group, tuple(carried),
        )
        return carried, back

    carried, terms, pasts = (), [], []
    for chunk in range(chunks):
        (early, late), (before_early, before_late) = halves[chunk], before[chunk]
        if chunk:
            *carried, before_early, before_late = together(*carried, before_early, before_late)
        before_late = jnp.where(last_block, early, before_late)

        def past_of(device):
            before = jnp.where(is_early(device), before_early, before_late)
            if parts == 1:
                return before
            own = jnp.where(is_early(device), early, late)
            return part_rows(jnp.concatenate([before, own], axis=1), device, window)

        pasts.append([turned(past_of(other(turn)), turn) for turn in range(1, sharers)])
        carried, back = run(0, chunk, past_of(place), carried)
        terms.append([back])

    for chunk in range(chunks):
        for turn in range(1, sharers):
            carried, back = run(turn, chunk, pasts[chunk][turn - 1], carried)
            terms[chunk].append(turned(back, -turn))

    query_grads, *own = carried
    results = ()
    for chunk in range(chunks):
        to_before, to_own = [], []
        for slot in (early_slot, 1 - early_slot):
            if parts == 1:
                to_before.append(pick(terms[chunk], lax.rem(slot - place + sharers, sharers)))
                to_own.append(None)
            else:
                total = jnp.zeros((2, 2 * window, terms[chunk][0].shape[2]), jnp.float32)
                for turn in range(sharers):
                    device = other(turn)
                    mine = jnp.where(device // parts == slot, terms[chunk][turn].astype(jnp.float32), 0.0)
                    wide = jnp.pad(mine, ((0, 0), (window, window), (0, 0)))
                    total += lax.dynamic_slice_in_dim(
                        wide, window - device % parts * rows, 2 * window, 1
                    )
                to_before.append(total[:, :window].astype(jnp.bfloat16))
                to_own.append(total[:, window:])
        for_early, for_late = shifted(to_before[0], -1), shifted(to_before[1], 1)
        for_early = jnp.where(last_block, to_before[1], for_early)
        sums = [
            came if more is None else (came.astype(jnp.float32) + more).astype(jnp.bfloat16)
            for came, more in zip((for_early, for_late), to_own)
        ]

        def rows_of(device):
            return part_rows(jnp.where(is_early(device), sums[0], sums[1]), device, rows)

        for turn in range(sharers):
            back = rows_of(other(turn))
            if turn:
                back = turned(back, turn)
            results = finish(
                groups[turn].reshape(1),
                own,
                back,
                chunk * per_piece,
                heads_per_group,
                tuple(results),
            )
    return (query_grads, *results)


def solution(mesh):
    spread = P(("blk", "head"), None)
    return jax.shard_map(
        local,
        mesh=mesh,
        in_specs=(spread,) * 5 + (P(), P()),
        out_specs=(spread,) * 3,
        check_vma=False,
    )
```

```python
import functools

import jax
import jax.numpy as jnp
from jax import lax
from jax.experimental import pallas as pl
from jax.experimental.pallas import tpu as pltpu
from jax.sharding import PartitionSpec as P

HEAD_SIZE = 128
NEGATIVE = -1e30
LOG2_E = 1.4426950408889634
CHUNKS = 2
TILE = 128
STRIP = 64
VMEM_BYTES = 60 * 1024 * 1024


def dot(left, right, left_dim, right_dim):
    return lax.dot_general(
        left, right, (((left_dim,), (right_dim,)), ((), ())), preferred_element_type=jnp.float32
    )


def strips(count):
    return [slice(start, start + STRIP) for start in range(0, count, STRIP)]


def folded(strip, reduce):
    return reduce(strip.reshape(strip.shape[0] // 8, 8, strip.shape[1]), axis=0)


def attention_body(count, per_piece, carried, group_ref, low_ref, q_ref, k_ref, v_ref, o_ref, do_ref, *refs):
    past_refs, refs = refs[:count], refs[count + carried :]
    dq_ref, dk_ref, dv_ref = refs[:3]
    back_refs, refs = refs[3 : 3 + count], refs[3 + count :]
    k_all, v_all, k_turned, dk_sum, dv_sum, scores, slopes, weights_b, slopes_b = refs
    rows, head = k_ref.shape
    window = past_refs[0].shape[1]
    piece = pl.program_id(0) // per_piece
    members = q_ref.shape[1] // head
    span, lanes = window + TILE, members * TILE
    scale = head**-0.5
    for i, past_ref in enumerate(past_refs):

        @pl.when(piece == i)
        def _(past_ref=past_ref):
            k_all[:window] = past_ref[0]
            v_all[:window] = past_ref[1]

    k_all[window:] = k_ref[...]
    v_all[window:] = v_ref[...]
    k_turned[...] = k_all[...].T
    dk_sum[...] = jnp.zeros_like(dk_sum)
    dv_sum[...] = jnp.zeros_like(dv_sum)
    lane = lax.broadcasted_iota(jnp.int32, (1, lanes), 1) % TILE
    tiles = range(rows // TILE)

    def stacked(ref, start):
        return jnp.concatenate(
            [ref[start : start + TILE, m * head : (m + 1) * head] for m in range(members)], axis=0
        )

    def enter(tile):
        keys = pl.ds(tile * TILE, span)
        queries, grads = stacked(q_ref, tile * TILE), stacked(do_ref, tile * TILE)
        scores[tile] = dot(k_all[keys], queries, 1, 1)
        slopes[tile] = dot(v_all[keys], grads, 1, 1)
        return queries, grads

    def weigh(tile, grads):
        start = tile * TILE
        product = grads.astype(jnp.float32) * stacked(o_ref, start).astype(jnp.float32)
        delta = jnp.sum(product.T, axis=0, keepdims=True)
        low = jnp.concatenate([low_ref[:, start : start + TILE]] * members, axis=1) - start

        def visible(strip):
            index = strip.start + lax.broadcasted_iota(jnp.int32, (STRIP, lanes), 0)
            seen = index >= low
            return seen & (index <= window + lane) if strip.stop > window else seen

        top = jnp.full((8, lanes), NEGATIVE, jnp.float32)
        for strip in strips(span):
            masked = jnp.where(visible(strip), scores[tile, strip], NEGATIVE)
            top = jnp.maximum(top, folded(masked, jnp.max))
        top = jnp.max(top, axis=0, keepdims=True)
        total = jnp.zeros((8, lanes), jnp.float32)
        for strip in strips(span):
            terms = jnp.exp2((scores[tile, strip] - top) * (scale * LOG2_E))
            terms = jnp.where(visible(strip), terms, 0.0)
            total = total + folded(terms, jnp.sum)
            scores[tile, strip] = terms
        inverse = 1.0 / jnp.sum(total, axis=0, keepdims=True)
        for strip in strips(span):
            weights = scores[tile, strip] * inverse
            weights_b[tile, strip] = weights.astype(jnp.bfloat16)
            slopes_b[tile, strip] = (weights * (slopes[tile, strip] - delta)).astype(jnp.bfloat16)

    def leave(tile, queries, grads):
        start = tile * TILE
        keys = pl.ds(start, span)
        dv_sum[keys] += dot(weights_b[tile], grads, 1, 0)
        dk_sum[keys] += dot(slopes_b[tile], queries, 1, 0)
        dq = (dot(k_turned[:, keys], slopes_b[tile], 1, 0) * scale).T
        for m in range(members):
            dq_ref[start : start + TILE, m * head : (m + 1) * head] = dq[
                m * TILE : (m + 1) * TILE
            ].astype(dq_ref.dtype)

    entered = {0: enter(0)}
    for tile in tiles:
        if tile + 1 in tiles:
            entered[tile + 1] = enter(tile + 1)
        weigh(tile, entered[tile][1])
        leave(tile, *entered[tile])
    for i, back_ref in enumerate(back_refs):

        @pl.when(piece == i)
        def _(back_ref=back_ref):
            back_ref[0] = dk_sum[:window].astype(back_ref.dtype)
            back_ref[1] = dv_sum[:window].astype(back_ref.dtype)

    dk_ref[...] = dk_sum[window:]
    dv_ref[...] = dv_sum[window:]


def attention(groups, low, row_arrays, pasts, first_head, heads_per_group, carried):
    queries, keys, values, outputs, grads = row_arrays
    rows, window, per_piece = keys.shape[0], pasts[0].shape[1], pasts[0].shape[2] // HEAD_SIZE
    wide = queries.shape[1] // keys.shape[1] * HEAD_SIZE

    def column(step, group_ref):
        group = group_ref[step // per_piece]
        return (0, group * heads_per_group + first_head + step % per_piece)

    def past_spec(piece):
        def place(step, group_ref):
            return (0, 0, jnp.clip(step - piece * per_piece, 0, per_piece - 1))

        return pl.BlockSpec((2, window, HEAD_SIZE), place)

    query_spec = pl.BlockSpec((rows, wide), column)
    key_spec = pl.BlockSpec((rows, HEAD_SIZE), column)
    past_specs = [past_spec(piece) for piece in range(len(pasts))]
    low_spec = pl.BlockSpec((1, rows), lambda step, group_ref: (0, 0))
    square = (rows // TILE, window + TILE, wide // HEAD_SIZE * TILE)
    count = len(pasts) * per_piece
    tiles = count * queries.shape[1] // keys.shape[1] * rows * (window + TILE)
    return pl.pallas_call(
        functools.partial(attention_body, len(pasts), per_piece, len(carried)),
        grid_spec=pltpu.PrefetchScalarGridSpec(
            num_scalar_prefetch=1,
            grid=(count,),
            in_specs=[low_spec, query_spec, key_spec, key_spec, query_spec, query_spec]
            + past_specs
            + [pl.BlockSpec(memory_space=pl.ANY)] * len(carried),
            out_specs=[query_spec, key_spec, key_spec] + past_specs,
            scratch_shapes=[
                pltpu.VMEM((window + rows, HEAD_SIZE), jnp.bfloat16),
                pltpu.VMEM((window + rows, HEAD_SIZE), jnp.bfloat16),
                pltpu.VMEM((HEAD_SIZE, window + rows), jnp.bfloat16),
                pltpu.VMEM((window + rows, HEAD_SIZE), jnp.float32),
                pltpu.VMEM((window + rows, HEAD_SIZE), jnp.float32),
                pltpu.VMEM(square, jnp.float32),
                pltpu.VMEM(square, jnp.float32),
                pltpu.VMEM(square, jnp.bfloat16),
                pltpu.VMEM(square, jnp.bfloat16),
            ],
        ),
        out_shape=[
            jax.ShapeDtypeStruct(queries.shape, jnp.bfloat16),
            jax.ShapeDtypeStruct(keys.shape, jnp.float32),
            jax.ShapeDtypeStruct(keys.shape, jnp.float32),
        ]
        + [jax.ShapeDtypeStruct(past.shape, jnp.bfloat16) for past in pasts],
        input_output_aliases={7 + len(pasts) + i: i for i in range(len(carried))},
        compiler_params=pltpu.CompilerParams(vmem_limit_bytes=VMEM_BYTES),
        cost_estimate=pl.CostEstimate(
            flops=10 * tiles * HEAD_SIZE, bytes_accessed=count * rows * 2400, transcendentals=tiles
        ),
        name="attention",
    )(groups, low, *row_arrays, *pasts, *carried)


def finish_body(carried, group_ref, dk_ref, dv_ref, back_ref, *refs):
    key_out, value_out = refs[carried:]
    scale = HEAD_SIZE**-0.5
    key_out[...] = ((dk_ref[...] + back_ref[0].astype(jnp.float32)) * scale).astype(key_out.dtype)
    value_out[...] = (dv_ref[...] + back_ref[1].astype(jnp.float32)).astype(value_out.dtype)


def finish(group, own, back, first_head, heads_per_group, carried):
    rows, wide = back.shape[1:]
    per_piece = wide // HEAD_SIZE

    def column(step, group_ref):
        return (0, (group_ref[0] * heads_per_group + first_head) // per_piece)

    key_spec = pl.BlockSpec((rows, wide), column)
    back_spec = pl.BlockSpec((2, rows, wide), lambda step, group_ref: (0, 0, 0))
    return pl.pallas_call(
        functools.partial(finish_body, len(carried)),
        grid_spec=pltpu.PrefetchScalarGridSpec(
            num_scalar_prefetch=1,
            grid=(1,),
            in_specs=[key_spec, key_spec, back_spec]
            + [pl.BlockSpec(memory_space=pl.ANY)] * len(carried),
            out_specs=[key_spec, key_spec],
        ),
        out_shape=[jax.ShapeDtypeStruct(own[0].shape, jnp.bfloat16)] * 2,
        input_output_aliases={4 + i: i for i in range(len(carried))},
        compiler_params=pltpu.CompilerParams(vmem_limit_bytes=VMEM_BYTES),
        cost_estimate=pl.CostEstimate(
            flops=2 * rows * wide, bytes_accessed=rows * wide * 16, transcendentals=0
        ),
        name="finish",
    )(group, *own, back, *carried)


def together(*values):
    return lax.optimization_barrier(values)


def pick(items, index):
    result = items[-1]
    for place in range(len(items) - 2, -1, -1):
        result = jnp.where(index == place, items[place], result)
    return result


def local(queries, keys, values, outputs, out_grads, segment_ids, block_order):
    blocks, sharers = lax.axis_size("blk"), lax.axis_size("head")
    block, place = lax.axis_index("blk"), lax.axis_index("head")
    rows = keys.shape[0]
    window = rows * sharers // 2
    parts = sharers // 2
    key_heads = keys.shape[1] // HEAD_SIZE
    heads_per_group = key_heads // sharers
    chunks = min(CHUNKS, heads_per_group)
    per_piece = heads_per_group // chunks
    slots = lax.dynamic_slice_in_dim(block_order, 2 * block, 2)
    early_slot = (slots[0] > slots[1]).astype(jnp.int32)
    last_block = block == blocks - 1

    def other(turn):
        return lax.rem(place + turn + sharers, sharers)

    def turned(value, turn):
        pairs = [(source, (source + turn) % sharers) for source in range(sharers)]
        return lax.ppermute(value, "head", pairs)

    def shifted(value, step):
        first, end = max(0, -step), min(blocks, blocks - step)
        return lax.ppermute(value, "blk", [(source, source + step) for source in range(first, end)])

    def columns(array, group, chunk):
        pieces = []
        for g in range(sharers):
            start = (g * heads_per_group + chunk * per_piece) * HEAD_SIZE
            pieces.append(array[:, start : start + per_piece * HEAD_SIZE])
        return pick(pieces, group)

    def piece_of(group, chunk):
        return jnp.stack([columns(keys, group, chunk), columns(values, group, chunk)])

    def is_early(device):
        return device // parts == early_slot

    def part_rows(array, device, count):
        if parts == 1:
            return array[:, :count]
        return lax.dynamic_slice_in_dim(array, device % parts * rows, count, 1)

    my_half = pick([slots[0], slots[1]], place // parts)
    start = my_half * window + place % parts * rows
    padded = jnp.concatenate([jnp.full((window,), -1, jnp.int32), segment_ids])
    near = lax.dynamic_slice_in_dim(padded, start, window + rows)
    low = jnp.sum((near[None, :] < near[window:, None]).astype(jnp.int32), axis=1)[None, :]

    row_arrays = (queries, keys, values, outputs, out_grads)
    groups = [other(-turn) for turn in range(sharers)]

    def halves_of(pieces):
        return [
            jnp.concatenate(
                [
                    pick(pieces, lax.rem(place - (slot * parts + p) + sharers, sharers))
                    for p in range(parts)
                ],
                axis=1,
            )
            for slot in (early_slot, 1 - early_slot)
        ]

    halves = []
    for chunk in range(chunks):
        pieces = [piece_of(place, chunk)]
        pieces += [turned(piece_of(other(turn), chunk), turn) for turn in range(1, sharers)]
        halves.append(halves_of(pieces))
    before = [(shifted(early, 1), shifted(late, -1)) for early, late in halves]

    def run(chunk, turns, carried):
        query_grads, key_sums, value_sums, *backs = attention(
            jnp.stack([groups[turn] for turn in turns]), low, row_arrays,
            [pasts[chunk][turn] for turn in turns],
            chunk * per_piece, heads_per_group, carried,
        )
        return (query_grads, key_sums, value_sums), backs

    carried, terms, pasts = (), [], []
    for chunk in range(chunks):
        (early, late), (before_early, before_late) = halves[chunk], before[chunk]
        if chunk:
            *carried, before_early, before_late = together(*carried, before_early, before_late)
            carried = tuple(carried)
        before_late = jnp.where(last_block, early, before_late)

        def past_of(device):
            before = jnp.where(is_early(device), before_early, before_late)
            if parts == 1:
                return before
            own = jnp.where(is_early(device), early, late)
            return part_rows(jnp.concatenate([before, own], axis=1), device, window)

        pasts.append(
            [past_of(place)] + [turned(past_of(other(turn)), turn) for turn in range(1, sharers)]
        )
        if chunk == 0:
            carried, backs = run(0, [0], carried)
            terms.append(backs)

    if chunks > 1:
        pasts[0][1], _ = together(pasts[0][1], pasts[1][0])
    carried, backs = run(0, range(1, sharers), carried)
    terms[0] += [turned(back, -turn) for turn, back in enumerate(backs, 1)]
    for chunk in range(1, chunks):
        carried, (back, *backs) = run(chunk, range(sharers), carried)
        terms.append([back] + [turned(back, -turn) for turn, back in enumerate(backs, 1)])

    query_grads, *own = carried
    results = ()
    for chunk in range(chunks):
        to_before, to_own = [], []
        for slot in (early_slot, 1 - early_slot):
            if parts == 1:
                to_before.append(pick(terms[chunk], lax.rem(slot - place + sharers, sharers)))
                to_own.append(None)
            else:
                total = jnp.zeros((2, 2 * window, terms[chunk][0].shape[2]), jnp.float32)
                for turn in range(sharers):
                    device = other(turn)
                    mine = jnp.where(device // parts == slot, terms[chunk][turn].astype(jnp.float32), 0.0)
                    wide = jnp.pad(mine, ((0, 0), (window, window), (0, 0)))
                    total += lax.dynamic_slice_in_dim(
                        wide, window - device % parts * rows, 2 * window, 1
                    )
                to_before.append(total[:, :window].astype(jnp.bfloat16))
                to_own.append(total[:, window:])
        for_early, for_late = shifted(to_before[0], -1), shifted(to_before[1], 1)
        for_early = jnp.where(last_block, to_before[1], for_early)
        sums = [
            came if more is None else (came.astype(jnp.float32) + more).astype(jnp.bfloat16)
            for came, more in zip((for_early, for_late), to_own)
        ]

        def rows_of(device):
            return part_rows(jnp.where(is_early(device), sums[0], sums[1]), device, rows)

        for turn in range(sharers):
            back = rows_of(other(turn))
            if turn:
                back = turned(back, turn)
            results = finish(
                groups[turn].reshape(1),
                own,
                back,
                chunk * per_piece,
                heads_per_group,
                tuple(results),
            )
    return (query_grads, *results)


def solution(mesh):
    spread = P(("blk", "head"), None)
    return jax.shard_map(
        local,
        mesh=mesh,
        in_specs=(spread,) * 5 + (P(), P()),
        out_specs=(spread,) * 3,
        check_vma=False,
    )
```

```python
import functools

import jax
import jax.numpy as jnp
from jax import lax
from jax.experimental import pallas as pl
from jax.experimental.pallas import tpu as pltpu
from jax.sharding import PartitionSpec as P

HEAD_SIZE = 128
NEGATIVE = -1e30
LOG2_E = 1.4426950408889634
CHUNKS = 2
DIRECT_CHUNKS = 4
TILE = 128
STRIP = 64
VMEM_BYTES = 60 * 1024 * 1024


def dot(left, right, left_dim, right_dim):
    return lax.dot_general(
        left, right, (((left_dim,), (right_dim,)), ((), ())), preferred_element_type=jnp.float32
    )


def strips(count):
    return [slice(start, start + STRIP) for start in range(0, count, STRIP)]


def folded(strip, reduce):
    return reduce(strip.reshape(strip.shape[0] // 8, 8, strip.shape[1]), axis=0)


def attention_body(
    choices, carried, group_ref, which_ref, low_ref, q_ref, k_ref, v_ref, o_ref, do_ref, *refs
):
    past_refs, refs = refs[:choices], refs[choices:]
    dq_ref, dk_ref, dv_ref, back_ref = refs[carried : carried + 4]
    k_all, v_all, k_turned, dk_sum, dv_sum, scores, slopes, weights_b, slopes_b = refs[carried + 4 :]
    rows, head = k_ref.shape
    window = past_refs[0].shape[1]
    members = q_ref.shape[1] // head
    span, lanes = window + TILE, members * TILE
    scale = head**-0.5
    for choice, past_ref in enumerate(past_refs):

        @pl.when(which_ref[0] == choice)
        def _(past_ref=past_ref):
            k_all[:window] = past_ref[0]
            v_all[:window] = past_ref[1]

    k_all[window:] = k_ref[...]
    v_all[window:] = v_ref[...]
    k_turned[...] = k_all[...].T
    dk_sum[...] = jnp.zeros_like(dk_sum)
    dv_sum[...] = jnp.zeros_like(dv_sum)
    lane = lax.broadcasted_iota(jnp.int32, (1, lanes), 1) % TILE
    tiles = range(rows // TILE)

    def stacked(ref, start):
        return jnp.concatenate(
            [ref[start : start + TILE, m * head : (m + 1) * head] for m in range(members)], axis=0
        )

    def enter(tile):
        keys = pl.ds(tile * TILE, span)
        queries, grads = stacked(q_ref, tile * TILE), stacked(do_ref, tile * TILE)
        scores[tile] = dot(k_all[keys], queries, 1, 1)
        slopes[tile] = dot(v_all[keys], grads, 1, 1)
        return queries, grads

    def weigh(tile, grads):
        start = tile * TILE
        product = grads.astype(jnp.float32) * stacked(o_ref, start).astype(jnp.float32)
        delta = jnp.sum(product.T, axis=0, keepdims=True)
        low = jnp.concatenate([low_ref[:, start : start + TILE]] * members, axis=1) - start

        def visible(strip):
            index = strip.start + lax.broadcasted_iota(jnp.int32, (STRIP, lanes), 0)
            seen = index >= low
            return seen & (index <= window + lane) if strip.stop > window else seen

        top = jnp.full((8, lanes), NEGATIVE, jnp.float32)
        for strip in strips(span):
            masked = jnp.where(visible(strip), scores[tile, strip], NEGATIVE)
            top = jnp.maximum(top, folded(masked, jnp.max))
        top = jnp.max(top, axis=0, keepdims=True)
        total = jnp.zeros((8, lanes), jnp.float32)
        for strip in strips(span):
            terms = jnp.exp2((scores[tile, strip] - top) * (scale * LOG2_E))
            terms = jnp.where(visible(strip), terms, 0.0)
            total = total + folded(terms, jnp.sum)
            scores[tile, strip] = terms
        inverse = 1.0 / jnp.sum(total, axis=0, keepdims=True)
        for strip in strips(span):
            weights = scores[tile, strip] * inverse
            weights_b[tile, strip] = weights.astype(jnp.bfloat16)
            slopes_b[tile, strip] = (weights * (slopes[tile, strip] - delta)).astype(jnp.bfloat16)

    def leave(tile, queries, grads):
        start = tile * TILE
        keys = pl.ds(start, span)
        dv_sum[keys] += dot(weights_b[tile], grads, 1, 0)
        dk_sum[keys] += dot(slopes_b[tile], queries, 1, 0)
        dq = (dot(k_turned[:, keys], slopes_b[tile], 1, 0) * scale).T
        for m in range(members):
            dq_ref[start : start + TILE, m * head : (m + 1) * head] = dq[
                m * TILE : (m + 1) * TILE
            ].astype(dq_ref.dtype)

    entered = {0: enter(0)}
    for tile in tiles:
        if tile + 1 in tiles:
            entered[tile + 1] = enter(tile + 1)
        weigh(tile, entered[tile][1])
        leave(tile, *entered[tile])
    back_ref[0] = dk_sum[:window].astype(back_ref.dtype)
    back_ref[1] = dv_sum[:window].astype(back_ref.dtype)
    dk_ref[...] = dk_sum[window:]
    dv_ref[...] = dv_sum[window:]


def choice_specs(arrays):
    def place(choice, step, group_ref, which_ref):
        return (0, 0, jnp.where(which_ref[0] == choice, step, 0))

    return [
        pl.BlockSpec((2, array.shape[1], HEAD_SIZE), functools.partial(place, choice))
        for choice, array in enumerate(arrays)
    ]


def attention(group, which, low, row_arrays, pasts, first_head, heads_per_group, carried):
    queries, keys, values, outputs, grads = row_arrays
    rows, window, count = keys.shape[0], pasts[0].shape[1], pasts[0].shape[2] // HEAD_SIZE
    wide = queries.shape[1] // keys.shape[1] * HEAD_SIZE

    def column(step, group_ref, which_ref):
        return (0, group_ref[0] * heads_per_group + first_head + step)

    query_spec = pl.BlockSpec((rows, wide), column)
    key_spec = pl.BlockSpec((rows, HEAD_SIZE), column)
    back_spec = pl.BlockSpec((2, window, HEAD_SIZE), lambda step, *refs: (0, 0, step))
    low_spec = pl.BlockSpec((1, rows), lambda step, *refs: (0, 0))
    square = (rows // TILE, window + TILE, wide // HEAD_SIZE * TILE)
    tiles = count * queries.shape[1] // keys.shape[1] * rows * (window + TILE)
    return pl.pallas_call(
        functools.partial(attention_body, len(pasts), len(carried)),
        grid_spec=pltpu.PrefetchScalarGridSpec(
            num_scalar_prefetch=2,
            grid=(count,),
            in_specs=[low_spec, query_spec, key_spec, key_spec, query_spec, query_spec]
            + choice_specs(pasts)
            + [pl.BlockSpec(memory_space=pl.ANY)] * len(carried),
            out_specs=[query_spec, key_spec, key_spec, back_spec],
            scratch_shapes=[
                pltpu.VMEM((window + rows, HEAD_SIZE), jnp.bfloat16),
                pltpu.VMEM((window + rows, HEAD_SIZE), jnp.bfloat16),
                pltpu.VMEM((HEAD_SIZE, window + rows), jnp.bfloat16),
                pltpu.VMEM((window + rows, HEAD_SIZE), jnp.float32),
                pltpu.VMEM((window + rows, HEAD_SIZE), jnp.float32),
                pltpu.VMEM(square, jnp.float32),
                pltpu.VMEM(square, jnp.float32),
                pltpu.VMEM(square, jnp.bfloat16),
                pltpu.VMEM(square, jnp.bfloat16),
            ],
        ),
        out_shape=[
            jax.ShapeDtypeStruct(queries.shape, jnp.bfloat16),
            jax.ShapeDtypeStruct(keys.shape, jnp.float32),
            jax.ShapeDtypeStruct(keys.shape, jnp.float32),
            jax.ShapeDtypeStruct(pasts[0].shape, jnp.bfloat16),
        ],
        input_output_aliases={8 + len(pasts) + i: i for i in range(len(carried))},
        compiler_params=pltpu.CompilerParams(vmem_limit_bytes=VMEM_BYTES),
        cost_estimate=pl.CostEstimate(
            flops=10 * tiles * HEAD_SIZE, bytes_accessed=count * rows * 2400, transcendentals=tiles
        ),
        name="attention",
    )(group, which, low, *row_arrays, *pasts, *carried)


def finish_body(choices, carried, group_ref, which_ref, dk_ref, dv_ref, *refs):
    key_out, value_out = refs[choices + carried :]
    scale = HEAD_SIZE**-0.5
    for choice, back_ref in enumerate(refs[:choices]):

        @pl.when(which_ref[0] == choice)
        def _(back_ref=back_ref):
            key_sum = dk_ref[...] + back_ref[0].astype(jnp.float32)
            key_out[...] = (key_sum * scale).astype(key_out.dtype)
            value_out[...] = (dv_ref[...] + back_ref[1].astype(jnp.float32)).astype(value_out.dtype)


def finish(group, which, own, backs, first_head, heads_per_group, carried):
    rows, count = backs[0].shape[1], backs[0].shape[2] // HEAD_SIZE

    def column(step, group_ref, which_ref):
        return (0, group_ref[0] * heads_per_group + first_head + step)

    key_spec = pl.BlockSpec((rows, HEAD_SIZE), column)
    return pl.pallas_call(
        functools.partial(finish_body, len(backs), len(carried)),
        grid_spec=pltpu.PrefetchScalarGridSpec(
            num_scalar_prefetch=2,
            grid=(count,),
            in_specs=[key_spec, key_spec]
            + choice_specs(backs)
            + [pl.BlockSpec(memory_space=pl.ANY)] * len(carried),
            out_specs=[key_spec, key_spec],
        ),
        out_shape=[jax.ShapeDtypeStruct(own[0].shape, jnp.bfloat16)] * 2,
        input_output_aliases={4 + len(backs) + i: i for i in range(len(carried))},
        compiler_params=pltpu.CompilerParams(vmem_limit_bytes=VMEM_BYTES),
        cost_estimate=pl.CostEstimate(
            flops=count * rows * 512, bytes_accessed=count * rows * 2048, transcendentals=0
        ),
        name="finish",
    )(group, which, *own, *backs, *carried)


def together(*values):
    return lax.optimization_barrier(values)


def pick(items, index):
    result = items[-1]
    for place in range(len(items) - 2, -1, -1):
        result = jnp.where(index == place, items[place], result)
    return result


def first_visible(segment_ids, start, window, rows):
    padded = jnp.concatenate([jnp.full((window,), -1, jnp.int32), segment_ids])
    near = lax.dynamic_slice_in_dim(padded, start, window + rows)
    return jnp.sum((near[None, :] < near[window:, None]).astype(jnp.int32), axis=1)[None, :]


def local_direct(queries, keys, values, outputs, out_grads, segment_ids, block_order):
    blocks = lax.axis_size("blk")
    block, place = lax.axis_index("blk"), lax.axis_index("head")
    rows, key_heads = keys.shape[0], keys.shape[1] // HEAD_SIZE
    per_chunk = key_heads // DIRECT_CHUNKS
    last_block = block == blocks - 1

    def slots_of(block):
        return lax.dynamic_slice_in_dim(block_order, 2 * jnp.clip(block, 0, blocks - 1), 2)

    def early_slot_of(block):
        slots = slots_of(block)
        return (slots[0] > slots[1]).astype(jnp.int32)

    def swapped(value):
        return lax.ppermute(value, "head", [(0, 1), (1, 0)])

    def shifted(value, step):
        first, end = max(0, -step), min(blocks, blocks - step)
        return lax.ppermute(value, "blk", [(source, source + step) for source in range(first, end)])

    early_slot = early_slot_of(block)
    early = place == early_slot
    same_left = early_slot_of(block - 1) == early_slot
    same_right = (early_slot_of(block + 1) == early_slot) & ~last_block
    which_past = jnp.where(early, jnp.where(same_left, 0, 2), jnp.where(same_right, 1, 2)).reshape(1)
    which_back = jnp.where(early, jnp.where(same_right, 1, 2), jnp.where(same_left, 0, 2)).reshape(1)
    slots = slots_of(block)
    low = first_visible(segment_ids, pick([slots[0], slots[1]], place) * rows, rows, rows)
    zero = jnp.zeros((1,), jnp.int32)
    row_arrays = (queries, keys, values, outputs, out_grads)

    shifts, theirs, pasts = [], [], []

    def shift(chunk):
        columns = slice(chunk * per_chunk * HEAD_SIZE, (chunk + 1) * per_chunk * HEAD_SIZE)
        piece = jnp.stack([keys[:, columns], values[:, columns]])
        if chunk >= 2:
            piece, *_ = together(piece, theirs[chunk - 2], *(past[2] for past in pasts[: chunk - 2]))
        shifts.append((piece, shifted(piece, 1), shifted(piece, -1)))

    def swap(chunk):
        piece, from_left, from_right = shifts[chunk]
        if chunk:
            from_left, from_right, _ = together(from_left, from_right, theirs[chunk - 1])
        theirs.append(jnp.where(early, jnp.where(last_block, piece, from_right), from_left))
        return from_left, from_right, swapped(theirs[chunk])

    shift(0)
    for chunk in range(DIRECT_CHUNKS):
        if chunk + 1 < DIRECT_CHUNKS:
            shift(chunk + 1)
        pasts.append(swap(chunk))

    carried, terms, backs = (), [], []

    def swap_back(chunk):
        term, from_left, from_right = terms[chunk]
        if backs:
            from_left, from_right, _ = together(from_left, from_right, backs[-1][0])
        theirs = jnp.where(early, from_left, jnp.where(last_block, term, from_right))
        backs.append((theirs, (from_left, from_right, swapped(theirs))))

    for chunk in range(DIRECT_CHUNKS):
        if chunk == DIRECT_CHUNKS - 1:
            swap_back(0)
            *carried, _ = together(*carried, backs[0][0])
        *carried, term = attention(
            zero, which_past, low, row_arrays, pasts[chunk], chunk * per_chunk, 0, tuple(carried)
        )
        terms.append((term, shifted(term, 1), shifted(term, -1)))
    query_grads, *own = carried

    results = ()
    for chunk in range(DIRECT_CHUNKS):
        if chunk:
            swap_back(chunk)
        results = finish(
            zero, which_back, own, backs[chunk][1], chunk * per_chunk, 0, tuple(results)
        )
    return (query_grads, *results)


def local_exchanged(queries, keys, values, outputs, out_grads, segment_ids, block_order):
    blocks, sharers = lax.axis_size("blk"), lax.axis_size("head")
    block, place = lax.axis_index("blk"), lax.axis_index("head")
    rows = keys.shape[0]
    window = rows * sharers // 2
    parts = sharers // 2
    key_heads = keys.shape[1] // HEAD_SIZE
    heads_per_group = key_heads // sharers
    chunks = min(CHUNKS, heads_per_group)
    per_piece = heads_per_group // chunks
    slots = lax.dynamic_slice_in_dim(block_order, 2 * block, 2)
    early_slot = (slots[0] > slots[1]).astype(jnp.int32)
    last_block = block == blocks - 1

    def other(turn):
        return lax.rem(place + turn + sharers, sharers)

    def turned(value, turn):
        pairs = [(source, (source + turn) % sharers) for source in range(sharers)]
        return lax.ppermute(value, "head", pairs)

    def shifted(value, step):
        first, end = max(0, -step), min(blocks, blocks - step)
        return lax.ppermute(value, "blk", [(source, source + step) for source in range(first, end)])

    def columns(array, group, chunk):
        pieces = []
        for g in range(sharers):
            start = (g * heads_per_group + chunk * per_piece) * HEAD_SIZE
            pieces.append(array[:, start : start + per_piece * HEAD_SIZE])
        return pick(pieces, group)

    def piece_of(group, chunk):
        return jnp.stack([columns(keys, group, chunk), columns(values, group, chunk)])

    def is_early(device):
        return device // parts == early_slot

    def part_rows(array, device, count):
        if parts == 1:
            return array[:, :count]
        return lax.dynamic_slice_in_dim(array, device % parts * rows, count, 1)

    my_half = pick([slots[0], slots[1]], place // parts)
    zero = jnp.zeros((1,), jnp.int32)
    low = first_visible(segment_ids, my_half * window + place % parts * rows, window, rows)

    row_arrays = (queries, keys, values, outputs, out_grads)
    groups = [other(-turn) for turn in range(sharers)]

    def halves_of(pieces):
        return [
            jnp.concatenate(
                [
                    pick(pieces, lax.rem(place - (slot * parts + p) + sharers, sharers))
                    for p in range(parts)
                ],
                axis=1,
            )
            for slot in (early_slot, 1 - early_slot)
        ]

    halves = []
    for chunk in range(chunks):
        pieces = [piece_of(place, chunk)]
        pieces += [turned(piece_of(other(turn), chunk), turn) for turn in range(1, sharers)]
        halves.append(halves_of(pieces))
    before = [(shifted(early, 1), shifted(late, -1)) for early, late in halves]

    def run(turn, chunk, past, carried):
        *carried, back = attention(
            groups[turn].reshape(1), zero, low, row_arrays, [past],
            chunk * per_piece, heads_per_group, tuple(carried),
        )
        return carried, back

    carried, terms, pasts = (), [], []
    for chunk in range(chunks):
        (early, late), (before_early, before_late) = halves[chunk], before[chunk]
        if chunk:
            *carried, before_early, before_late = together(*carried, before_early, before_late)
        before_late = jnp.where(last_block, early, before_late)

        def past_of(device):
            before = jnp.where(is_early(device), before_early, before_late)
            if parts == 1:
                return before
            own = jnp.where(is_early(device), early, late)
            return part_rows(jnp.concatenate([before, own], axis=1), device, window)

        pasts.append([turned(past_of(other(turn)), turn) for turn in range(1, sharers)])
        carried, back = run(0, chunk, past_of(place), carried)
        terms.append([back])

    for chunk in range(chunks):
        for turn in range(1, sharers):
            carried, back = run(turn, chunk, pasts[chunk][turn - 1], carried)
            terms[chunk].append(turned(back, -turn))

    query_grads, *own = carried
    results = ()
    for chunk in range(chunks):
        to_before, to_own = [], []
        for slot in (early_slot, 1 - early_slot):
            if parts == 1:
                to_before.append(pick(terms[chunk], lax.rem(slot - place + sharers, sharers)))
                to_own.append(None)
            else:
                total = jnp.zeros((2, 2 * window, terms[chunk][0].shape[2]), jnp.float32)
                for turn in range(sharers):
                    device = other(turn)
                    mine = jnp.where(device // parts == slot, terms[chunk][turn].astype(jnp.float32), 0.0)
                    wide = jnp.pad(mine, ((0, 0), (window, window), (0, 0)))
                    total += lax.dynamic_slice_in_dim(
                        wide, window - device % parts * rows, 2 * window, 1
                    )
                to_before.append(total[:, :window].astype(jnp.bfloat16))
                to_own.append(total[:, window:])
        for_early, for_late = shifted(to_before[0], -1), shifted(to_before[1], 1)
        for_early = jnp.where(last_block, to_before[1], for_early)
        sums = [
            came if more is None else (came.astype(jnp.float32) + more).astype(jnp.bfloat16)
            for came, more in zip((for_early, for_late), to_own)
        ]

        def rows_of(device):
            return part_rows(jnp.where(is_early(device), sums[0], sums[1]), device, rows)

        for turn in range(sharers):
            back = rows_of(other(turn))
            if turn:
                back = turned(back, turn)
            results = finish(
                groups[turn].reshape(1), zero, own, [back],
                chunk * per_piece, heads_per_group, tuple(results),
            )
    return (query_grads, *results)


def solution(mesh):
    spread = P(("blk", "head"), None)
    return jax.shard_map(
        local_direct if mesh.shape["head"] == 2 else local_exchanged,
        mesh=mesh,
        in_specs=(spread,) * 5 + (P(), P()),
        out_specs=(spread,) * 3,
        check_vma=False,
    )
```

```python
import functools

import jax
import jax.numpy as jnp
from jax import lax
from jax.experimental import pallas as pl
from jax.experimental.pallas import tpu as pltpu
from jax.sharding import PartitionSpec as P

HEAD_SIZE = 128
NEGATIVE = -1e30
LOG2_E = 1.4426950408889634
CHUNKS = 2
TILE = 128
STRIP = 64
VMEM_BYTES = 24 * 1024 * 1024


def dot(left, right, left_dim, right_dim):
    return lax.dot_general(
        left, right, (((left_dim,), (right_dim,)), ((), ())), preferred_element_type=jnp.float32
    )


def strips(count):
    return [slice(start, start + STRIP) for start in range(0, count, STRIP)]


def folded(strip, reduce):
    return reduce(strip.reshape(strip.shape[0] // 8, 8, strip.shape[1]), axis=0)


def arrange_body(q_ref, k_ref, v_ref, o_ref, do_ref, q_out, do_out, delta_out, k_out, k_turned_out, v_out):
    rows, head = k_ref.shape
    members = q_ref.shape[1] // head
    for tile in range(rows // TILE):
        own = slice(tile * TILE, (tile + 1) * TILE)
        for m in range(members):
            place = slice((tile * members + m) * TILE, (tile * members + m + 1) * TILE)
            columns = slice(m * head, (m + 1) * head)
            q_out[0, place] = q_ref[own, columns]
            do_out[0, place] = do_ref[own, columns]
            product = do_ref[own, columns].astype(jnp.float32) * o_ref[own, columns].astype(jnp.float32)
            delta_out[0, :, place] = jnp.sum(product.T, axis=0, keepdims=True)
    k_out[0] = k_ref[...]
    k_turned_out[0] = k_ref[...].T
    v_out[0] = v_ref[...]


def arrange(row_arrays, first_head, heads_per_group, per_piece):
    queries, keys, values, outputs, grads = row_arrays
    rows, members = keys.shape[0], queries.shape[1] // keys.shape[1]
    groups = keys.shape[1] // HEAD_SIZE // heads_per_group
    count = groups * per_piece

    def column(group, step):
        return (0, group * heads_per_group + first_head + step)

    def leading(group, step):
        return (group * per_piece + step, 0, 0)

    query_spec = pl.BlockSpec((rows, members * HEAD_SIZE), column)
    key_spec = pl.BlockSpec((rows, HEAD_SIZE), column)
    shapes = [
        ((members * rows, HEAD_SIZE), jnp.bfloat16),
        ((members * rows, HEAD_SIZE), jnp.bfloat16),
        ((1, members * rows), jnp.float32),
        ((rows, HEAD_SIZE), jnp.bfloat16),
        ((HEAD_SIZE, rows), jnp.bfloat16),
        ((rows, HEAD_SIZE), jnp.bfloat16),
    ]
    return pl.pallas_call(
        arrange_body,
        grid=(groups, per_piece),
        in_specs=[query_spec, key_spec, key_spec, query_spec, query_spec],
        out_specs=[pl.BlockSpec((1, *shape), leading) for shape, _ in shapes],
        out_shape=[jax.ShapeDtypeStruct((count, *shape), dtype) for shape, dtype in shapes],
        compiler_params=pltpu.CompilerParams(vmem_limit_bytes=VMEM_BYTES),
        cost_estimate=pl.CostEstimate(
            flops=count * rows * 1024, bytes_accessed=count * rows * 4096, transcendentals=0
        ),
        name="arrange",
    )(queries, keys, values, outputs, grads)


def attention_body(
    carried, group_ref, low_ref, q_ref, do_ref, delta_ref, k_ref, k_turned_ref, v_ref, past_ref, *refs
):
    dq_ref, dk_ref, dv_ref, back_ref = refs[carried : carried + 4]
    k_all, v_all, k_turned, dk_sum, dv_sum, scores, slopes, weights_b, slopes_b = refs[carried + 4 :]
    rows, head = k_ref.shape[1:]
    window = past_ref.shape[1]
    members = q_ref.shape[1] // rows
    span, lanes = window + TILE, members * TILE
    scale = head**-0.5
    k_all[:window] = past_ref[0]
    k_all[window:] = k_ref[0]
    v_all[:window] = past_ref[1]
    v_all[window:] = v_ref[0]
    k_turned[:, :window] = past_ref[0].T
    k_turned[:, window:] = k_turned_ref[0]
    dk_sum[...] = jnp.zeros_like(dk_sum)
    dv_sum[...] = jnp.zeros_like(dv_sum)
    lane = lax.broadcasted_iota(jnp.int32, (1, lanes), 1) % TILE
    tiles = range(rows // TILE)

    def enter(tile):
        keys = pl.ds(tile * TILE, span)
        place = pl.ds(tile * lanes, lanes)
        queries, grads = q_ref[0, place], do_ref[0, place]
        scores[tile] = dot(k_all[keys], queries, 1, 1)
        slopes[tile] = dot(v_all[keys], grads, 1, 1)
        return queries, grads

    def weigh(tile):
        start = tile * TILE
        delta = delta_ref[0, :, pl.ds(tile * lanes, lanes)]
        low = jnp.concatenate([low_ref[:, start : start + TILE]] * members, axis=1) - start

        def visible(strip):
            index = strip.start + lax.broadcasted_iota(jnp.int32, (STRIP, lanes), 0)
            seen = index >= low
            return seen & (index <= window + lane) if strip.stop > window else seen

        top = jnp.full((8, lanes), NEGATIVE, jnp.float32)
        for strip in strips(span):
            masked = jnp.where(visible(strip), scores[tile, strip], NEGATIVE)
            top = jnp.maximum(top, folded(masked, jnp.max))
        top = jnp.max(top, axis=0, keepdims=True)
        total = jnp.zeros((8, lanes), jnp.float32)
        for strip in strips(span):
            terms = jnp.exp2((scores[tile, strip] - top) * (scale * LOG2_E))
            terms = jnp.where(visible(strip), terms, 0.0)
            total = total + folded(terms, jnp.sum)
            scores[tile, strip] = terms
        inverse = 1.0 / jnp.sum(total, axis=0, keepdims=True)
        for strip in strips(span):
            weights = scores[tile, strip] * inverse
            weights_b[tile, strip] = weights.astype(jnp.bfloat16)
            slopes_b[tile, strip] = (weights * (slopes[tile, strip] - delta)).astype(jnp.bfloat16)

    def leave(tile, queries, grads):
        start = tile * TILE
        keys = pl.ds(start, span)
        dv_sum[keys] += dot(weights_b[tile], grads, 1, 0)
        dk_sum[keys] += dot(slopes_b[tile], queries, 1, 0)
        dq = (dot(k_turned[:, keys], slopes_b[tile], 1, 0) * scale).T
        for m in range(members):
            dq_ref[start : start + TILE, m * head : (m + 1) * head] = dq[
                m * TILE : (m + 1) * TILE
            ].astype(dq_ref.dtype)

    entered = {0: enter(0)}
    for tile in tiles:
        if tile + 1 in tiles:
            entered[tile + 1] = enter(tile + 1)
        if tile:
            leave(tile - 1, *entered[tile - 1])
        weigh(tile)
    leave(tiles[-1], *entered[tiles[-1]])
    back_ref[0] = dk_sum[:window].astype(back_ref.dtype)
    back_ref[1] = dv_sum[:window].astype(back_ref.dtype)
    dk_ref[0] = dk_sum[window:].astype(dk_ref.dtype)
    dv_ref[0] = dv_sum[window:].astype(dv_ref.dtype)


def attention(group, low, arranged, past, first_head, heads_per_group, heads, carried):
    rows, window, count = arranged[3].shape[1], past.shape[1], past.shape[2] // HEAD_SIZE
    members = arranged[0].shape[1] // rows

    def leading(step, group_ref):
        return (group_ref[0] * count + step, 0, 0)

    def column(step, group_ref):
        return (0, group_ref[0] * heads_per_group + first_head + step)

    past_spec = pl.BlockSpec((2, window, HEAD_SIZE), lambda step, group_ref: (0, 0, step))
    low_spec = pl.BlockSpec((1, rows), lambda step, group_ref: (0, 0))
    own_spec = pl.BlockSpec((1, rows, HEAD_SIZE), lambda step, group_ref: (step, 0, 0))
    own_shape = jax.ShapeDtypeStruct((count, rows, HEAD_SIZE), jnp.bfloat16)
    square = (rows // TILE, window + TILE, members * TILE)
    tiles = count * members * rows * (window + TILE)
    return pl.pallas_call(
        functools.partial(attention_body, len(carried)),
        grid_spec=pltpu.PrefetchScalarGridSpec(
            num_scalar_prefetch=1,
            grid=(count,),
            in_specs=[low_spec]
            + [pl.BlockSpec((1, *array.shape[1:]), leading) for array in arranged]
            + [past_spec]
            + [pl.BlockSpec(memory_space=pl.ANY)] * len(carried),
            out_specs=[pl.BlockSpec((rows, members * HEAD_SIZE), column), own_spec, own_spec, past_spec],
            scratch_shapes=[
                pltpu.VMEM((window + rows, HEAD_SIZE), jnp.bfloat16),
                pltpu.VMEM((window + rows, HEAD_SIZE), jnp.bfloat16),
                pltpu.VMEM((HEAD_SIZE, window + rows), jnp.bfloat16),
                pltpu.VMEM((window + rows, HEAD_SIZE), jnp.float32),
                pltpu.VMEM((window + rows, HEAD_SIZE), jnp.float32),
                pltpu.VMEM(square, jnp.float32),
                pltpu.VMEM(square, jnp.float32),
                pltpu.VMEM(square, jnp.bfloat16),
                pltpu.VMEM(square, jnp.bfloat16),
            ],
        ),
        out_shape=[
            jax.ShapeDtypeStruct((rows, heads * members * HEAD_SIZE), jnp.bfloat16),
            own_shape,
            own_shape,
            jax.ShapeDtypeStruct(past.shape, jnp.bfloat16),
        ],
        input_output_aliases={9 + i: i for i in range(len(carried))},
        compiler_params=pltpu.CompilerParams(vmem_limit_bytes=VMEM_BYTES),
        cost_estimate=pl.CostEstimate(
            flops=10 * tiles * HEAD_SIZE, bytes_accessed=count * rows * 2400, transcendentals=tiles
        ),
        name="attention",
    )(group, low, *arranged, past, *carried)


def finish_body(carried, group_ref, dk_ref, dv_ref, back_ref, *refs):
    key_out, value_out = refs[carried:]
    sums = [
        own[0].astype(jnp.float32) + back_ref[i].astype(jnp.float32)
        for i, own in enumerate((dk_ref, dv_ref))
    ]
    key_out[...] = (sums[0] * HEAD_SIZE**-0.5).astype(key_out.dtype)
    value_out[...] = sums[1].astype(value_out.dtype)


def finish(group, own, back, first_head, heads_per_group, heads, carried):
    rows, count = back.shape[1], back.shape[2] // HEAD_SIZE

    def column(step, group_ref):
        return (0, group_ref[0] * heads_per_group + first_head + step)

    key_spec = pl.BlockSpec((rows, HEAD_SIZE), column)
    own_spec = pl.BlockSpec((1, rows, HEAD_SIZE), lambda step, group_ref: (step, 0, 0))
    back_spec = pl.BlockSpec((2, rows, HEAD_SIZE), lambda step, group_ref: (0, 0, step))
    return pl.pallas_call(
        functools.partial(finish_body, len(carried)),
        grid_spec=pltpu.PrefetchScalarGridSpec(
            num_scalar_prefetch=1,
            grid=(count,),
            in_specs=[own_spec, own_spec, back_spec]
            + [pl.BlockSpec(memory_space=pl.ANY)] * len(carried),
            out_specs=[key_spec, key_spec],
        ),
        out_shape=[jax.ShapeDtypeStruct((rows, heads * HEAD_SIZE), jnp.bfloat16)] * 2,
        input_output_aliases={4 + i: i for i in range(len(carried))},
        compiler_params=pltpu.CompilerParams(vmem_limit_bytes=VMEM_BYTES),
        cost_estimate=pl.CostEstimate(
            flops=count * rows * 512, bytes_accessed=count * rows * 2048, transcendentals=0
        ),
        name="finish",
    )(group, *own, back, *carried)


def together(*values):
    return lax.optimization_barrier(values)


def pick(items, index):
    result = items[-1]
    for place in range(len(items) - 2, -1, -1):
        result = jnp.where(index == place, items[place], result)
    return result


def local(queries, keys, values, outputs, out_grads, segment_ids, block_order):
    blocks, sharers = lax.axis_size("blk"), lax.axis_size("head")
    block, place = lax.axis_index("blk"), lax.axis_index("head")
    rows = keys.shape[0]
    window = rows * sharers // 2
    parts = sharers // 2
    key_heads = keys.shape[1] // HEAD_SIZE
    heads_per_group = key_heads // sharers
    chunks = min(CHUNKS, heads_per_group)
    per_piece = heads_per_group // chunks
    slots = lax.dynamic_slice_in_dim(block_order, 2 * block, 2)
    early_slot = (slots[0] > slots[1]).astype(jnp.int32)
    last_block = block == blocks - 1

    def other(turn):
        return lax.rem(place + turn + sharers, sharers)

    def turned(value, turn):
        pairs = [(source, (source + turn) % sharers) for source in range(sharers)]
        return lax.ppermute(value, "head", pairs)

    def shifted(value, step):
        first, end = max(0, -step), min(blocks, blocks - step)
        return lax.ppermute(value, "blk", [(source, source + step) for source in range(first, end)])

    def columns(array, group, chunk):
        pieces = []
        for g in range(sharers):
            start = (g * heads_per_group + chunk * per_piece) * HEAD_SIZE
            pieces.append(array[:, start : start + per_piece * HEAD_SIZE])
        return pick(pieces, group)

    def piece_of(group, chunk):
        return jnp.stack([columns(keys, group, chunk), columns(values, group, chunk)])

    def is_early(device):
        return device // parts == early_slot

    def part_rows(array, device, count):
        if parts == 1:
            return array[:, :count]
        return lax.dynamic_slice_in_dim(array, device % parts * rows, count, 1)

    my_half = pick([slots[0], slots[1]], place // parts)
    start = my_half * window + place % parts * rows
    padded = jnp.concatenate([jnp.full((window,), -1, jnp.int32), segment_ids])
    near = lax.dynamic_slice_in_dim(padded, start, window + rows)
    low = jnp.sum((near[None, :] < near[window:, None]).astype(jnp.int32), axis=1)[None, :]

    row_arrays = (queries, keys, values, outputs, out_grads)
    groups = [other(-turn) for turn in range(sharers)]

    def halves_of(pieces):
        return [
            jnp.concatenate(
                [
                    pick(pieces, lax.rem(place - (slot * parts + p) + sharers, sharers))
                    for p in range(parts)
                ],
                axis=1,
            )
            for slot in (early_slot, 1 - early_slot)
        ]

    arranged, halves = [], []
    for chunk in range(chunks):
        pieces = [piece_of(place, chunk)]
        pieces += [turned(piece_of(other(turn), chunk), turn) for turn in range(1, sharers)]
        arrays = arrange(row_arrays, chunk * per_piece, heads_per_group, per_piece)
        *arrays, pieces[-1] = together(*arrays, pieces[-1])
        arranged.append(arrays)
        halves.append(halves_of(pieces))
    before = [(shifted(early, 1), shifted(late, -1)) for early, late in halves]

    def run(turn, chunk, past, carried):
        query_grads, *own[chunk, turn], back = attention(
            groups[turn].reshape(1), low, arranged[chunk], past,
            chunk * per_piece, heads_per_group, key_heads, carried,
        )
        return (query_grads,), back

    carried, own, terms, pasts = (), {}, [], []
    for chunk in range(chunks):
        (early, late), (before_early, before_late) = halves[chunk], before[chunk]
        if chunk:
            *carried, before_early, before_late = together(*carried, before_early, before_late)
        before_late = jnp.where(last_block, early, before_late)

        def past_of(device):
            before = jnp.where(is_early(device), before_early, before_late)
            if parts == 1:
                return before
            own = jnp.where(is_early(device), early, late)
            return part_rows(jnp.concatenate([before, own], axis=1), device, window)

        pasts.append([turned(past_of(other(turn)), turn) for turn in range(1, sharers)])
        carried, back = run(0, chunk, past_of(place), carried)
        terms.append([back])

    for chunk in range(chunks):
        for turn in range(1, sharers):
            carried, back = run(turn, chunk, pasts[chunk][turn - 1], carried)
            terms[chunk].append(turned(back, -turn))

    (query_grads,) = carried
    results = ()
    for chunk in range(chunks):
        to_before, to_own = [], []
        for slot in (early_slot, 1 - early_slot):
            if parts == 1:
                to_before.append(pick(terms[chunk], lax.rem(slot - place + sharers, sharers)))
                to_own.append(None)
            else:
                total = jnp.zeros((2, 2 * window, terms[chunk][0].shape[2]), jnp.float32)
                for turn in range(sharers):
                    device = other(turn)
                    mine = jnp.where(device // parts == slot, terms[chunk][turn].astype(jnp.float32), 0.0)
                    wide = jnp.pad(mine, ((0, 0), (window, window), (0, 0)))
                    total += lax.dynamic_slice_in_dim(
                        wide, window - device % parts * rows, 2 * window, 1
                    )
                to_before.append(total[:, :window].astype(jnp.bfloat16))
                to_own.append(total[:, window:])
        for_early, for_late = shifted(to_before[0], -1), shifted(to_before[1], 1)
        for_early = jnp.where(last_block, to_before[1], for_early)
        sums = [
            came if more is None else (came.astype(jnp.float32) + more).astype(jnp.bfloat16)
            for came, more in zip((for_early, for_late), to_own)
        ]

        def rows_of(device):
            return part_rows(jnp.where(is_early(device), sums[0], sums[1]), device, rows)

        for turn in range(sharers):
            back = rows_of(other(turn))
            if turn:
                back = turned(back, turn)
            results = finish(
                groups[turn].reshape(1), own[chunk, turn], back,
                chunk * per_piece, heads_per_group, key_heads, tuple(results),
            )
    return (query_grads, *results)


def solution(mesh):
    spread = P(("blk", "head"), None)
    return jax.shard_map(
        local,
        mesh=mesh,
        in_specs=(spread,) * 5 + (P(), P()),
        out_specs=(spread,) * 3,
        check_vma=False,
    )
```

```python
import functools

import jax
import jax.numpy as jnp
from jax import lax
from jax.experimental import pallas as pl
from jax.experimental.pallas import tpu as pltpu
from jax.sharding import PartitionSpec as P

HEAD_SIZE = 128
NEGATIVE = -1e30
LOG2_E = 1.4426950408889634
CHUNKS = 2
TILE = 128
STRIP = 64
VMEM_BYTES = 16 * 1024 * 1024
SMALL_VMEM_BYTES = 6 * 1024 * 1024


def dot(left, right, left_dim, right_dim):
    return lax.dot_general(
        left, right, (((left_dim,), (right_dim,)), ((), ())), preferred_element_type=jnp.float32
    )


def strips(count):
    return [slice(start, start + STRIP) for start in range(0, count, STRIP)]


def folded(strip, reduce):
    return reduce(strip.reshape(strip.shape[0] // 8, 8, strip.shape[1]), axis=0)


def arrange_body(q_ref, k_ref, v_ref, o_ref, do_ref, q_out, do_out, delta_out, k_out, k_turned_out, v_out):
    rows, head = k_ref.shape
    members = q_ref.shape[1] // head
    for tile in range(rows // TILE):
        own = slice(tile * TILE, (tile + 1) * TILE)
        for m in range(members):
            place = slice((tile * members + m) * TILE, (tile * members + m + 1) * TILE)
            columns = slice(m * head, (m + 1) * head)
            q_out[0, place] = q_ref[own, columns]
            do_out[0, place] = do_ref[own, columns]
            product = do_ref[own, columns].astype(jnp.float32) * o_ref[own, columns].astype(jnp.float32)
            delta_out[0, :, place] = jnp.sum(product.T, axis=0, keepdims=True)
    k_out[0] = k_ref[...]
    k_turned_out[0] = k_ref[...].T
    v_out[0] = v_ref[...]


def arrange(row_arrays):
    queries, keys, values, outputs, grads = row_arrays
    rows, members = keys.shape[0], queries.shape[1] // keys.shape[1]
    count = keys.shape[1] // HEAD_SIZE

    def column(step):
        return (0, step)

    def leading(step):
        return (step, 0, 0)

    query_spec = pl.BlockSpec((rows, members * HEAD_SIZE), column)
    key_spec = pl.BlockSpec((rows, HEAD_SIZE), column)
    shapes = [
        ((members * rows, HEAD_SIZE), jnp.bfloat16),
        ((members * rows, HEAD_SIZE), jnp.bfloat16),
        ((1, members * rows), jnp.float32),
        ((rows, HEAD_SIZE), jnp.bfloat16),
        ((HEAD_SIZE, rows), jnp.bfloat16),
        ((rows, HEAD_SIZE), jnp.bfloat16),
    ]
    return pl.pallas_call(
        arrange_body,
        grid=(count,),
        in_specs=[query_spec, key_spec, key_spec, query_spec, query_spec],
        out_specs=[pl.BlockSpec((1, *shape), leading) for shape, _ in shapes],
        out_shape=[jax.ShapeDtypeStruct((count, *shape), dtype) for shape, dtype in shapes],
        compiler_params=pltpu.CompilerParams(vmem_limit_bytes=SMALL_VMEM_BYTES),
        cost_estimate=pl.CostEstimate(
            flops=count * rows * 1024, bytes_accessed=count * rows * 4096, transcendentals=0
        ),
        name="arrange",
    )(queries, keys, values, outputs, grads)


def attention_body(
    carried, group_ref, low_ref, q_ref, do_ref, delta_ref, k_ref, k_turned_ref, v_ref, past_ref, *refs
):
    dq_ref, dk_ref, dv_ref, back_ref = refs[carried : carried + 4]
    k_all, v_all, k_turned, dk_sum, dv_sum, scores, slopes, weights_b, slopes_b = refs[carried + 4 :]
    rows, head = k_ref.shape[1:]
    window = past_ref.shape[1]
    members = q_ref.shape[1] // rows
    span, lanes = window + TILE, members * TILE
    scale = head**-0.5
    k_all[:window] = past_ref[0]
    k_all[window:] = k_ref[0]
    v_all[:window] = past_ref[1]
    v_all[window:] = v_ref[0]
    k_turned[:, :window] = past_ref[0].T
    k_turned[:, window:] = k_turned_ref[0]
    dk_sum[...] = jnp.zeros_like(dk_sum)
    dv_sum[...] = jnp.zeros_like(dv_sum)
    lane = lax.broadcasted_iota(jnp.int32, (1, lanes), 1) % TILE
    tiles = range(rows // TILE)

    def enter(tile):
        keys = pl.ds(tile * TILE, span)
        place = pl.ds(tile * lanes, lanes)
        queries, grads = q_ref[0, place], do_ref[0, place]
        scores[tile] = dot(k_all[keys], queries, 1, 1)
        slopes[tile] = dot(v_all[keys], grads, 1, 1)
        return queries, grads

    def weigh(tile):
        start = tile * TILE
        delta = delta_ref[0, :, pl.ds(tile * lanes, lanes)]
        low = jnp.concatenate([low_ref[:, start : start + TILE]] * members, axis=1) - start

        def visible(strip):
            index = strip.start + lax.broadcasted_iota(jnp.int32, (STRIP, lanes), 0)
            seen = index >= low
            return seen & (index <= window + lane) if strip.stop > window else seen

        top = jnp.full((8, lanes), NEGATIVE, jnp.float32)
        for strip in strips(span):
            masked = jnp.where(visible(strip), scores[tile, strip], NEGATIVE)
            top = jnp.maximum(top, folded(masked, jnp.max))
        top = jnp.max(top, axis=0, keepdims=True)
        total = jnp.zeros((8, lanes), jnp.float32)
        for strip in strips(span):
            terms = jnp.exp2((scores[tile, strip] - top) * (scale * LOG2_E))
            terms = jnp.where(visible(strip), terms, 0.0)
            total = total + folded(terms, jnp.sum)
            scores[tile, strip] = terms
        inverse = 1.0 / jnp.sum(total, axis=0, keepdims=True)
        for strip in strips(span):
            weights = scores[tile, strip] * inverse
            weights_b[tile, strip] = weights.astype(jnp.bfloat16)
            slopes_b[tile, strip] = (weights * (slopes[tile, strip] - delta)).astype(jnp.bfloat16)

    def leave(tile, queries, grads):
        start = tile * TILE
        keys = pl.ds(start, span)
        dv_sum[keys] += dot(weights_b[tile], grads, 1, 0)
        dk_sum[keys] += dot(slopes_b[tile], queries, 1, 0)
        dq = (dot(k_turned[:, keys], slopes_b[tile], 1, 0) * scale).T
        for m in range(members):
            dq_ref[start : start + TILE, m * head : (m + 1) * head] = dq[
                m * TILE : (m + 1) * TILE
            ].astype(dq_ref.dtype)

    entered = {0: enter(0)}
    for tile in tiles:
        if tile + 1 in tiles:
            entered[tile + 1] = enter(tile + 1)
        if tile:
            leave(tile - 1, *entered[tile - 1])
        weigh(tile)
    leave(tiles[-1], *entered[tiles[-1]])
    back_ref[0] = dk_sum[:window].astype(back_ref.dtype)
    back_ref[1] = dv_sum[:window].astype(back_ref.dtype)
    dk_ref[0] = dk_sum[window:].astype(dk_ref.dtype)
    dv_ref[0] = dv_sum[window:].astype(dv_ref.dtype)


def attention(group, low, arranged, past, first_head, heads_per_group, heads, carried):
    rows, window, count = arranged[3].shape[1], past.shape[1], past.shape[2] // HEAD_SIZE
    members = arranged[0].shape[1] // rows

    def leading(step, group_ref):
        return (group_ref[0] * heads_per_group + first_head + step, 0, 0)

    def column(step, group_ref):
        return (0, group_ref[0] * heads_per_group + first_head + step)

    past_spec = pl.BlockSpec((2, window, HEAD_SIZE), lambda step, group_ref: (0, 0, step))
    low_spec = pl.BlockSpec((1, rows), lambda step, group_ref: (0, 0))
    own_spec = pl.BlockSpec((1, rows, HEAD_SIZE), lambda step, group_ref: (step, 0, 0))
    own_shape = jax.ShapeDtypeStruct((count, rows, HEAD_SIZE), jnp.bfloat16)
    square = (rows // TILE, window + TILE, members * TILE)
    tiles = count * members * rows * (window + TILE)
    return pl.pallas_call(
        functools.partial(attention_body, len(carried)),
        grid_spec=pltpu.PrefetchScalarGridSpec(
            num_scalar_prefetch=1,
            grid=(count,),
            in_specs=[low_spec]
            + [pl.BlockSpec((1, *array.shape[1:]), leading) for array in arranged]
            + [past_spec]
            + [pl.BlockSpec(memory_space=pl.ANY)] * len(carried),
            out_specs=[pl.BlockSpec((rows, members * HEAD_SIZE), column), own_spec, own_spec, past_spec],
            scratch_shapes=[
                pltpu.VMEM((window + rows, HEAD_SIZE), jnp.bfloat16),
                pltpu.VMEM((window + rows, HEAD_SIZE), jnp.bfloat16),
                pltpu.VMEM((HEAD_SIZE, window + rows), jnp.bfloat16),
                pltpu.VMEM((window + rows, HEAD_SIZE), jnp.float32),
                pltpu.VMEM((window + rows, HEAD_SIZE), jnp.float32),
                pltpu.VMEM(square, jnp.float32),
                pltpu.VMEM(square, jnp.float32),
                pltpu.VMEM(square, jnp.bfloat16),
                pltpu.VMEM(square, jnp.bfloat16),
            ],
        ),
        out_shape=[
            jax.ShapeDtypeStruct((rows, heads * members * HEAD_SIZE), jnp.bfloat16),
            own_shape,
            own_shape,
            jax.ShapeDtypeStruct(past.shape, jnp.bfloat16),
        ],
        input_output_aliases={9 + i: i for i in range(len(carried))},
        compiler_params=pltpu.CompilerParams(vmem_limit_bytes=VMEM_BYTES),
        cost_estimate=pl.CostEstimate(
            flops=10 * tiles * HEAD_SIZE, bytes_accessed=count * rows * 2400, transcendentals=tiles
        ),
        name="attention",
    )(group, low, *arranged, past, *carried)


def finish_body(carried, group_ref, dk_ref, dv_ref, back_ref, *refs):
    key_out, value_out = refs[carried:]
    sums = [
        own[0].astype(jnp.float32) + back_ref[i].astype(jnp.float32)
        for i, own in enumerate((dk_ref, dv_ref))
    ]
    key_out[...] = (sums[0] * HEAD_SIZE**-0.5).astype(key_out.dtype)
    value_out[...] = sums[1].astype(value_out.dtype)


def finish(group, own, back, first_head, heads_per_group, heads, carried):
    rows, count = back.shape[1], back.shape[2] // HEAD_SIZE

    def column(step, group_ref):
        return (0, group_ref[0] * heads_per_group + first_head + step)

    key_spec = pl.BlockSpec((rows, HEAD_SIZE), column)
    own_spec = pl.BlockSpec((1, rows, HEAD_SIZE), lambda step, group_ref: (step, 0, 0))
    back_spec = pl.BlockSpec((2, rows, HEAD_SIZE), lambda step, group_ref: (0, 0, step))
    return pl.pallas_call(
        functools.partial(finish_body, len(carried)),
        grid_spec=pltpu.PrefetchScalarGridSpec(
            num_scalar_prefetch=1,
            grid=(count,),
            in_specs=[own_spec, own_spec, back_spec]
            + [pl.BlockSpec(memory_space=pl.ANY)] * len(carried),
            out_specs=[key_spec, key_spec],
        ),
        out_shape=[jax.ShapeDtypeStruct((rows, heads * HEAD_SIZE), jnp.bfloat16)] * 2,
        input_output_aliases={4 + i: i for i in range(len(carried))},
        compiler_params=pltpu.CompilerParams(vmem_limit_bytes=SMALL_VMEM_BYTES),
        cost_estimate=pl.CostEstimate(
            flops=count * rows * 512, bytes_accessed=count * rows * 2048, transcendentals=0
        ),
        name="finish",
    )(group, *own, back, *carried)


def together(*values):
    return lax.optimization_barrier(values)


def pick(items, index):
    result = items[-1]
    for place in range(len(items) - 2, -1, -1):
        result = jnp.where(index == place, items[place], result)
    return result


def local(queries, keys, values, outputs, out_grads, segment_ids, block_order):
    blocks, sharers = lax.axis_size("blk"), lax.axis_size("head")
    block, place = lax.axis_index("blk"), lax.axis_index("head")
    rows = keys.shape[0]
    window = rows * sharers // 2
    parts = sharers // 2
    key_heads = keys.shape[1] // HEAD_SIZE
    heads_per_group = key_heads // sharers
    chunks = min(CHUNKS, heads_per_group)
    per_piece = heads_per_group // chunks
    slots = lax.dynamic_slice_in_dim(block_order, 2 * block, 2)
    early_slot = (slots[0] > slots[1]).astype(jnp.int32)
    last_block = block == blocks - 1

    def other(turn):
        return lax.rem(place + turn + sharers, sharers)

    def turned(value, turn):
        pairs = [(source, (source + turn) % sharers) for source in range(sharers)]
        return lax.ppermute(value, "head", pairs)

    def shifted(value, step):
        first, end = max(0, -step), min(blocks, blocks - step)
        return lax.ppermute(value, "blk", [(source, source + step) for source in range(first, end)])

    def columns(array, group, chunk):
        pieces = []
        for g in range(sharers):
            start = (g * heads_per_group + chunk * per_piece) * HEAD_SIZE
            pieces.append(array[:, start : start + per_piece * HEAD_SIZE])
        return pick(pieces, group)

    def piece_of(group, chunk):
        return jnp.stack([columns(keys, group, chunk), columns(values, group, chunk)])

    def is_early(device):
        return device // parts == early_slot

    def part_rows(array, device, count):
        if parts == 1:
            return array[:, :count]
        return lax.dynamic_slice_in_dim(array, device % parts * rows, count, 1)

    my_half = pick([slots[0], slots[1]], place // parts)
    start = my_half * window + place % parts * rows
    padded = jnp.concatenate([jnp.full((window,), -1, jnp.int32), segment_ids])
    near = lax.dynamic_slice_in_dim(padded, start, window + rows)
    low = jnp.sum((near[None, :] < near[window:, None]).astype(jnp.int32), axis=1)[None, :]

    row_arrays = (queries, keys, values, outputs, out_grads)
    groups = [other(-turn) for turn in range(sharers)]

    def halves_of(pieces):
        return [
            jnp.concatenate(
                [
                    pick(pieces, lax.rem(place - (slot * parts + p) + sharers, sharers))
                    for p in range(parts)
                ],
                axis=1,
            )
            for slot in (early_slot, 1 - early_slot)
        ]

    arranged, halves = arrange(row_arrays), []
    for chunk in range(chunks):
        pieces = [piece_of(place, chunk)]
        pieces += [turned(piece_of(other(turn), chunk), turn) for turn in range(1, sharers)]
        if not halves:
            *arranged, pieces[-1] = together(*arranged, pieces[-1])
        halves.append(halves_of(pieces))
    before = [(shifted(early, 1), shifted(late, -1)) for early, late in halves]

    def run(turn, chunk, past, carried):
        query_grads, *own[chunk, turn], back = attention(
            groups[turn].reshape(1), low, arranged, past,
            chunk * per_piece, heads_per_group, key_heads, carried,
        )
        return (query_grads,), back

    carried, own, terms, pasts = (), {}, [], []
    for chunk in range(chunks):
        (early, late), (before_early, before_late) = halves[chunk], before[chunk]
        if chunk:
            *carried, before_early, before_late = together(*carried, before_early, before_late)
        before_late = jnp.where(last_block, early, before_late)

        def past_of(device):
            before = jnp.where(is_early(device), before_early, before_late)
            if parts == 1:
                return before
            own = jnp.where(is_early(device), early, late)
            return part_rows(jnp.concatenate([before, own], axis=1), device, window)

        pasts.append([turned(past_of(other(turn)), turn) for turn in range(1, sharers)])
        carried, back = run(0, chunk, past_of(place), carried)
        terms.append([back])

    for chunk in range(chunks):
        for turn in range(1, sharers):
            carried, back = run(turn, chunk, pasts[chunk][turn - 1], carried)
            terms[chunk].append(turned(back, -turn))

    (query_grads,) = carried
    results = ()
    for chunk in range(chunks):
        to_before, to_own = [], []
        for slot in (early_slot, 1 - early_slot):
            if parts == 1:
                to_before.append(pick(terms[chunk], lax.rem(slot - place + sharers, sharers)))
                to_own.append(None)
            else:
                total = jnp.zeros((2, 2 * window, terms[chunk][0].shape[2]), jnp.float32)
                for turn in range(sharers):
                    device = other(turn)
                    mine = jnp.where(device // parts == slot, terms[chunk][turn].astype(jnp.float32), 0.0)
                    wide = jnp.pad(mine, ((0, 0), (window, window), (0, 0)))
                    total += lax.dynamic_slice_in_dim(
                        wide, window - device % parts * rows, 2 * window, 1
                    )
                to_before.append(total[:, :window].astype(jnp.bfloat16))
                to_own.append(total[:, window:])
        for_early, for_late = shifted(to_before[0], -1), shifted(to_before[1], 1)
        for_early = jnp.where(last_block, to_before[1], for_early)
        sums = [
            came if more is None else (came.astype(jnp.float32) + more).astype(jnp.bfloat16)
            for came, more in zip((for_early, for_late), to_own)
        ]

        def rows_of(device):
            return part_rows(jnp.where(is_early(device), sums[0], sums[1]), device, rows)

        for turn in range(sharers):
            back = rows_of(other(turn))
            if turn:
                back = turned(back, turn)
            results = finish(
                groups[turn].reshape(1), own[chunk, turn], back,
                chunk * per_piece, heads_per_group, key_heads, tuple(results),
            )
    return (query_grads, *results)


def solution(mesh):
    spread = P(("blk", "head"), None)
    return jax.shard_map(
        local,
        mesh=mesh,
        in_specs=(spread,) * 5 + (P(), P()),
        out_specs=(spread,) * 3,
        check_vma=False,
    )
```

```python
import functools

import jax
import jax.numpy as jnp
from jax import lax
from jax.experimental import pallas as pl
from jax.experimental.pallas import tpu as pltpu
from jax.sharding import PartitionSpec as P

HEAD_SIZE = 128
NEGATIVE = -1e30
LOG2_E = 1.4426950408889634
CHUNKS = 2
TILE = 128
STRIP = 64
VMEM_BYTES = 60 * 1024 * 1024
FINISH_VMEM_BYTES = 6 * 1024 * 1024


def dot(left, right, left_dim, right_dim):
    return lax.dot_general(
        left, right, (((left_dim,), (right_dim,)), ((), ())), preferred_element_type=jnp.float32
    )


def strips(count):
    return [slice(start, start + STRIP) for start in range(0, count, STRIP)]


def folded(strip, reduce):
    return reduce(strip.reshape(strip.shape[0] // 8, 8, strip.shape[1]), axis=0)


def arrange_body(q_ref, k_ref, v_ref, o_ref, do_ref, q_out, do_out, delta_out, k_out, k_turned_out, v_out):
    rows, head = k_ref.shape
    members = q_ref.shape[1] // head
    for tile in range(rows // TILE):
        own = slice(tile * TILE, (tile + 1) * TILE)
        for m in range(members):
            place = slice((tile * members + m) * TILE, (tile * members + m + 1) * TILE)
            columns = slice(m * head, (m + 1) * head)
            q_out[0, place] = q_ref[own, columns]
            do_out[0, place] = do_ref[own, columns]
            product = do_ref[own, columns].astype(jnp.float32) * o_ref[own, columns].astype(jnp.float32)
            delta_out[0, :, place] = jnp.sum(product.T, axis=0, keepdims=True)
    k_out[0] = k_ref[...]
    k_turned_out[0] = k_ref[...].T
    v_out[0] = v_ref[...]


def arrange(row_arrays, first_head, heads_per_group, per_piece):
    queries, keys, values, outputs, grads = row_arrays
    rows, members = keys.shape[0], queries.shape[1] // keys.shape[1]
    groups = keys.shape[1] // HEAD_SIZE // heads_per_group
    count = groups * per_piece

    def column(group, step):
        return (0, group * heads_per_group + first_head + step)

    def leading(group, step):
        return (group * per_piece + step, 0, 0)

    query_spec = pl.BlockSpec((rows, members * HEAD_SIZE), column)
    key_spec = pl.BlockSpec((rows, HEAD_SIZE), column)
    shapes = [
        ((members * rows, HEAD_SIZE), jnp.bfloat16),
        ((members * rows, HEAD_SIZE), jnp.bfloat16),
        ((1, members * rows), jnp.float32),
        ((rows, HEAD_SIZE), jnp.bfloat16),
        ((HEAD_SIZE, rows), jnp.bfloat16),
        ((rows, HEAD_SIZE), jnp.bfloat16),
    ]
    return pl.pallas_call(
        arrange_body,
        grid=(groups, per_piece),
        in_specs=[query_spec, key_spec, key_spec, query_spec, query_spec],
        out_specs=[pl.BlockSpec((1, *shape), leading) for shape, _ in shapes],
        out_shape=[jax.ShapeDtypeStruct((count, *shape), dtype) for shape, dtype in shapes],
        compiler_params=pltpu.CompilerParams(vmem_limit_bytes=VMEM_BYTES),
        cost_estimate=pl.CostEstimate(
            flops=count * rows * 1024, bytes_accessed=count * rows * 4096, transcendentals=0
        ),
        name="arrange",
    )(queries, keys, values, outputs, grads)


def attention_body(
    carried, group_ref, low_ref, q_ref, do_ref, delta_ref, k_ref, k_turned_ref, v_ref, past_ref, *refs
):
    dq_ref, dk_ref, dv_ref, back_ref = refs[carried : carried + 4]
    k_all, v_all, k_turned, dk_sum, dv_sum, scores, slopes, weights_b, slopes_b = refs[carried + 4 :]
    rows, head = k_ref.shape[1:]
    window = past_ref.shape[1]
    members = q_ref.shape[1] // rows
    span, lanes = window + TILE, members * TILE
    scale = head**-0.5
    k_all[:window] = past_ref[0]
    k_all[window:] = k_ref[0]
    v_all[:window] = past_ref[1]
    v_all[window:] = v_ref[0]
    k_turned[:, :window] = past_ref[0].T
    k_turned[:, window:] = k_turned_ref[0]
    dk_sum[...] = jnp.zeros_like(dk_sum)
    dv_sum[...] = jnp.zeros_like(dv_sum)
    lane = lax.broadcasted_iota(jnp.int32, (1, lanes), 1) % TILE
    tiles = range(rows // TILE)

    def enter(tile):
        keys = pl.ds(tile * TILE, span)
        place = pl.ds(tile * lanes, lanes)
        queries, grads = q_ref[0, place], do_ref[0, place]
        scores[tile] = dot(k_all[keys], queries, 1, 1)
        slopes[tile] = dot(v_all[keys], grads, 1, 1)
        return queries, grads

    def weigh(tile):
        start = tile * TILE
        delta = delta_ref[0, :, pl.ds(tile * lanes, lanes)]
        low = jnp.concatenate([low_ref[:, start : start + TILE]] * members, axis=1) - start

        def visible(strip):
            index = strip.start + lax.broadcasted_iota(jnp.int32, (STRIP, lanes), 0)
            seen = index >= low
            return seen & (index <= window + lane) if strip.stop > window else seen

        top = jnp.full((8, lanes), NEGATIVE, jnp.float32)
        for strip in strips(span):
            masked = jnp.where(visible(strip), scores[tile, strip], NEGATIVE)
            top = jnp.maximum(top, folded(masked, jnp.max))
        top = jnp.max(top, axis=0, keepdims=True)
        total = jnp.zeros((8, lanes), jnp.float32)
        for strip in strips(span):
            terms = jnp.exp2((scores[tile, strip] - top) * (scale * LOG2_E))
            terms = jnp.where(visible(strip), terms, 0.0)
            total = total + folded(terms, jnp.sum)
            scores[tile, strip] = terms
        inverse = 1.0 / jnp.sum(total, axis=0, keepdims=True)
        for strip in strips(span):
            weights = scores[tile, strip] * inverse
            weights_b[tile, strip] = weights.astype(jnp.bfloat16)
            slopes_b[tile, strip] = (weights * (slopes[tile, strip] - delta)).astype(jnp.bfloat16)

    def leave(tile, queries, grads):
        start = tile * TILE
        keys = pl.ds(start, span)
        dv_sum[keys] += dot(weights_b[tile], grads, 1, 0)
        dk_sum[keys] += dot(slopes_b[tile], queries, 1, 0)
        dq = (dot(k_turned[:, keys], slopes_b[tile], 1, 0) * scale).T
        for m in range(members):
            dq_ref[start : start + TILE, m * head : (m + 1) * head] = dq[
                m * TILE : (m + 1) * TILE
            ].astype(dq_ref.dtype)

    entered = {0: enter(0)}
    for tile in tiles:
        if tile + 1 in tiles:
            entered[tile + 1] = enter(tile + 1)
        if tile:
            leave(tile - 1, *entered[tile - 1])
        weigh(tile)
    leave(tiles[-1], *entered[tiles[-1]])
    back_ref[0] = dk_sum[:window].astype(back_ref.dtype)
    back_ref[1] = dv_sum[:window].astype(back_ref.dtype)
    dk_ref[0] = dk_sum[window:].astype(dk_ref.dtype)
    dv_ref[0] = dv_sum[window:].astype(dv_ref.dtype)


def attention(group, low, arranged, past, first_head, heads_per_group, heads, carried):
    rows, window, count = arranged[3].shape[1], past.shape[1], past.shape[2] // HEAD_SIZE
    members = arranged[0].shape[1] // rows

    def leading(step, group_ref):
        return (group_ref[0] * count + step, 0, 0)

    def column(step, group_ref):
        return (0, group_ref[0] * heads_per_group + first_head + step)

    past_spec = pl.BlockSpec((2, window, HEAD_SIZE), lambda step, group_ref: (0, 0, step))
    low_spec = pl.BlockSpec((1, rows), lambda step, group_ref: (0, 0))
    own_spec = pl.BlockSpec((1, rows, HEAD_SIZE), lambda step, group_ref: (step, 0, 0))
    own_shape = jax.ShapeDtypeStruct((count, rows, HEAD_SIZE), jnp.bfloat16)
    square = (rows // TILE, window + TILE, members * TILE)
    tiles = count * members * rows * (window + TILE)
    return pl.pallas_call(
        functools.partial(attention_body, len(carried)),
        grid_spec=pltpu.PrefetchScalarGridSpec(
            num_scalar_prefetch=1,
            grid=(count,),
            in_specs=[low_spec]
            + [pl.BlockSpec((1, *array.shape[1:]), leading) for array in arranged]
            + [past_spec]
            + [pl.BlockSpec(memory_space=pl.ANY)] * len(carried),
            out_specs=[pl.BlockSpec((rows, members * HEAD_SIZE), column), own_spec, own_spec, past_spec],
            scratch_shapes=[
                pltpu.VMEM((window + rows, HEAD_SIZE), jnp.bfloat16),
                pltpu.VMEM((window + rows, HEAD_SIZE), jnp.bfloat16),
                pltpu.VMEM((HEAD_SIZE, window + rows), jnp.bfloat16),
                pltpu.VMEM((window + rows, HEAD_SIZE), jnp.float32),
                pltpu.VMEM((window + rows, HEAD_SIZE), jnp.float32),
                pltpu.VMEM(square, jnp.float32),
                pltpu.VMEM(square, jnp.float32),
                pltpu.VMEM(square, jnp.bfloat16),
                pltpu.VMEM(square, jnp.bfloat16),
            ],
        ),
        out_shape=[
            jax.ShapeDtypeStruct((rows, heads * members * HEAD_SIZE), jnp.bfloat16),
            own_shape,
            own_shape,
            jax.ShapeDtypeStruct(past.shape, jnp.bfloat16),
        ],
        input_output_aliases={9 + i: i for i in range(len(carried))},
        compiler_params=pltpu.CompilerParams(vmem_limit_bytes=VMEM_BYTES),
        cost_estimate=pl.CostEstimate(
            flops=10 * tiles * HEAD_SIZE, bytes_accessed=count * rows * 2400, transcendentals=tiles
        ),
        name="attention",
    )(group, low, *arranged, past, *carried)


def finish_body(carried, group_ref, dk_ref, dv_ref, back_ref, *refs):
    key_out, value_out = refs[carried:]
    sums = [
        own[0].astype(jnp.float32) + back_ref[i].astype(jnp.float32)
        for i, own in enumerate((dk_ref, dv_ref))
    ]
    key_out[...] = (sums[0] * HEAD_SIZE**-0.5).astype(key_out.dtype)
    value_out[...] = sums[1].astype(value_out.dtype)


def finish(group, own, back, first_head, heads_per_group, heads, carried):
    rows, count = back.shape[1], back.shape[2] // HEAD_SIZE

    def column(step, group_ref):
        return (0, group_ref[0] * heads_per_group + first_head + step)

    key_spec = pl.BlockSpec((rows, HEAD_SIZE), column)
    own_spec = pl.BlockSpec((1, rows, HEAD_SIZE), lambda step, group_ref: (step, 0, 0))
    back_spec = pl.BlockSpec((2, rows, HEAD_SIZE), lambda step, group_ref: (0, 0, step))
    return pl.pallas_call(
        functools.partial(finish_body, len(carried)),
        grid_spec=pltpu.PrefetchScalarGridSpec(
            num_scalar_prefetch=1,
            grid=(count,),
            in_specs=[own_spec, own_spec, back_spec]
            + [pl.BlockSpec(memory_space=pl.ANY)] * len(carried),
            out_specs=[key_spec, key_spec],
        ),
        out_shape=[jax.ShapeDtypeStruct((rows, heads * HEAD_SIZE), jnp.bfloat16)] * 2,
        input_output_aliases={4 + i: i for i in range(len(carried))},
        compiler_params=pltpu.CompilerParams(vmem_limit_bytes=FINISH_VMEM_BYTES),
        cost_estimate=pl.CostEstimate(
            flops=count * rows * 512, bytes_accessed=count * rows * 2048, transcendentals=0
        ),
        name="finish",
    )(group, *own, back, *carried)


def together(*values):
    return lax.optimization_barrier(values)


def pick(items, index):
    result = items[-1]
    for place in range(len(items) - 2, -1, -1):
        result = jnp.where(index == place, items[place], result)
    return result


def local(queries, keys, values, outputs, out_grads, segment_ids, block_order):
    blocks, sharers = lax.axis_size("blk"), lax.axis_size("head")
    block, place = lax.axis_index("blk"), lax.axis_index("head")
    rows = keys.shape[0]
    window = rows * sharers // 2
    parts = sharers // 2
    key_heads = keys.shape[1] // HEAD_SIZE
    heads_per_group = key_heads // sharers
    chunks = min(CHUNKS, heads_per_group)
    per_piece = heads_per_group // chunks
    slots = lax.dynamic_slice_in_dim(block_order, 2 * block, 2)
    early_slot = (slots[0] > slots[1]).astype(jnp.int32)
    last_block = block == blocks - 1

    def other(turn):
        return lax.rem(place + turn + sharers, sharers)

    def turned(value, turn):
        pairs = [(source, (source + turn) % sharers) for source in range(sharers)]
        return lax.ppermute(value, "head", pairs)

    def shifted(value, step):
        first, end = max(0, -step), min(blocks, blocks - step)
        return lax.ppermute(value, "blk", [(source, source + step) for source in range(first, end)])

    def columns(array, group, chunk):
        pieces = []
        for g in range(sharers):
            start = (g * heads_per_group + chunk * per_piece) * HEAD_SIZE
            pieces.append(array[:, start : start + per_piece * HEAD_SIZE])
        return pick(pieces, group)

    def piece_of(group, chunk):
        return jnp.stack([columns(keys, group, chunk), columns(values, group, chunk)])

    def is_early(device):
        return device // parts == early_slot

    def part_rows(array, device, count):
        if parts == 1:
            return array[:, :count]
        return lax.dynamic_slice_in_dim(array, device % parts * rows, count, 1)

    my_half = pick([slots[0], slots[1]], place // parts)
    start = my_half * window + place % parts * rows
    padded = jnp.concatenate([jnp.full((window,), -1, jnp.int32), segment_ids])
    near = lax.dynamic_slice_in_dim(padded, start, window + rows)
    low = jnp.sum((near[None, :] < near[window:, None]).astype(jnp.int32), axis=1)[None, :]

    row_arrays = (queries, keys, values, outputs, out_grads)
    groups = [other(-turn) for turn in range(sharers)]

    def halves_of(pieces):
        return [
            jnp.concatenate(
                [
                    pick(pieces, lax.rem(place - (slot * parts + p) + sharers, sharers))
                    for p in range(parts)
                ],
                axis=1,
            )
            for slot in (early_slot, 1 - early_slot)
        ]

    arranged, halves = [], []
    for chunk in range(chunks):
        pieces = [piece_of(place, chunk)]
        pieces += [turned(piece_of(other(turn), chunk), turn) for turn in range(1, sharers)]
        arrays = arrange(row_arrays, chunk * per_piece, heads_per_group, per_piece)
        *arrays, pieces[-1] = together(*arrays, pieces[-1])
        arranged.append(arrays)
        halves.append(halves_of(pieces))
    before = [(shifted(early, 1), shifted(late, -1)) for early, late in halves]

    def run(turn, chunk, past, carried):
        query_grads, *own[chunk, turn], back = attention(
            groups[turn].reshape(1), low, arranged[chunk], past,
            chunk * per_piece, heads_per_group, key_heads, carried,
        )
        return (query_grads,), back

    carried, own, terms, pasts = (), {}, [], []
    for chunk in range(chunks):
        (early, late), (before_early, before_late) = halves[chunk], before[chunk]
        if chunk:
            *carried, before_early, before_late = together(*carried, before_early, before_late)
        before_late = jnp.where(last_block, early, before_late)

        def past_of(device):
            before = jnp.where(is_early(device), before_early, before_late)
            if parts == 1:
                return before
            own = jnp.where(is_early(device), early, late)
            return part_rows(jnp.concatenate([before, own], axis=1), device, window)

        pasts.append([turned(past_of(other(turn)), turn) for turn in range(1, sharers)])
        carried, back = run(0, chunk, past_of(place), carried)
        terms.append([back])

    for chunk in range(chunks):
        for turn in range(1, sharers):
            carried, back = run(turn, chunk, pasts[chunk][turn - 1], carried)
            terms[chunk].append(turned(back, -turn))

    (query_grads,) = carried
    results = ()
    for chunk in range(chunks):
        to_before, to_own = [], []
        for slot in (early_slot, 1 - early_slot):
            if parts == 1:
                to_before.append(pick(terms[chunk], lax.rem(slot - place + sharers, sharers)))
                to_own.append(None)
            else:
                total = jnp.zeros((2, 2 * window, terms[chunk][0].shape[2]), jnp.float32)
                for turn in range(sharers):
                    device = other(turn)
                    mine = jnp.where(device // parts == slot, terms[chunk][turn].astype(jnp.float32), 0.0)
                    wide = jnp.pad(mine, ((0, 0), (window, window), (0, 0)))
                    total += lax.dynamic_slice_in_dim(
                        wide, window - device % parts * rows, 2 * window, 1
                    )
                to_before.append(total[:, :window].astype(jnp.bfloat16))
                to_own.append(total[:, window:])
        for_early, for_late = shifted(to_before[0], -1), shifted(to_before[1], 1)
        for_early = jnp.where(last_block, to_before[1], for_early)
        sums = [
            came if more is None else (came.astype(jnp.float32) + more).astype(jnp.bfloat16)
            for came, more in zip((for_early, for_late), to_own)
        ]

        def rows_of(device):
            return part_rows(jnp.where(is_early(device), sums[0], sums[1]), device, rows)

        for turn in range(sharers):
            back = rows_of(other(turn))
            if turn:
                back = turned(back, turn)
            results = finish(
                groups[turn].reshape(1), own[chunk, turn], back,
                chunk * per_piece, heads_per_group, key_heads, tuple(results),
            )
    return (query_grads, *results)


def solution(mesh):
    spread = P(("blk", "head"), None)
    return jax.shard_map(
        local,
        mesh=mesh,
        in_specs=(spread,) * 5 + (P(), P()),
        out_specs=(spread,) * 3,
        check_vma=False,
    )
```

```python
import functools

import jax
import jax.numpy as jnp
from jax import lax
from jax.experimental import pallas as pl
from jax.experimental.pallas import tpu as pltpu
from jax.sharding import PartitionSpec as P

HEAD_SIZE = 128
NEGATIVE = -1e30
LOG2_E = 1.4426950408889634
CHUNKS = 2
TILE = 128
STRIP = 64
VMEM_BYTES = 60 * 1024 * 1024
FINISH_VMEM_BYTES = 6 * 1024 * 1024


def dot(left, right, left_dim, right_dim):
    return lax.dot_general(
        left, right, (((left_dim,), (right_dim,)), ((), ())), preferred_element_type=jnp.float32
    )


def strips(count):
    return [slice(start, start + STRIP) for start in range(0, count, STRIP)]


def folded(strip, reduce):
    return reduce(strip.reshape(strip.shape[0] // 8, 8, strip.shape[1]), axis=0)


def arrange_body(q_ref, k_ref, v_ref, o_ref, do_ref, q_out, do_out, delta_out, k_out, k_turned_out, v_out):
    rows, head = k_ref.shape
    members = q_ref.shape[1] // head
    for tile in range(rows // TILE):
        own = slice(tile * TILE, (tile + 1) * TILE)
        for m in range(members):
            place = slice((tile * members + m) * TILE, (tile * members + m + 1) * TILE)
            columns = slice(m * head, (m + 1) * head)
            q_out[0, place] = q_ref[own, columns]
            do_out[0, place] = do_ref[own, columns]
            product = do_ref[own, columns].astype(jnp.float32) * o_ref[own, columns].astype(jnp.float32)
            delta_out[0, :, place] = jnp.sum(product.T, axis=0, keepdims=True)
    k_out[0] = k_ref[...]
    k_turned_out[0] = k_ref[...].T
    v_out[0] = v_ref[...]


def arrange(row_arrays, first_head, heads_per_group, per_piece):
    queries, keys, values, outputs, grads = row_arrays
    rows, members = keys.shape[0], queries.shape[1] // keys.shape[1]
    groups = keys.shape[1] // HEAD_SIZE // heads_per_group
    count = groups * per_piece

    def column(group, step):
        return (0, group * heads_per_group + first_head + step)

    def leading(group, step):
        return (group * per_piece + step, 0, 0)

    query_spec = pl.BlockSpec((rows, members * HEAD_SIZE), column)
    key_spec = pl.BlockSpec((rows, HEAD_SIZE), column)
    shapes = [
        ((members * rows, HEAD_SIZE), jnp.bfloat16),
        ((members * rows, HEAD_SIZE), jnp.bfloat16),
        ((1, members * rows), jnp.float32),
        ((rows, HEAD_SIZE), jnp.bfloat16),
        ((HEAD_SIZE, rows), jnp.bfloat16),
        ((rows, HEAD_SIZE), jnp.bfloat16),
    ]
    return pl.pallas_call(
        arrange_body,
        grid=(groups, per_piece),
        in_specs=[query_spec, key_spec, key_spec, query_spec, query_spec],
        out_specs=[pl.BlockSpec((1, *shape), leading) for shape, _ in shapes],
        out_shape=[jax.ShapeDtypeStruct((count, *shape), dtype) for shape, dtype in shapes],
        compiler_params=pltpu.CompilerParams(vmem_limit_bytes=VMEM_BYTES),
        cost_estimate=pl.CostEstimate(
            flops=count * rows * 1024, bytes_accessed=count * rows * 4096, transcendentals=0
        ),
        name="arrange",
    )(queries, keys, values, outputs, grads)


def attention_body(
    carried, group_ref, low_ref, q_ref, do_ref, delta_ref, k_ref, k_turned_ref, v_ref, past_ref, *refs
):
    dq_ref, dk_ref, dv_ref, back_ref = refs[carried : carried + 4]
    k_all, v_all, k_turned, dk_sum, dv_sum, scores, slopes, weights_b, slopes_b = refs[carried + 4 :]
    rows, head = k_ref.shape[1:]
    window = past_ref.shape[1]
    members = q_ref.shape[1] // rows
    span, lanes = window + TILE, members * TILE
    scale = head**-0.5
    k_all[:window] = past_ref[0]
    k_all[window:] = k_ref[0]
    v_all[:window] = past_ref[1]
    v_all[window:] = v_ref[0]
    k_turned[:, :window] = past_ref[0].T
    k_turned[:, window:] = k_turned_ref[0]
    dk_sum[...] = jnp.zeros_like(dk_sum)
    dv_sum[...] = jnp.zeros_like(dv_sum)
    lane = lax.broadcasted_iota(jnp.int32, (1, lanes), 1) % TILE
    tiles = range(rows // TILE)

    def enter(tile):
        keys = pl.ds(tile * TILE, span)
        place = pl.ds(tile * lanes, lanes)
        queries, grads = q_ref[0, place], do_ref[0, place]
        scores[tile] = dot(k_all[keys], queries, 1, 1)
        slopes[tile] = dot(v_all[keys], grads, 1, 1)
        return queries, grads

    def weigh(tile):
        start = tile * TILE
        delta = delta_ref[0, :, pl.ds(tile * lanes, lanes)]
        low = jnp.concatenate([low_ref[:, start : start + TILE]] * members, axis=1) - start

        def visible(strip):
            index = strip.start + lax.broadcasted_iota(jnp.int32, (STRIP, lanes), 0)
            seen = index >= low
            return seen & (index <= window + lane) if strip.stop > window else seen

        top = jnp.full((8, lanes), NEGATIVE, jnp.float32)
        for strip in strips(span):
            masked = jnp.where(visible(strip), scores[tile, strip], NEGATIVE)
            top = jnp.maximum(top, folded(masked, jnp.max))
        top = jnp.max(top, axis=0, keepdims=True)
        total = jnp.zeros((8, lanes), jnp.float32)
        for strip in strips(span):
            terms = jnp.exp2((scores[tile, strip] - top) * (scale * LOG2_E))
            terms = jnp.where(visible(strip), terms, 0.0)
            total = total + folded(terms, jnp.sum)
            scores[tile, strip] = terms
        inverse = 1.0 / jnp.sum(total, axis=0, keepdims=True)
        for strip in strips(span):
            weights = scores[tile, strip] * inverse
            weights_b[tile, strip] = weights.astype(jnp.bfloat16)
            slopes_b[tile, strip] = (weights * (slopes[tile, strip] - delta)).astype(jnp.bfloat16)

    def leave(tile, queries, grads):
        start = tile * TILE
        keys = pl.ds(start, span)
        dv_sum[keys] += dot(weights_b[tile], grads, 1, 0)
        dk_sum[keys] += dot(slopes_b[tile], queries, 1, 0)
        dq = (dot(k_turned[:, keys], slopes_b[tile], 1, 0) * scale).T
        for m in range(members):
            dq_ref[start : start + TILE, m * head : (m + 1) * head] = dq[
                m * TILE : (m + 1) * TILE
            ].astype(dq_ref.dtype)

    entered = {0: enter(0)}
    for tile in tiles:
        if tile + 1 in tiles:
            entered[tile + 1] = enter(tile + 1)
        if tile:
            leave(tile - 1, *entered[tile - 1])
        weigh(tile)
    leave(tiles[-1], *entered[tiles[-1]])
    back_ref[0] = dk_sum[:window].astype(back_ref.dtype)
    back_ref[1] = dv_sum[:window].astype(back_ref.dtype)
    dk_ref[0] = dk_sum[window:].astype(dk_ref.dtype)
    dv_ref[0] = dv_sum[window:].astype(dv_ref.dtype)


def attention(group, low, arranged, past, first_head, heads_per_group, heads, carried):
    rows, window, count = arranged[3].shape[1], past.shape[1], past.shape[2] // HEAD_SIZE
    members = arranged[0].shape[1] // rows

    def leading(step, group_ref):
        return (group_ref[0] * count + step, 0, 0)

    def column(step, group_ref):
        return (0, group_ref[0] * heads_per_group + first_head + step)

    past_spec = pl.BlockSpec((2, window, HEAD_SIZE), lambda step, group_ref: (0, 0, step))
    low_spec = pl.BlockSpec((1, rows), lambda step, group_ref: (0, 0))
    own_spec = pl.BlockSpec((1, rows, HEAD_SIZE), lambda step, group_ref: (step, 0, 0))
    own_shape = jax.ShapeDtypeStruct((count, rows, HEAD_SIZE), jnp.bfloat16)
    square = (rows // TILE, window + TILE, members * TILE)
    tiles = count * members * rows * (window + TILE)
    return pl.pallas_call(
        functools.partial(attention_body, len(carried)),
        grid_spec=pltpu.PrefetchScalarGridSpec(
            num_scalar_prefetch=1,
            grid=(count,),
            in_specs=[low_spec]
            + [pl.BlockSpec((1, *array.shape[1:]), leading) for array in arranged]
            + [past_spec]
            + [pl.BlockSpec(memory_space=pl.ANY)] * len(carried),
            out_specs=[pl.BlockSpec((rows, members * HEAD_SIZE), column), own_spec, own_spec, past_spec],
            scratch_shapes=[
                pltpu.VMEM((window + rows, HEAD_SIZE), jnp.bfloat16),
                pltpu.VMEM((window + rows, HEAD_SIZE), jnp.bfloat16),
                pltpu.VMEM((HEAD_SIZE, window + rows), jnp.bfloat16),
                pltpu.VMEM((window + rows, HEAD_SIZE), jnp.float32),
                pltpu.VMEM((window + rows, HEAD_SIZE), jnp.float32),
                pltpu.VMEM(square, jnp.float32),
                pltpu.VMEM(square, jnp.float32),
                pltpu.VMEM(square, jnp.bfloat16),
                pltpu.VMEM(square, jnp.bfloat16),
            ],
        ),
        out_shape=[
            jax.ShapeDtypeStruct((rows, heads * members * HEAD_SIZE), jnp.bfloat16),
            own_shape,
            own_shape,
            jax.ShapeDtypeStruct(past.shape, jnp.bfloat16),
        ],
        input_output_aliases={9 + i: i for i in range(len(carried))},
        compiler_params=pltpu.CompilerParams(vmem_limit_bytes=VMEM_BYTES),
        cost_estimate=pl.CostEstimate(
            flops=10 * tiles * HEAD_SIZE, bytes_accessed=count * rows * 2400, transcendentals=tiles
        ),
        name="attention",
    )(group, low, *arranged, past, *carried)


def finish_body(carried, group_ref, dk_ref, dv_ref, back_ref, *refs):
    key_out, value_out = refs[carried:]
    sums = [
        own[0].astype(jnp.float32) + back_ref[i].astype(jnp.float32)
        for i, own in enumerate((dk_ref, dv_ref))
    ]
    key_out[...] = (sums[0] * HEAD_SIZE**-0.5).astype(key_out.dtype)
    value_out[...] = sums[1].astype(value_out.dtype)


def finish(group, own, back, first_head, heads_per_group, heads, carried):
    rows, count = back.shape[1], back.shape[2] // HEAD_SIZE

    def column(step, group_ref):
        return (0, group_ref[0] * heads_per_group + first_head + step)

    key_spec = pl.BlockSpec((rows, HEAD_SIZE), column)
    own_spec = pl.BlockSpec((1, rows, HEAD_SIZE), lambda step, group_ref: (step, 0, 0))
    back_spec = pl.BlockSpec((2, rows, HEAD_SIZE), lambda step, group_ref: (0, 0, step))
    return pl.pallas_call(
        functools.partial(finish_body, len(carried)),
        grid_spec=pltpu.PrefetchScalarGridSpec(
            num_scalar_prefetch=1,
            grid=(count,),
            in_specs=[own_spec, own_spec, back_spec]
            + [pl.BlockSpec(memory_space=pl.ANY)] * len(carried),
            out_specs=[key_spec, key_spec],
        ),
        out_shape=[jax.ShapeDtypeStruct((rows, heads * HEAD_SIZE), jnp.bfloat16)] * 2,
        input_output_aliases={4 + i: i for i in range(len(carried))},
        compiler_params=pltpu.CompilerParams(vmem_limit_bytes=FINISH_VMEM_BYTES),
        cost_estimate=pl.CostEstimate(
            flops=count * rows * 512, bytes_accessed=count * rows * 2048, transcendentals=0
        ),
        name="finish",
    )(group, *own, back, *carried)


def together(*values):
    return lax.optimization_barrier(values)


def pick(items, index):
    result = items[-1]
    for place in range(len(items) - 2, -1, -1):
        result = jnp.where(index == place, items[place], result)
    return result


def local(queries, keys, values, outputs, out_grads, segment_ids, block_order):
    blocks, sharers = lax.axis_size("blk"), lax.axis_size("head")
    block, place = lax.axis_index("blk"), lax.axis_index("head")
    rows = keys.shape[0]
    window = rows * sharers // 2
    parts = sharers // 2
    key_heads = keys.shape[1] // HEAD_SIZE
    heads_per_group = key_heads // sharers
    chunks = min(CHUNKS, heads_per_group)
    per_piece = heads_per_group // chunks
    slots = lax.dynamic_slice_in_dim(block_order, 2 * block, 2)
    early_slot = (slots[0] > slots[1]).astype(jnp.int32)
    last_block = block == blocks - 1

    def other(turn):
        return lax.rem(place + turn + sharers, sharers)

    def turned(value, turn):
        pairs = [(source, (source + turn) % sharers) for source in range(sharers)]
        return lax.ppermute(value, "head", pairs)

    def shifted(value, step):
        first, end = max(0, -step), min(blocks, blocks - step)
        return lax.ppermute(value, "blk", [(source, source + step) for source in range(first, end)])

    def columns(array, group, chunk):
        pieces = []
        for g in range(sharers):
            start = (g * heads_per_group + chunk * per_piece) * HEAD_SIZE
            pieces.append(array[:, start : start + per_piece * HEAD_SIZE])
        return pick(pieces, group)

    def piece_of(group, chunk):
        return jnp.stack([columns(keys, group, chunk), columns(values, group, chunk)])

    def is_early(device):
        return device // parts == early_slot

    def part_rows(array, device, count):
        if parts == 1:
            return array[:, :count]
        return lax.dynamic_slice_in_dim(array, device % parts * rows, count, 1)

    my_half = pick([slots[0], slots[1]], place // parts)
    start = my_half * window + place % parts * rows
    padded = jnp.concatenate([jnp.full((window,), -1, jnp.int32), segment_ids])
    near = lax.dynamic_slice_in_dim(padded, start, window + rows)
    low = jnp.sum((near[None, :] < near[window:, None]).astype(jnp.int32), axis=1)[None, :]

    row_arrays = (queries, keys, values, outputs, out_grads)
    groups = [other(-turn) for turn in range(sharers)]

    def halves_of(pieces):
        return [
            jnp.concatenate(
                [
                    pick(pieces, lax.rem(place - (slot * parts + p) + sharers, sharers))
                    for p in range(parts)
                ],
                axis=1,
            )
            for slot in (early_slot, 1 - early_slot)
        ]

    arranged, halves = [], []
    for chunk in range(chunks):
        pieces = [piece_of(place, chunk)]
        pieces += [turned(piece_of(other(turn), chunk), turn) for turn in range(1, sharers)]
        arrays = arrange(row_arrays, chunk * per_piece, heads_per_group, per_piece)
        *arrays, pieces[-1] = together(*arrays, pieces[-1])
        arranged.append(arrays)
        halves.append(halves_of(pieces))
    before = [(shifted(early, 1), shifted(late, -1)) for early, late in halves]

    def run(turn, chunk, past, carried):
        query_grads, *own[chunk, turn], back = attention(
            groups[turn].reshape(1), low, arranged[chunk], past,
            chunk * per_piece, heads_per_group, key_heads, carried,
        )
        return (query_grads,), back

    carried, own, terms, pasts = (), {}, [], []
    for chunk in range(chunks):
        (early, late), (before_early, before_late) = halves[chunk], before[chunk]
        if chunk:
            *carried, before_early, before_late = together(*carried, before_early, before_late)
        before_late = jnp.where(last_block, early, before_late)

        def past_of(device):
            before = jnp.where(is_early(device), before_early, before_late)
            if parts == 1:
                return before
            own = jnp.where(is_early(device), early, late)
            return part_rows(jnp.concatenate([before, own], axis=1), device, window)

        pasts.append(
            [past_of(place)] + [turned(past_of(other(turn)), turn) for turn in range(1, sharers)]
        )
        if chunk == 0:
            carried, back = run(0, 0, pasts[0][0], carried)
            terms.append([back])

    if chunks > 1:
        pasts[0][1], _ = together(pasts[0][1], pasts[1][0])
    for chunk in range(chunks):
        swapped = []
        for turn in range(1, sharers):
            carried, back = run(turn, chunk, pasts[chunk][turn], carried)
            swapped.append(turned(back, -turn))
        if chunk:
            carried, back = run(0, chunk, pasts[chunk][0], carried)
            terms.append([back])
        terms[chunk] += swapped

    (query_grads,) = carried
    results = ()
    for chunk in range(chunks):
        to_before, to_own = [], []
        for slot in (early_slot, 1 - early_slot):
            if parts == 1:
                to_before.append(pick(terms[chunk], lax.rem(slot - place + sharers, sharers)))
                to_own.append(None)
            else:
                total = jnp.zeros((2, 2 * window, terms[chunk][0].shape[2]), jnp.float32)
                for turn in range(sharers):
                    device = other(turn)
                    mine = jnp.where(device // parts == slot, terms[chunk][turn].astype(jnp.float32), 0.0)
                    wide = jnp.pad(mine, ((0, 0), (window, window), (0, 0)))
                    total += lax.dynamic_slice_in_dim(
                        wide, window - device % parts * rows, 2 * window, 1
                    )
                to_before.append(total[:, :window].astype(jnp.bfloat16))
                to_own.append(total[:, window:])
        for_early, for_late = shifted(to_before[0], -1), shifted(to_before[1], 1)
        for_early = jnp.where(last_block, to_before[1], for_early)
        sums = [
            came if more is None else (came.astype(jnp.float32) + more).astype(jnp.bfloat16)
            for came, more in zip((for_early, for_late), to_own)
        ]

        def rows_of(device):
            return part_rows(jnp.where(is_early(device), sums[0], sums[1]), device, rows)

        for turn in range(sharers):
            back = rows_of(other(turn))
            if turn:
                back = turned(back, turn)
            results = finish(
                groups[turn].reshape(1), own[chunk, turn], back,
                chunk * per_piece, heads_per_group, key_heads, tuple(results),
            )
    return (query_grads, *results)


def solution(mesh):
    spread = P(("blk", "head"), None)
    return jax.shard_map(
        local,
        mesh=mesh,
        in_specs=(spread,) * 5 + (P(), P()),
        out_specs=(spread,) * 3,
        check_vma=False,
    )
```

```python
import functools

import jax
import jax.numpy as jnp
from jax import lax
from jax.experimental import pallas as pl
from jax.experimental.pallas import tpu as pltpu
from jax.sharding import PartitionSpec as P

HEAD_SIZE = 128
NEGATIVE = -1e30
LOG2_E = 1.4426950408889634
CHUNKS = 2
TILE = 128
STRIP = 64
VMEM_BYTES = 60 * 1024 * 1024
FINISH_VMEM_BYTES = 6 * 1024 * 1024


def dot(left, right, left_dim, right_dim):
    return lax.dot_general(
        left, right, (((left_dim,), (right_dim,)), ((), ())), preferred_element_type=jnp.float32
    )


def strips(count):
    return [slice(start, start + STRIP) for start in range(0, count, STRIP)]


def folded(strip, reduce):
    return reduce(strip.reshape(strip.shape[0] // 8, 8, strip.shape[1]), axis=0)


def arrange_body(q_ref, k_ref, v_ref, o_ref, do_ref, q_out, do_out, delta_out, k_out, k_turned_out, v_out):
    rows, head = k_ref.shape
    members = q_ref.shape[1] // head
    for tile in range(rows // TILE):
        own = slice(tile * TILE, (tile + 1) * TILE)
        for m in range(members):
            place = slice((tile * members + m) * TILE, (tile * members + m + 1) * TILE)
            columns = slice(m * head, (m + 1) * head)
            q_out[0, place] = q_ref[own, columns]
            do_out[0, place] = do_ref[own, columns]
            product = do_ref[own, columns].astype(jnp.float32) * o_ref[own, columns].astype(jnp.float32)
            delta_out[0, :, place] = jnp.sum(product.T, axis=0, keepdims=True)
    k_out[0] = k_ref[...]
    k_turned_out[0] = k_ref[...].T
    v_out[0] = v_ref[...]


def arrange(row_arrays, first_head, heads_per_group, per_piece):
    queries, keys, values, outputs, grads = row_arrays
    rows, members = keys.shape[0], queries.shape[1] // keys.shape[1]
    groups = keys.shape[1] // HEAD_SIZE // heads_per_group
    count = groups * per_piece

    def column(group, step):
        return (0, group * heads_per_group + first_head + step)

    def leading(group, step):
        return (group * per_piece + step, 0, 0)

    query_spec = pl.BlockSpec((rows, members * HEAD_SIZE), column)
    key_spec = pl.BlockSpec((rows, HEAD_SIZE), column)
    shapes = [
        ((members * rows, HEAD_SIZE), jnp.bfloat16),
        ((members * rows, HEAD_SIZE), jnp.bfloat16),
        ((1, members * rows), jnp.float32),
        ((rows, HEAD_SIZE), jnp.bfloat16),
        ((HEAD_SIZE, rows), jnp.bfloat16),
        ((rows, HEAD_SIZE), jnp.bfloat16),
    ]
    return pl.pallas_call(
        arrange_body,
        grid=(groups, per_piece),
        in_specs=[query_spec, key_spec, key_spec, query_spec, query_spec],
        out_specs=[pl.BlockSpec((1, *shape), leading) for shape, _ in shapes],
        out_shape=[jax.ShapeDtypeStruct((count, *shape), dtype) for shape, dtype in shapes],
        compiler_params=pltpu.CompilerParams(vmem_limit_bytes=VMEM_BYTES),
        cost_estimate=pl.CostEstimate(
            flops=count * rows * 1024, bytes_accessed=count * rows * 4096, transcendentals=0
        ),
        name="arrange",
    )(queries, keys, values, outputs, grads)


def attention_body(
    carried, group_ref, low_ref, q_ref, do_ref, delta_ref, k_ref, k_turned_ref, v_ref, past_ref, *refs
):
    dq_ref, dk_ref, dv_ref, back_ref = refs[carried : carried + 4]
    k_all, v_all, k_turned, dk_sum, dv_sum, scores, slopes, weights_b, slopes_b = refs[carried + 4 :]
    rows, head = k_ref.shape[1:]
    window = past_ref.shape[1]
    members = q_ref.shape[1] // rows
    span, lanes = window + TILE, members * TILE
    scale = head**-0.5
    k_all[:window] = past_ref[0]
    k_all[window:] = k_ref[0]
    v_all[:window] = past_ref[1]
    v_all[window:] = v_ref[0]
    k_turned[:, :window] = past_ref[0].T
    k_turned[:, window:] = k_turned_ref[0]
    dk_sum[...] = jnp.zeros_like(dk_sum)
    dv_sum[...] = jnp.zeros_like(dv_sum)
    lane = lax.broadcasted_iota(jnp.int32, (1, lanes), 1) % TILE
    tiles = range(rows // TILE)

    def enter(tile):
        keys = pl.ds(tile * TILE, span)
        place = pl.ds(tile * lanes, lanes)
        queries, grads = q_ref[0, place], do_ref[0, place]
        scores[tile] = dot(k_all[keys], queries, 1, 1)
        slopes[tile] = dot(v_all[keys], grads, 1, 1)
        return queries, grads

    def weigh(tile):
        start = tile * TILE
        delta = delta_ref[0, :, pl.ds(tile * lanes, lanes)]
        low = jnp.concatenate([low_ref[:, start : start + TILE]] * members, axis=1) - start

        def visible(strip):
            index = strip.start + lax.broadcasted_iota(jnp.int32, (STRIP, lanes), 0)
            seen = index >= low
            return seen & (index <= window + lane) if strip.stop > window else seen

        top = jnp.full((8, lanes), NEGATIVE, jnp.float32)
        for strip in strips(span):
            masked = jnp.where(visible(strip), scores[tile, strip], NEGATIVE)
            top = jnp.maximum(top, folded(masked, jnp.max))
        top = jnp.max(top, axis=0, keepdims=True)
        total = jnp.zeros((8, lanes), jnp.float32)
        for strip in strips(span):
            terms = jnp.exp2((scores[tile, strip] - top) * (scale * LOG2_E))
            terms = jnp.where(visible(strip), terms, 0.0)
            total = total + folded(terms, jnp.sum)
            scores[tile, strip] = terms
        inverse = 1.0 / jnp.sum(total, axis=0, keepdims=True)
        for strip in strips(span):
            weights = scores[tile, strip] * inverse
            weights_b[tile, strip] = weights.astype(jnp.bfloat16)
            slopes_b[tile, strip] = (weights * (slopes[tile, strip] - delta)).astype(jnp.bfloat16)

    def leave(tile, queries, grads):
        start = tile * TILE
        keys = pl.ds(start, span)
        dv_sum[keys] += dot(weights_b[tile], grads, 1, 0)
        dk_sum[keys] += dot(slopes_b[tile], queries, 1, 0)
        dq = (dot(k_turned[:, keys], slopes_b[tile], 1, 0) * scale).T
        for m in range(members):
            dq_ref[start : start + TILE, m * head : (m + 1) * head] = dq[
                m * TILE : (m + 1) * TILE
            ].astype(dq_ref.dtype)

    entered = {0: enter(0)}
    for tile in tiles:
        if tile + 1 in tiles:
            entered[tile + 1] = enter(tile + 1)
        if tile:
            leave(tile - 1, *entered[tile - 1])
        weigh(tile)
    leave(tiles[-1], *entered[tiles[-1]])
    back_ref[0] = dk_sum[:window].astype(back_ref.dtype)
    back_ref[1] = dv_sum[:window].astype(back_ref.dtype)
    dk_ref[0] = dk_sum[window:].astype(dk_ref.dtype)
    dv_ref[0] = dv_sum[window:].astype(dv_ref.dtype)


def attention(group, low, arranged, past, first_head, heads_per_group, heads, carried):
    rows, window, count = arranged[3].shape[1], past.shape[1], past.shape[2] // HEAD_SIZE
    members = arranged[0].shape[1] // rows

    def leading(step, group_ref):
        return (group_ref[0] * count + step, 0, 0)

    def column(step, group_ref):
        return (0, group_ref[0] * heads_per_group + first_head + step)

    past_spec = pl.BlockSpec((2, window, HEAD_SIZE), lambda step, group_ref: (0, 0, step))
    low_spec = pl.BlockSpec((1, rows), lambda step, group_ref: (0, 0))
    own_spec = pl.BlockSpec((1, rows, HEAD_SIZE), lambda step, group_ref: (step, 0, 0))
    own_shape = jax.ShapeDtypeStruct((count, rows, HEAD_SIZE), jnp.bfloat16)
    square = (rows // TILE, window + TILE, members * TILE)
    tiles = count * members * rows * (window + TILE)
    return pl.pallas_call(
        functools.partial(attention_body, len(carried)),
        grid_spec=pltpu.PrefetchScalarGridSpec(
            num_scalar_prefetch=1,
            grid=(count,),
            in_specs=[low_spec]
            + [pl.BlockSpec((1, *array.shape[1:]), leading) for array in arranged]
            + [past_spec]
            + [pl.BlockSpec(memory_space=pl.ANY)] * len(carried),
            out_specs=[pl.BlockSpec((rows, members * HEAD_SIZE), column), own_spec, own_spec, past_spec],
            scratch_shapes=[
                pltpu.VMEM((window + rows, HEAD_SIZE), jnp.bfloat16),
                pltpu.VMEM((window + rows, HEAD_SIZE), jnp.bfloat16),
                pltpu.VMEM((HEAD_SIZE, window + rows), jnp.bfloat16),
                pltpu.VMEM((window + rows, HEAD_SIZE), jnp.float32),
                pltpu.VMEM((window + rows, HEAD_SIZE), jnp.float32),
                pltpu.VMEM(square, jnp.float32),
                pltpu.VMEM(square, jnp.float32),
                pltpu.VMEM(square, jnp.bfloat16),
                pltpu.VMEM(square, jnp.bfloat16),
            ],
        ),
        out_shape=[
            jax.ShapeDtypeStruct((rows, heads * members * HEAD_SIZE), jnp.bfloat16),
            own_shape,
            own_shape,
            jax.ShapeDtypeStruct(past.shape, jnp.bfloat16),
        ],
        input_output_aliases={9 + i: i for i in range(len(carried))},
        compiler_params=pltpu.CompilerParams(vmem_limit_bytes=VMEM_BYTES),
        cost_estimate=pl.CostEstimate(
            flops=10 * tiles * HEAD_SIZE, bytes_accessed=count * rows * 2400, transcendentals=tiles
        ),
        name="attention",
    )(group, low, *arranged, past, *carried)


def finish_body(carried, group_ref, dk_ref, dv_ref, back_ref, *refs):
    key_out, value_out = refs[carried:]
    sums = [
        own[0].astype(jnp.float32) + back_ref[i].astype(jnp.float32)
        for i, own in enumerate((dk_ref, dv_ref))
    ]
    key_out[...] = (sums[0] * HEAD_SIZE**-0.5).astype(key_out.dtype)
    value_out[...] = sums[1].astype(value_out.dtype)


def finish(group, own, back, first_head, heads_per_group, heads, carried):
    rows, count = back.shape[1], back.shape[2] // HEAD_SIZE

    def column(step, group_ref):
        return (0, group_ref[0] * heads_per_group + first_head + step)

    key_spec = pl.BlockSpec((rows, HEAD_SIZE), column)
    own_spec = pl.BlockSpec((1, rows, HEAD_SIZE), lambda step, group_ref: (step, 0, 0))
    back_spec = pl.BlockSpec((2, rows, HEAD_SIZE), lambda step, group_ref: (0, 0, step))
    return pl.pallas_call(
        functools.partial(finish_body, len(carried)),
        grid_spec=pltpu.PrefetchScalarGridSpec(
            num_scalar_prefetch=1,
            grid=(count,),
            in_specs=[own_spec, own_spec, back_spec]
            + [pl.BlockSpec(memory_space=pl.ANY)] * len(carried),
            out_specs=[key_spec, key_spec],
        ),
        out_shape=[jax.ShapeDtypeStruct((rows, heads * HEAD_SIZE), jnp.bfloat16)] * 2,
        input_output_aliases={4 + i: i for i in range(len(carried))},
        compiler_params=pltpu.CompilerParams(vmem_limit_bytes=FINISH_VMEM_BYTES),
        cost_estimate=pl.CostEstimate(
            flops=count * rows * 512, bytes_accessed=count * rows * 2048, transcendentals=0
        ),
        name="finish",
    )(group, *own, back, *carried)


def together(*values):
    return lax.optimization_barrier(values)


def pick(items, index):
    result = items[-1]
    for place in range(len(items) - 2, -1, -1):
        result = jnp.where(index == place, items[place], result)
    return result


def local(queries, keys, values, outputs, out_grads, segment_ids, block_order):
    blocks, sharers = lax.axis_size("blk"), lax.axis_size("head")
    block, place = lax.axis_index("blk"), lax.axis_index("head")
    rows = keys.shape[0]
    window = rows * sharers // 2
    parts = sharers // 2
    key_heads = keys.shape[1] // HEAD_SIZE
    heads_per_group = key_heads // sharers
    chunks = min(CHUNKS, heads_per_group)
    per_piece = heads_per_group // chunks
    slots = lax.dynamic_slice_in_dim(block_order, 2 * block, 2)
    early_slot = (slots[0] > slots[1]).astype(jnp.int32)
    last_block = block == blocks - 1

    def other(turn):
        return lax.rem(place + turn + sharers, sharers)

    def turned(value, turn):
        pairs = [(source, (source + turn) % sharers) for source in range(sharers)]
        return lax.ppermute(value, "head", pairs)

    def shifted(value, step):
        first, end = max(0, -step), min(blocks, blocks - step)
        return lax.ppermute(value, "blk", [(source, source + step) for source in range(first, end)])

    def columns(array, group, chunk):
        pieces = []
        for g in range(sharers):
            start = (g * heads_per_group + chunk * per_piece) * HEAD_SIZE
            pieces.append(array[:, start : start + per_piece * HEAD_SIZE])
        return pick(pieces, group)

    def piece_of(group, chunk):
        return jnp.stack([columns(keys, group, chunk), columns(values, group, chunk)])

    def is_early(device):
        return device // parts == early_slot

    def part_rows(array, device, count):
        if parts == 1:
            return array[:, :count]
        return lax.dynamic_slice_in_dim(array, device % parts * rows, count, 1)

    my_half = pick([slots[0], slots[1]], place // parts)
    start = my_half * window + place % parts * rows
    padded = jnp.concatenate([jnp.full((window,), -1, jnp.int32), segment_ids])
    near = lax.dynamic_slice_in_dim(padded, start, window + rows)
    low = jnp.sum((near[None, :] < near[window:, None]).astype(jnp.int32), axis=1)[None, :]

    row_arrays = (queries, keys, values, outputs, out_grads)
    groups = [other(-turn) for turn in range(sharers)]

    def halves_of(pieces):
        return [
            jnp.concatenate(
                [
                    pick(pieces, lax.rem(place - (slot * parts + p) + sharers, sharers))
                    for p in range(parts)
                ],
                axis=1,
            )
            for slot in (early_slot, 1 - early_slot)
        ]

    arranged, halves = [], []
    for chunk in range(chunks):
        pieces = [piece_of(place, chunk)]
        pieces += [turned(piece_of(other(turn), chunk), turn) for turn in range(1, sharers)]
        arrays = arrange(row_arrays, chunk * per_piece, heads_per_group, per_piece)
        if not halves:
            low, pieces[-1] = together(low, pieces[-1])
        *arrays, pieces[-1] = together(*arrays, pieces[-1])
        arranged.append(arrays)
        halves.append(halves_of(pieces))
    before = [(shifted(early, 1), shifted(late, -1)) for early, late in halves]

    def run(turn, chunk, past, carried):
        query_grads, *own[chunk, turn], back = attention(
            groups[turn].reshape(1), low, arranged[chunk], past,
            chunk * per_piece, heads_per_group, key_heads, carried,
        )
        return (query_grads,), back

    carried, own, terms, pasts = (), {}, [], []
    for chunk in range(chunks):
        (early, late), (before_early, before_late) = halves[chunk], before[chunk]
        if chunk:
            *carried, before_early, before_late = together(*carried, before_early, before_late)
        before_late = jnp.where(last_block, early, before_late)

        def past_of(device):
            before = jnp.where(is_early(device), before_early, before_late)
            if parts == 1:
                return before
            own = jnp.where(is_early(device), early, late)
            return part_rows(jnp.concatenate([before, own], axis=1), device, window)

        pasts.append(
            [past_of(place)] + [turned(past_of(other(turn)), turn) for turn in range(1, sharers)]
        )
        if chunk == 0:
            carried, back = run(0, 0, pasts[0][0], carried)
            terms.append([back])

    if chunks > 1:
        pasts[0][1], _ = together(pasts[0][1], pasts[1][0])
    for chunk in range(chunks):
        swapped = []
        for turn in range(1, sharers):
            carried, back = run(turn, chunk, pasts[chunk][turn], carried)
            swapped.append(turned(back, -turn))
        if chunk:
            carried, back = run(0, chunk, pasts[chunk][0], carried)
            terms.append([back])
        terms[chunk] += swapped

    (query_grads,) = carried
    results = ()
    for chunk in range(chunks):
        to_before, to_own = [], []
        for slot in (early_slot, 1 - early_slot):
            if parts == 1:
                to_before.append(pick(terms[chunk], lax.rem(slot - place + sharers, sharers)))
                to_own.append(None)
            else:
                total = jnp.zeros((2, 2 * window, terms[chunk][0].shape[2]), jnp.float32)
                for turn in range(sharers):
                    device = other(turn)
                    mine = jnp.where(device // parts == slot, terms[chunk][turn].astype(jnp.float32), 0.0)
                    wide = jnp.pad(mine, ((0, 0), (window, window), (0, 0)))
                    total += lax.dynamic_slice_in_dim(
                        wide, window - device % parts * rows, 2 * window, 1
                    )
                to_before.append(total[:, :window].astype(jnp.bfloat16))
                to_own.append(total[:, window:])
        for_early, for_late = shifted(to_before[0], -1), shifted(to_before[1], 1)
        for_early = jnp.where(last_block, to_before[1], for_early)
        sums = [
            came if more is None else (came.astype(jnp.float32) + more).astype(jnp.bfloat16)
            for came, more in zip((for_early, for_late), to_own)
        ]

        def rows_of(device):
            return part_rows(jnp.where(is_early(device), sums[0], sums[1]), device, rows)

        for turn in range(sharers):
            back = rows_of(other(turn))
            if turn:
                back = turned(back, turn)
            results = finish(
                groups[turn].reshape(1), own[chunk, turn], back,
                chunk * per_piece, heads_per_group, key_heads, tuple(results),
            )
    return (query_grads, *results)


def solution(mesh):
    spread = P(("blk", "head"), None)
    return jax.shard_map(
        local,
        mesh=mesh,
        in_specs=(spread,) * 5 + (P(), P()),
        out_specs=(spread,) * 3,
        check_vma=False,
    )
```
